32 devices in a mesh: segment: 2 (over core), dom: 8 (over z, y), rep: 2 (over x).
Axes of the slice: x: 2, y: 2, z: 4, core: 2. Of those that a mesh axis runs over, the one named last changes fastest.
Arguments:
- node_latent: bfloat16 [4, 1024, 512], P('rep', 'dom'), may hold values from -6 to 6
- edge_latent: bfloat16 [4, 3072, 512], P('rep', 'dom'), may hold values from -6 to 6
- node_cot: bfloat16 [4, 1024, 512], P('rep', 'dom'), may hold values from -6 to 6
- edge_src: int32 [3072], P('dom'), may hold values from 0 to 191, as said below
- edge_dst: int32 [3072], P('dom'), may hold values from 0 to 127
- edge_count: int32 [8], P('dom'), may hold values from 192 to 384, as said below
- send_index: int32 [8, 4, 16], P('dom'), may hold values from 0 to 127, as said below
- w_edge_in: bfloat16 [2, 1536, 512], P('segment'), may hold values from -0.15625 to 0.15625
- w_edge_out: bfloat16 [2, 512, 512], P('segment'), may hold values from -0.25 to 0.25
- w_node_in: bfloat16 [2, 1024, 512], P('segment'), may hold values from -0.1875 to 0.1875
- w_node_out: bfloat16 [2, 512, 512], P('segment'), may hold values from -0.25 to 0.25
- gain_edge: float32 [2, 512], P('segment'), may hold values from 0.1 to 1.9
- gain_node: float32 [2, 512], P('segment'), may hold values from 0.1 to 1.9
Outputs:
- node_pair: bfloat16 [2, 4, 1024, 512], P('segment', 'rep', 'dom')
- edge_pair: bfloat16 [2, 4, 3072, 512], P('segment', 'rep', 'dom')
- grad_edge_in: float32 [2, 1536, 512], P('segment', ('dom', 'rep'))
- grad_edge_out: float32 [2, 512, 512], P('segment', ('dom', 'rep'))
- grad_node_in: float32 [2, 1024, 512], P('segment', ('dom', 'rep'))
- grad_node_out: float32 [2, 512, 512], P('segment', ('dom', 'rep'))
- grad_gain_edge: float32 [2, 512], P('segment', ('dom', 'rep'))
- grad_gain_node: float32 [2, 512], P('segment', ('dom', 'rep'))
The draws below stay inside these ranges and needn't reach their ends.
Inputs may be any that keep to these rules, and one draw needn't show every extreme that they name: `edge_src`: each value is below 192; a value 128 + j * 16 + k of partition p refers to round j only where partition p - o_j exists. `edge_count`: some partition has all 384 slots live. `send_index`: the 16 rows of one partition and round are distinct.
All inputs are finite; a program needn't handle non-finite values.
Results may differ from the reference program's by a relative error of at most 0.039.
Values may be sent and summed in bfloat16 or wider, within the bound.
No kernel may reach another device: no remote copies, remote signals or barrier semaphores. Data moves between devices by JAX's collectives and lax.ppermute only.
A program may use at most 128 MiB of HBM per device.

```python
import jax
import jax.numpy as jnp
from jax import lax

D = 512
NODE_DEV = 128
EDGE_DEV = 384
HALO = 16
ROUNDS = 4
SNAP = 4
NODES = 1024
EDGES = 3072
N_DOM = 8


def edge_lists(key):
    key_src = jax.random.fold_in(key, 11)
    key_dst = jax.random.fold_in(key, 12)
    slots = NODE_DEV + ROUNDS * HALO
    pick = jax.random.randint(key_src, (EDGES,), 0, slots)
    partition = jnp.arange(EDGES, dtype=jnp.int32) // EDGE_DEV
    round_of = jnp.clip((pick - NODE_DEV) // HALO, 0, ROUNDS - 1)
    offsets = jnp.array([1, -1, 2, -2], dtype=jnp.int32)
    anchor = partition - offsets[round_of]
    usable = (pick < NODE_DEV) | (anchor >= 0) & (anchor < N_DOM)
    sender = jnp.where(usable, pick, pick % NODE_DEV).astype(jnp.int32)
    target = jax.random.randint(key_dst, (EDGES,), 0, NODE_DEV)
    target = jnp.where(sender == target, (target + 1) % NODE_DEV, target).astype(jnp.int32)
    return (sender, target)


def draw_edge_src(key, part):
    return edge_lists(key)[0]


def draw_edge_dst(key, part):
    return edge_lists(key)[1]


def draw_edge_count(key, part):
    counts = jax.random.randint(jax.random.fold_in(key, 21), (N_DOM,), EDGE_DEV // 2, EDGE_DEV + 1)
    fullest = jax.random.randint(jax.random.fold_in(key, 22), (), 0, N_DOM)
    return jnp.where(jnp.arange(N_DOM) == fullest, EDGE_DEV, counts).astype(jnp.int32)


def draw_send_index(key, part):
    keys = jax.random.split(jax.random.fold_in(key, 31), N_DOM * ROUNDS)
    rows = jax.vmap(lambda k: jax.random.permutation(k, NODE_DEV)[:HALO])(keys)
    return rows.reshape(N_DOM, ROUNDS, HALO).astype(jnp.int32)


def level_of(own_key, extent, pieces, smallest, top_value):
    def one(position, blocks):
        heights = jax.random.uniform(jax.random.fold_in(jax.random.fold_in(own_key, 6), position), (blocks,), jnp.float32, smallest / len(pieces), top_value / len(pieces))
        return jnp.repeat(jnp.exp(heights), extent[position] // blocks).reshape((-1,) + (1,) * (len(extent) - position - 1))

    level = one(*pieces[0])
    for cut in pieces[1:]:
        level = level * one(*cut)
    return level


def normal_values(rng, extent, width, reach, cuts=(), kind=jnp.bfloat16):
    result = jax.random.normal(rng, extent, jnp.float32) * width
    if len(cuts) > 0:
        result = level_of(rng, extent, cuts, -0.22, 0.18) * result
    return jnp.clip(result, min=-reach, max=reach).astype(kind)


def setup_inputs(seed: int = 0) -> dict:
    key_list = jax.random.split(jax.random.key(seed), 14)
    return {
        "node_latent": normal_values(key_list[0], (SNAP, NODES, D), 1.0, 6.0, ((0, 2), (1, 8))),
        "edge_latent": normal_values(key_list[1], (SNAP, EDGES, D), 1.0, 6.0, ((0, 2), (1, 8))),
        "node_cot": normal_values(key_list[2], (SNAP, NODES, D), 1.0, 6.0, ((0, 2), (1, 8))),
        "edge_src": draw_edge_src(jax.random.fold_in(key_list[13], 71), 0),
        "edge_dst": draw_edge_dst(jax.random.fold_in(key_list[13], 71), 0),
        "edge_count": draw_edge_count(jax.random.fold_in(key_list[13], 71), 0),
        "send_index": draw_send_index(jax.random.fold_in(key_list[13], 71), 0),
        "w_edge_in": normal_values(key_list[7], (2, 3 * D, D), (3 * D) ** -0.5, 0.15625, ((0, 2),)),
        "w_edge_out": normal_values(key_list[8], (2, D, D), D ** -0.5, 0.25, ((0, 2),)),
        "w_node_in": normal_values(key_list[9], (2, 2 * D, D), (2 * D) ** -0.5, 0.1875, ((0, 2),)),
        "w_node_out": normal_values(key_list[10], (2, D, D), D ** -0.5, 0.25, ((0, 2),)),
        "gain_edge": jnp.clip(1.0 + 0.18 * jax.random.normal(key_list[11], (2, D), jnp.float32), 0.1, 1.9),
        "gain_node": jnp.clip(1.0 + 0.18 * jax.random.normal(key_list[12], (2, D), jnp.float32), 0.1, 1.9),
    }


OFFSETS = (1, -1, 2, -2)
EPS = 1e-05

def norm_rows(values, gain):
    center = values - lax.optimization_barrier(jnp.mean(values, axis=-1, keepdims=True))
    spread = lax.optimization_barrier(jnp.mean(center * center, axis=-1, keepdims=True))
    return center * lax.rsqrt(spread + EPS) * gain

def layer(table, edges, weights, src, dst, live):
    w_ein, w_eout, w_nin, w_nout, g_edge, g_node = weights
    own = table[:NODE_DEV]
    sender = jnp.take(table, src, axis=0)
    receiver = jnp.take(table, dst, axis=0)
    joined = jnp.concatenate([edges, sender, receiver], axis=1)
    pre = jnp.dot(joined, w_ein.astype(jnp.bfloat16), preferred_element_type=jnp.float32)
    middle = jax.nn.silu(pre).astype(jnp.bfloat16)
    outer = jnp.dot(middle, w_eout.astype(jnp.bfloat16), preferred_element_type=jnp.float32)
    moved = edges.astype(jnp.float32)
    edge_new = jnp.where(live[:, None], moved + norm_rows(outer, g_edge), moved).astype(jnp.bfloat16)
    owners = jnp.arange(NODE_DEV, dtype=jnp.int32)
    incidence = ((dst[None, :] == owners[:, None]) & live[None, :]).astype(jnp.bfloat16)
    summed = jnp.dot(incidence, edge_new, preferred_element_type=jnp.float32).astype(jnp.bfloat16)
    node_in = jnp.concatenate([own, summed], axis=1)
    pre_node = jnp.dot(node_in, w_nin.astype(jnp.bfloat16), preferred_element_type=jnp.float32)
    mid_node = jax.nn.silu(pre_node).astype(jnp.bfloat16)
    out_node = jnp.dot(mid_node, w_nout.astype(jnp.bfloat16), preferred_element_type=jnp.float32)
    node_new = (own.astype(jnp.float32) + norm_rows(out_node, g_node)).astype(jnp.bfloat16)
    return (node_new, edge_new)

def tables(own, send_index):
    parts = [own]
    for j, step in enumerate(OFFSETS):
        sent = jax.vmap(lambda rows, idx: jnp.take(rows, idx, axis=0))(own, send_index[:, j])
        blank = jnp.zeros((abs(step),) + sent.shape[1:], sent.dtype)
        if step > 0:
            got = jnp.concatenate([blank, sent[:-step]], axis=0)
        else:
            got = jnp.concatenate([sent[-step:], blank], axis=0)
        parts.append(got)
    return jnp.concatenate(parts, axis=1)

def return_halo(d_table, send_index):
    d_own = d_table[:, :NODE_DEV].astype(jnp.float32)
    owners = jnp.arange(NODE_DEV, dtype=jnp.int32)
    for j, step in enumerate(OFFSETS):
        piece = d_table[:, NODE_DEV + j * HALO:NODE_DEV + (j + 1) * HALO]
        blank = jnp.zeros((abs(step),) + piece.shape[1:], piece.dtype)
        if step > 0:
            back = jnp.concatenate([piece[step:], blank], axis=0)
        else:
            back = jnp.concatenate([blank, piece[:step]], axis=0)
        incidence = (send_index[:, j, None, :] == owners[None, :, None]).astype(jnp.float32)
        d_own = d_own + jnp.einsum('nrh,nhd->nrd', incidence, back.astype(jnp.float32))
    return d_own.astype(jnp.bfloat16)

def backward_segment(weights, table, edges, cot_node, cot_edge, src, dst, live, send_index):

    def one(total, item):
        tab, edg, c_node, c_edge, s_idx, d_idx, alive = item
        _, pull = jax.vjp(lambda a, b, w: layer(a, b, w, s_idx, d_idx, alive), tab, edg, weights)
        d_tab, d_edg, d_w = pull((c_node, c_edge))
        total = jax.tree.map(lambda x, y: x + y.astype(jnp.float32), total, d_w)
        return (total, (d_tab, d_edg))
    start = jax.tree.map(jnp.zeros_like, weights)
    total, (d_tab, d_edg) = lax.scan(one, start, (table, edges, cot_node, cot_edge, src, dst, live))
    return (total, return_halo(d_tab, send_index), d_edg)

def reference(node_latent, edge_latent, node_cot, edge_src, edge_dst, edge_count, send_index, w_edge_in, w_edge_out, w_node_in, w_node_out, gain_edge, gain_node):
    src = edge_src.reshape(N_DOM, EDGE_DEV)
    dst = edge_dst.reshape(N_DOM, EDGE_DEV)
    live = jnp.arange(EDGE_DEV, dtype=jnp.int32)[None, :] < edge_count[:, None]
    segment_w = []
    for s in range(2):
        segment_w.append((w_edge_in[s].astype(jnp.float32), w_edge_out[s].astype(jnp.float32), w_node_in[s].astype(jnp.float32), w_node_out[s].astype(jnp.float32), gain_edge[s], gain_node[s]))
    forward = jax.vmap(layer, in_axes=(0, 0, None, 0, 0, 0))
    totals = [jax.tree.map(jnp.zeros_like, segment_w[0]), jax.tree.map(jnp.zeros_like, segment_w[1])]
    grad_nodes, grad_edges, last_nodes, last_edges = ([], [], [], [])
    for k in range(SNAP):
        h_zero = node_latent[k].reshape(N_DOM, NODE_DEV, D)
        e_zero = edge_latent[k].reshape(N_DOM, EDGE_DEV, D)
        t_zero = tables(h_zero, send_index)
        h_one, e_one = forward(t_zero, e_zero, segment_w[0], src, dst, live)
        t_one = tables(h_one, send_index)
        h_two, e_two = forward(t_one, e_one, segment_w[1], src, dst, live)
        c_node = node_cot[k].reshape(N_DOM, NODE_DEV, D)
        g_one, dh_one, de_one = backward_segment(segment_w[1], t_one, e_one, c_node, jnp.zeros_like(e_two), src, dst, live, send_index)
        g_zero, dh_zero, de_zero = backward_segment(segment_w[0], t_zero, e_zero, dh_one, de_one, src, dst, live, send_index)
        totals[0] = jax.tree.map(lambda x, y: x + y, totals[0], g_zero)
        totals[1] = jax.tree.map(lambda x, y: x + y, totals[1], g_one)
        grad_nodes.append(dh_zero.reshape(NODES, D))
        grad_edges.append(de_zero.reshape(EDGES, D))
        last_nodes.append(h_two.reshape(NODES, D))
        last_edges.append(e_two.reshape(EDGES, D))
    node_pair = jnp.stack([jnp.stack(grad_nodes), jnp.stack(last_nodes)])
    edge_pair = jnp.stack([jnp.stack(grad_edges), jnp.stack(last_edges)])
    factor = float(SNAP * NODES) ** (-0.5)
    outs = [jnp.stack([totals[0][i], totals[1][i]]) * factor for i in range(6)]
    return (node_pair, edge_pair, outs[0], outs[1], outs[2], outs[3], outs[4], outs[5])
```

```python
import functools

import jax
import jax.numpy as jnp
from jax import lax
from jax.experimental import pallas as pl
from jax.experimental.pallas import tpu as pltpu
from jax.sharding import PartitionSpec as P

NODE_DEV = 128
HALO = 16
ROUNDS = 4
D = 512
EPS = 1e-05
CHUNK = 128
BF = jnp.bfloat16
F32 = jnp.float32
VMEM_LIMIT = 60 * 1024 * 1024

ROWS = {"ein": 3 * D, "eout": D, "nin": 2 * D, "nout": D}
GROUPS = {"node": ("nin", "nout"), "edge": ("ein", "eout")}
SEQUENCE = {"node": (0, 1, 2, 3), "edge": (1, 0, 2, 3)}


def mm(a, b):
    return lax.dot_general(a, b, (((1,), (0,)), ((), ())), preferred_element_type=F32)


def mm_t(a, b):
    return lax.dot_general(a, b, (((1,), (1,)), ((), ())), preferred_element_type=F32)


def t_mm(a, b):
    return lax.dot_general(a, b, (((0,), (0,)), ((), ())), preferred_element_type=F32)


def one_hot(rows, index):
    where = lax.broadcasted_iota(jnp.int32, (rows, index.shape[1]), 0) == index
    return jnp.where(where, 1.0, 0.0).astype(BF)


def incidence(dst, count):
    edges = dst.shape[1]
    hit = lax.broadcasted_iota(jnp.int32, (NODE_DEV, edges), 0) == dst
    live = lax.broadcasted_iota(jnp.int32, (NODE_DEV, edges), 1) < count
    return jnp.where(hit & live, 1.0, 0.0).astype(BF)


def normed(values):
    center = values - jnp.mean(values, axis=-1, keepdims=True)
    spread = jnp.mean(center * center, axis=-1, keepdims=True)
    return center, lax.rsqrt(spread + EPS)


def silu_pair(pre):
    gate = lax.logistic(pre)
    return pre * gate, gate * (1.0 + pre * (1.0 - gate))


def norm_back(cot, hat, rate, gain):
    scaled = cot * gain
    first = jnp.mean(scaled, axis=-1, keepdims=True)
    second = jnp.mean(scaled * hat, axis=-1, keepdims=True)
    return rate * (scaled - first - hat * second)


def forward(own, edges, table, src, dst, count, weights, waits, gains, res):
    w_ein, w_eout, w_nin, w_nout = weights
    g_edge, g_node = gains
    rows = edges.shape[0]
    hot_src = one_hot(table.shape[0], src[...])
    hot_dst = one_hot(NODE_DEV, dst[...])
    waits[0]()
    waits[1]()
    for at in range(0, rows, CHUNK):
        part = slice(at, at + CHUNK)
        edge = edges[part]
        sender = t_mm(hot_src[:, part], table[...]).astype(BF)
        receiver = t_mm(hot_dst[:, part], own[...]).astype(BF)
        pre = mm(edge, w_ein[:D]) + mm(sender, w_ein[D : 2 * D]) + mm(receiver, w_ein[2 * D :])
        middle, slope = silu_pair(pre)
        middle = middle.astype(BF)
        center, rate = normed(mm(middle, w_eout[...]))
        live = lax.broadcasted_iota(jnp.int32, (CHUNK, 1), 0) + at < count
        rate = jnp.where(live, rate, 0.0)
        hat = center * rate
        res["edge_new"][part] = (edge.astype(F32) + hat * g_edge).astype(BF)
        res["edge_mid"][part] = middle
        res["edge_slope"][part] = slope.astype(BF)
        res["edge_hat"][part] = hat.astype(BF)
        res["edge_rate"][part] = jnp.broadcast_to(rate, (CHUNK, 128))
    agg = mm(incidence(dst[...], count), res["edge_new"][...]).astype(BF)
    waits[2]()
    waits[3]()
    pre = mm(own[...], w_nin[:D]) + mm(agg, w_nin[D:])
    middle, slope = silu_pair(pre)
    middle = middle.astype(BF)
    center, rate = normed(mm(middle, w_nout[...]))
    hat = center * rate
    res["node_new"][...] = (own[...].astype(F32) + hat * g_node).astype(BF)
    res["agg"][...] = agg
    res["node_mid"][...] = middle
    res["node_slope"][...] = slope.astype(BF)
    res["node_hat"][...] = hat.astype(BF)
    res["node_rate"][...] = jnp.broadcast_to(rate, (NODE_DEV, 128))


def slot_of(shard, me, shards, sequence):
    if shards == 1:
        return 0
    apart = jnp.bitwise_xor(jnp.int32(shard), me)
    slot = jnp.int32(0)
    for bit in sequence:
        slot = slot * 2 + jnp.bitwise_and(lax.shift_right_logical(apart, jnp.int32(bit)), 1)
    return slot


def emit(value, name, first_row, group, store, core, slots):
    shards = store.shape[1]
    half = ROWS[name] // shards // 2
    base = 0
    for other in GROUPS[group]:
        if other == name:
            break
        base += ROWS[other] // shards // 2
    value = value.astype(BF)
    last_row = first_row + value.shape[0]
    for piece in range(2 * shards):
        low, high = max(piece * half, first_row), min((piece + 1) * half, last_row)
        if low < high:
            keep = jnp.bitwise_xor(core, piece % 2)
            to = base + low - piece * half
            store[keep, slots[piece // 2], to : to + high - low, :] = value[
                low - first_row : high - first_row
            ]


def backward(
    cot_node, cot_edge, own, edges, table, src, dst, count, weights, gains, res, core, me, stores,
    outs, work, ready,
):
    w_ein, w_eout, w_nin, w_nout = weights
    g_edge, g_node = gains
    d_own_out, d_edges_out, halo_out, gain_out = outs
    d_outer, d_pre = work
    rows = edges.shape[0]
    shards = stores["node"].shape[1]
    slots = {
        g: [slot_of(i, me, shards, SEQUENCE[g]) for i in range(shards)] for g in GROUPS
    }

    def put(value, name, first_row):
        group = "node" if name in GROUPS["node"] else "edge"
        emit(value, name, first_row, group, stores[group], core, slots[group])

    hat = res["node_hat"][...].astype(F32)
    gain_node = jnp.sum(cot_node * hat, axis=0, keepdims=True)
    d_out = norm_back(cot_node, hat, res["node_rate"][:, :1], g_node).astype(BF)
    put(t_mm(res["node_mid"][...], d_out), "nout", 0)
    d_pre_node = (mm_t(d_out, w_nout[...]) * res["node_slope"][...].astype(F32)).astype(BF)
    put(t_mm(own[...], d_pre_node), "nin", 0)
    put(t_mm(res["agg"][...], d_pre_node), "nin", D)
    ready("node")
    d_own = cot_node + mm_t(d_pre_node, w_nin[:D])
    d_agg = mm_t(d_pre_node, w_nin[D:]).astype(BF)

    joins = incidence(dst[...], count)
    gain_edge = jnp.zeros((1, D), F32)
    for at in range(0, rows, CHUNK):
        part = slice(at, at + CHUNK)
        cot = t_mm(joins[:, part], d_agg)
        if cot_edge is not None:
            cot = cot + cot_edge[part].astype(F32)
        hat = res["edge_hat"][part].astype(F32)
        gain_edge = gain_edge + jnp.sum(cot * hat, axis=0, keepdims=True)
        outer = norm_back(cot, hat, res["edge_rate"][part, :1], g_edge).astype(BF)
        d_outer[part] = outer
        pre = (mm_t(outer, w_eout[...]) * res["edge_slope"][part].astype(F32)).astype(BF)
        d_pre[part] = pre
        d_edges_out[part] = (cot + mm_t(pre, w_ein[:D])).astype(BF)
    put(t_mm(res["edge_mid"][...], d_outer[...]), "eout", 0)
    put(t_mm(edges[...], d_pre[...]), "ein", 0)
    to_src = mm(one_hot(table.shape[0], src[...]), d_pre[...]).astype(BF)
    to_dst = mm(one_hot(NODE_DEV, dst[...]), d_pre[...]).astype(BF)
    put(t_mm(table[...], to_src), "ein", D)
    put(t_mm(own[...], to_dst), "ein", 2 * D)
    ready("edge")
    d_table = mm_t(to_src, w_ein[D : 2 * D])
    d_own = d_own + d_table[:NODE_DEV] + mm_t(to_dst, w_ein[2 * D :])
    d_own_out[...] = d_own
    halo_out[...] = d_table[NODE_DEV:].astype(BF)
    gain_out[...] = jnp.concatenate([gain_edge, gain_node, jnp.zeros((6, D), F32)], axis=0)


SAVED = (
    ("edge_mid", None),
    ("edge_slope", None),
    ("edge_hat", None),
    ("agg", NODE_DEV),
    ("node_mid", NODE_DEV),
    ("node_slope", NODE_DEV),
    ("node_hat", NODE_DEV),
)


def saved_rows(rows):
    return sum(h or rows for _, h in SAVED)


def views(rows, held, rates):
    out, at = {}, 0
    for name, height in SAVED:
        out[name] = held.at[at : at + (height or rows)]
        at += height or rows
    out["edge_rate"] = rates.at[:rows]
    out["node_rate"] = rates.at[rows : rows + NODE_DEV]
    return out


class Copies:
    def __init__(self, sems):
        self.sems, self.used, self.out = sems, 0, []

    def start(self, source, target):
        copy = pltpu.make_async_copy(source, target, self.sems.at[self.used])
        self.used += 1
        copy.start()
        return copy

    def send(self, source, target):
        self.out.append(self.start(source, target))

    def either(self, choice, yes, no, targets):
        sems = [self.sems.at[self.used + i] for i in range(len(targets))]
        self.used += len(targets)

        def start(refs):
            for ref, to, sem in zip(refs, targets, sems):
                pltpu.make_async_copy(ref, to, sem).start()

        pl.when(choice)(lambda: start(yes))
        pl.when(jnp.logical_not(choice))(lambda: start(no))
        return [
            pltpu.make_async_copy(ref, to, sem).wait for ref, to, sem in zip(yes, targets, sems)
        ]

    def finish(self):
        for copy in self.out:
            copy.wait()


def shard_number(shards):
    if shards == 1:
        return jnp.int32(0)
    return lax.axis_index("dom") * lax.axis_size("rep") + lax.axis_index("rep")


def first_rows(refs):
    return [ref.at[0] for ref in refs]


def halo_rows(table):
    return [table.at[NODE_DEV + j * HALO : NODE_DEV + (j + 1) * HALO] for j in range(ROUNDS)]


def send_rows(copies, held, outs):
    for j in range(ROUNDS):
        copies.send(held.at[j * HALO : (j + 1) * HALO], outs[j])


def lists_of(ints):
    rows = ints.shape[1]
    return ints.at[0:1, :rows], ints.at[1:2, :rows], ints[2:3, : ROUNDS * HALO]


def pick_kernel(ints, nodes, *rest):
    sent, (own, rows, sems) = rest[:ROUNDS], rest[ROUNDS:]
    copies = Copies(sems)
    copy = copies.start(nodes.at[lax.axis_index("segment")], own)
    hot = one_hot(NODE_DEV, lists_of(ints)[2])
    copy.wait()
    rows[...] = t_mm(hot, own[...]).astype(BF)
    send_rows(copies, rows, sent)
    copies.finish()


def first_kernel(count, ints, g_mine, g_other, nodes, latents, *rest):
    halo, mine, other, rest = rest[:4], rest[4:8], rest[8:12], rest[12:]
    (node_out, edge_out, saved_out, rate_out), sent, rest = rest[:4], rest[4:8], rest[8:]
    held, rest = rest[:4], rest[4:]
    table, edges, saved, rates, node_new, edge_new, rows, sems = rest
    core = lax.axis_index("segment")
    own = table.at[:NODE_DEV]
    copies = Copies(sems)
    coming = [copies.start(nodes.at[core], own), copies.start(latents.at[core], edges)]
    coming += [copies.start(ref, to) for ref, to in zip(halo, halo_rows(table))]
    waits = copies.either(core == 0, first_rows(mine), first_rows(other), held)
    src, dst, send_idx = lists_of(ints)
    gains = jnp.where(core == 0, g_mine[...], g_other[...])
    res = views(edges.shape[0], saved, rates)
    res.update(node_new=node_new, edge_new=edge_new)
    for copy in coming:
        copy.wait()
    forward(
        own, edges, table, src, dst, count[0], held, waits, (gains[:1], gains[1:2]), res
    )
    rows[...] = t_mm(one_hot(NODE_DEV, send_idx), node_new[...]).astype(BF)
    send_rows(copies, rows, sent)
    for source, target in zip(
        (node_new, edge_new, saved, rates), (node_out, edge_out, saved_out, rate_out)
    ):
        copies.send(source, target)
    copies.finish()


def back_outs(copies, stores, outs, work):
    d_own, d_edges, halo, gain, keeps, sends = outs
    d_own_s, d_edges_s, halo_s, gain_s = work

    def ready(group):
        i = 0 if group == "node" else 1
        copies.send(stores[group].at[1], sends[i])
        copies.send(stores[group].at[0], keeps[i])

    def finish():
        send_rows(copies, halo_s, halo)
        for source, target in ((d_own_s, d_own), (d_edges_s, d_edges), (gain_s, gain)):
            copies.send(source, target)
        copies.finish()

    return ready, finish


def second_kernel(count, ints, g_mine, g_other, nodes, latents, cots, *rest):
    halo, mine, other, rest = rest[:4], rest[4:8], rest[8:12], rest[12:]
    (node_out, edge_out), rest = rest[:2], rest[2:]
    outs, rest = (*rest[:2], rest[2:6], rest[6], rest[7:9], rest[9:11]), rest[11:]
    held, rest = rest[:4], rest[4:]
    table, edges, saved, rates, node_new, edge_new, cot, rest = *rest[:7], rest[7:]
    d_outer, d_pre, store_node, store_edge, *work, sems = rest
    core, me = lax.axis_index("segment"), shard_number(store_node.shape[1])
    own = table.at[:NODE_DEV]
    copies = Copies(sems)
    coming = [copies.start(nodes, own), copies.start(latents, edges)]
    coming += [copies.start(ref, to) for ref, to in zip(halo, halo_rows(table))]
    waits = copies.either(core == 1, first_rows(mine), first_rows(other), held)
    cot_copy = copies.start(cots.at[core], cot)
    src, dst, _ = lists_of(ints)
    gains = jnp.where(core == 1, g_mine[...], g_other[...])
    gains = (gains[:1], gains[1:2])
    res = views(edges.shape[0], saved, rates)
    res.update(node_new=node_new, edge_new=edge_new)
    for copy in coming:
        copy.wait()
    forward(own, edges, table, src, dst, count[0], held, waits, gains, res)
    copies.send(node_new, node_out)
    copies.send(edge_new, edge_out)
    cot_copy.wait()
    stores = {"node": store_node, "edge": store_edge}
    ready, finish = back_outs(copies, stores, outs, work)
    backward(
        cot[...].astype(F32), None, own, edges, table, src, dst, count[0], held, gains, res,
        core, me, stores, work, (d_outer, d_pre), ready,
    )
    finish()


def third_kernel(
    count, ints, g_mine, g_other, nodes, latents, d_own_in, d_edges_in, saved_in, rate_in, *rest
):
    halo, back, mine, other, rest = rest[:4], rest[4:8], rest[8:12], rest[12:16], rest[16:]
    outs, rest = (*rest[:2], rest[2:6], rest[6], rest[7:9], rest[9:11]), rest[11:]
    held, rest = rest[:4], rest[4:]
    table, edges, saved, rates, cot_own, cot_edge, got, rest = *rest[:7], rest[7:]
    d_outer, d_pre, store_node, store_edge, *work, sems = rest
    core, me = lax.axis_index("segment"), shard_number(store_node.shape[1])
    own = table.at[:NODE_DEV]
    copies = Copies(sems)
    coming = [
        copies.start(ref, got.at[j * HALO : (j + 1) * HALO]) for j, ref in enumerate(back)
    ]
    coming += [copies.start(d_own_in, cot_own), copies.start(rate_in, rates)]
    coming += [copies.start(saved_in, saved), copies.start(nodes.at[core], own)]
    coming += [copies.start(ref, to) for ref, to in zip(halo, halo_rows(table))]
    waits = copies.either(core == 0, first_rows(mine), first_rows(other), held)
    coming += [copies.start(d_edges_in, cot_edge), copies.start(latents.at[core], edges)]
    src, dst, send_idx = lists_of(ints)
    gains = jnp.where(core == 0, g_mine[...], g_other[...])
    gains = (gains[:1], gains[1:2])
    res = views(edges.shape[0], saved, rates)
    hot = one_hot(NODE_DEV, send_idx)
    for copy in coming:
        copy.wait()
    cot = (cot_own[...] + mm(hot, got[...])).astype(BF).astype(F32)
    for wait in waits:
        wait()
    stores = {"node": store_node, "edge": store_edge}
    ready, finish = back_outs(copies, stores, outs, work)
    backward(
        cot, cot_edge, own, edges, table, src, dst, count[0], held, gains, res,
        core, me, stores, work, (d_outer, d_pre), ready,
    )
    finish()


def last_kernel(ints, d_own, b0, b1, b2, b3, out):
    back = jnp.concatenate([b0[...], b1[...], b2[...], b3[...]], axis=0)
    out[...] = (d_own[...] + mm(one_hot(NODE_DEV, lists_of(ints)[2]), back)).astype(BF)


def weight_scratch():
    return [pltpu.VMEM((r, D), BF) for r in ROWS.values()]


SMEM = pl.BlockSpec(memory_space=pltpu.SMEM)
VMEM = pl.BlockSpec(memory_space=pltpu.VMEM)
ANY = pl.BlockSpec(memory_space=pl.ANY)


def shape(dims, dtype):
    return jax.ShapeDtypeStruct(tuple(dims), dtype)


def call(kernel, in_specs, outs, out_specs, scratch, flops, traffic):
    return pl.pallas_call(
        kernel,
        in_specs=in_specs,
        out_shape=outs,
        out_specs=out_specs,
        scratch_shapes=scratch,
        compiler_params=pltpu.CompilerParams(vmem_limit_bytes=VMEM_LIMIT),
        cost_estimate=pl.CostEstimate(flops=flops, bytes_accessed=traffic, transcendentals=0),
    )


def swap_pairs(size, distance):
    even, odd = [], []
    for p in range(size - distance):
        pair = [(p, p + distance), (p + distance, p)]
        (even if p % (2 * distance) < distance else odd).extend(pair)
    return even, odd


def exchange(pieces):
    size = lax.axis_size("dom")
    routes = swap_pairs(size, 1) + swap_pairs(size, 2)
    return [lax.ppermute(piece, "dom", route) for piece, route in zip(pieces, routes)]


def other_core(value):
    return lax.ppermute(value, "segment", [(0, 1), (1, 0)])


def across(value, bit):
    if bit == 0:
        return lax.ppermute(value, "rep", [(0, 1), (1, 0)])
    step = 1 << (bit - 1)
    return lax.ppermute(value, "dom", [(p, p ^ step) for p in range(lax.axis_size("dom"))])


def added(pieces):
    total = pieces[0].astype(F32)
    for piece in pieces[1:]:
        total = total + piece.astype(F32)
    return total


def tied(values, others):
    return lax.optimization_barrier((list(values), list(others)))[0]


class Halving:
    def __init__(self, keep, got):
        self.terms = [keep, got]

    def gone(self):
        slots = self.terms[0].shape[0] // 2
        value = added([t[slots:] for t in self.terms]).astype(BF)
        self.terms = [t[:slots] for t in self.terms]
        return value

    def sum(self):
        return added(self.terms)[0]


def body(
    node_latent,
    edge_latent,
    node_cot,
    edge_src,
    edge_dst,
    edge_count,
    send_index,
    w_edge_in,
    w_edge_out,
    w_node_in,
    w_node_out,
    gain_edge,
    gain_node,
):
    micro, _, _ = node_latent.shape
    rows = edge_latent.shape[1]
    assert micro == lax.axis_size("segment") == 2
    doms, reps = lax.axis_size("dom"), lax.axis_size("rep")
    core, part, rep = (lax.axis_index(a) for a in ("segment", "dom", "rep"))
    shards = doms * reps if doms * reps == 16 else 1
    first = core == 0

    odd_one, odd_two = part % 2 == 1, (part // 2) % 2 == 1
    flip = jnp.where(jnp.bitwise_and(edge_src, 2 * HALO) != 0, ~odd_two, ~odd_one)
    src = jnp.where(flip & (edge_src >= NODE_DEV), jnp.bitwise_xor(edge_src, HALO), edge_src)
    lists = send_index[0]
    order = [
        jnp.where(odd_one, lists[1], lists[0]),
        jnp.where(odd_one, lists[0], lists[1]),
        jnp.where(odd_two, lists[3], lists[2]),
        jnp.where(odd_two, lists[2], lists[3]),
    ]
    send_idx = jnp.pad(jnp.concatenate(order), (0, rows - ROUNDS * HALO))
    ints = jnp.stack([src, edge_dst, send_idx])

    dma = pltpu.SemaphoreType.DMA
    halo_shapes = [shape((HALO, D), BF)] * ROUNDS
    node_s, edge_s = pltpu.VMEM((NODE_DEV, D), BF), pltpu.VMEM((rows, D), BF)
    sent_s = pltpu.VMEM((ROUNDS * HALO, D), BF)
    sent = call(
        pick_kernel,
        [VMEM, ANY],
        halo_shapes,
        [ANY] * ROUNDS,
        [node_s, sent_s, dma((8,))],
        10**7,
        10**6,
    )(ints, node_latent)
    halo_zero = exchange(sent)
    mine = (w_edge_in, w_edge_out, w_node_in, w_node_out)
    other = tuple(other_core(w) for w in mine)
    g_mine = jnp.concatenate([gain_edge, gain_node], axis=0)
    small = (edge_count, ints, g_mine, other_core(g_mine))
    small_specs = [SMEM, VMEM, VMEM, VMEM]

    table_s = pltpu.VMEM((NODE_DEV + ROUNDS * HALO, D), BF)
    saved_dims, rate_dims = (saved_rows(rows), D), (rows + NODE_DEV, 128)
    layer_s = [
        *weight_scratch(),
        table_s,
        edge_s,
        pltpu.VMEM(saved_dims, BF),
        pltpu.VMEM(rate_dims, F32),
    ]
    node_one, edge_one, saved, rates, *sent = call(
        first_kernel,
        small_specs + [ANY] * (2 + 4 + 8),
        [
            shape((NODE_DEV, D), BF),
            shape((rows, D), BF),
            shape(saved_dims, BF),
            shape(rate_dims, F32),
            *halo_shapes,
        ],
        [ANY] * 8,
        [*layer_s, node_s, edge_s, sent_s, dma((20,))],
        11 * 10**8,
        8 * 10**6,
    )(*small, node_latent, edge_latent, *halo_zero, *mine, *other)
    halo_one = exchange(sent)

    sizes = [sum(ROWS[n] for n in names) // shards // 2 for names in GROUPS.values()]
    share = [shape((shards, size, D), BF) for size in sizes]
    back_shapes = [
        shape((NODE_DEV, D), F32),
        shape((rows, D), BF),
        *halo_shapes,
        shape((8, D), F32),
        *share,
        *share,
    ]
    back_s = [
        edge_s,
        edge_s,
        *[pltpu.VMEM((2, shards, size, D), BF) for size in sizes],
        pltpu.VMEM((NODE_DEV, D), F32),
        edge_s,
        sent_s,
        pltpu.VMEM((8, D), F32),
        dma((40,)),
    ]
    done = call(
        second_kernel,
        small_specs + [ANY] * (3 + 4 + 8),
        [shape((NODE_DEV, D), BF), shape((rows, D), BF)] + back_shapes,
        [ANY] * (2 + len(back_shapes)),
        [*layer_s, node_s, edge_s, node_s, *back_s],
        28 * 10**8,
        14 * 10**6,
    )(*small, node_one, edge_one, node_cot, *halo_one, *mine, *other)
    node_two, edge_two, d_own, d_edges = done[:4]
    gain_one, keep_one, send_one = done[8], done[9:11], done[11:13]
    back = exchange(done[4:8])
    got_one = [other_core(v) for v in send_one]
    if shards > 1:
        one = [Halving(k, g) for k, g in zip(keep_one, got_one)]
        gone = [h.gone() for h in one]
        back = tied(back, gone)
        one[0].terms.append(across(gone[0], 0))
        one[1].terms.append(across(gone[1], 1))

    done = call(
        third_kernel,
        small_specs + [ANY] * (6 + 8 + 8),
        back_shapes,
        [ANY] * len(back_shapes),
        [*layer_s, pltpu.VMEM((NODE_DEV, D), F32), edge_s, sent_s, *back_s],
        18 * 10**8,
        14 * 10**6,
    )(
        *small, node_latent, edge_latent, d_own, d_edges, saved, rates, *halo_zero, *back,
        *mine, *other,
    )
    d_own, d_edges = done[:2]
    gain_zero, keep_zero, send_zero = done[6], done[7:9], done[9:11]
    got_zero = [other_core(v) for v in send_zero]
    back = exchange(done[2:6])
    sums = jnp.where(first, gain_zero, gain_one)[:2]
    sums = sums + other_core(jnp.where(first, gain_one, gain_zero)[:2])

    if shards > 1:
        zero = [Halving(k, g) for k, g in zip(keep_zero, got_zero)]

        def step(bits, halves, after):
            gone = [h.gone() for h in halves]
            if after:
                gone = tied(gone, after)
            got = [across(v, bit) for v, bit in zip(gone, bits)]
            for h, v in zip(halves, got):
                h.terms.append(v)
            return got

        def joint(bit, halves, after):
            gone = [h.gone() for h in halves]
            if after:
                gone = tied(gone, after)
            got = across(jnp.concatenate(gone, axis=1), bit)
            at = 0
            for h, v in zip(halves, gone):
                h.terms.append(got[:, at : at + v.shape[1]])
                at += v.shape[1]
            return [got]

        last_one = [h.terms[-1] for h in one]
        zero_first = step((0, 1), zero, last_one)
        last_one = step((1, 0), one, None)
        zero_second = step((1, 0), zero, last_one)
        last_one = joint(2, one, None)
        joint(2, zero, last_one)
        last_one = joint(3, one, None)
        joint(3, zero, last_one)
        one, zero = ([h.sum() for h in v] for v in (one, zero))
        for bit in range(4):
            sums = sums + across(sums, bit)
    else:
        one = [added([k, g])[0] for k, g in zip(keep_one, got_one)]
        zero = [added([k, other_core(s)])[0] for k, s in zip(keep_zero, send_zero)]
        sums = lax.psum(sums, ("dom", "rep"))

    d_nodes = call(
        last_kernel,
        [VMEM] * 6,
        shape((NODE_DEV, D), BF),
        VMEM,
        [],
        10**7,
        10**6,
    )(ints, d_own, *back)

    def paired(gradient, latent):
        got = other_core(jnp.where(first, latent, gradient))
        low = jnp.where(first, gradient, got)
        high = jnp.where(first, got, latent)
        return jnp.stack([low, high])[None]

    factor = float(micro * reps * NODE_DEV * doms) ** (-0.5)
    one, zero = (jnp.concatenate(v, axis=0) for v in (one, zero))
    got = other_core(jnp.where(first, one, zero))
    kept = jnp.where(first, zero, one)
    low, high = jnp.where(first, kept, got), jnp.where(first, got, kept)
    grads, at = {}, 0
    for names in GROUPS.values():
        for name in names:
            to = at + ROWS[name] // shards // 2
            grads[name] = jnp.concatenate([low[at:to], high[at:to]], axis=0)
            at = to
    if shards == 1:
        grads = {
            k: lax.psum_scatter(v, ("dom", "rep"), scatter_dimension=0, tiled=True)
            for k, v in grads.items()
        }
    width = D // (doms * reps)
    sums = lax.dynamic_slice_in_dim(sums, (part * reps + rep) * width, width, axis=1) * factor
    return (
        paired(d_nodes, node_two),
        paired(d_edges, edge_two),
        (grads["ein"] * factor)[None],
        (grads["eout"] * factor)[None],
        (grads["nin"] * factor)[None],
        (grads["nout"] * factor)[None],
        sums[:1],
        sums[1:],
    )


def solution(mesh):
    placed = (
        P("rep", "dom", None),
        P("rep", "dom", None),
        P("rep", "dom", None),
        P("dom"),
        P("dom"),
        P("dom"),
        P("dom", None, None),
        P("segment", None, None),
        P("segment", None, None),
        P("segment", None, None),
        P("segment", None, None),
        P("segment", None),
        P("segment", None),
    )
    return jax.shard_map(
        body,
        mesh=mesh,
        in_specs=placed,
        out_specs=(
            P("segment", "rep", "dom", None),
            P("segment", "rep", "dom", None),
            P("segment", ("dom", "rep"), None),
            P("segment", ("dom", "rep"), None),
            P("segment", ("dom", "rep"), None),
            P("segment", ("dom", "rep"), None),
            P("segment", ("dom", "rep")),
            P("segment", ("dom", "rep")),
        ),
        check_vma=False,
    )
```

```python
import functools

import jax
import jax.numpy as jnp
from jax import lax
from jax.experimental import pallas as pl
from jax.experimental.pallas import tpu as pltpu
from jax.sharding import PartitionSpec as P

NODE_DEV = 128
HALO = 16
OFFSETS = (1, -1, 2, -2)
ROUNDS = len(OFFSETS)
D = 512
EPS = 1e-05
CHUNK = 384
BF = jnp.bfloat16
F32 = jnp.float32
GAINS = 16
VMEM_LIMIT = 63 * 1024 * 1024

ROWS = {"ein": 3 * D, "eout": D, "nin": 2 * D, "nout": D}
GROUPS = {"node": ("nin", "nout"), "edge": ("ein", "eout")}
SEQUENCE = (
    {"node": (0, 1, 3, 2), "edge": (1, 0, 3, 2)},
    {"node": (0, 2, 3, 1), "edge": (1, 2, 3, 0)},
)


def mm(a, b):
    return lax.dot_general(a, b, (((1,), (0,)), ((), ())), preferred_element_type=F32)


def mm_t(a, b):
    return lax.dot_general(a, b, (((1,), (1,)), ((), ())), preferred_element_type=F32)


def t_mm(a, b):
    return lax.dot_general(a, b, (((0,), (0,)), ((), ())), preferred_element_type=F32)


def one_hot(rows, index):
    where = lax.broadcasted_iota(jnp.int32, (rows, index.shape[1]), 0) == index
    return jnp.where(where, 1.0, 0.0).astype(BF)


def incidence(dst, count):
    edges = dst.shape[1]
    hit = lax.broadcasted_iota(jnp.int32, (NODE_DEV, edges), 0) == dst
    live = lax.broadcasted_iota(jnp.int32, (NODE_DEV, edges), 1) < count
    return jnp.where(hit & live, 1.0, 0.0).astype(BF)


def normed(values):
    center = values - jnp.mean(values, axis=-1, keepdims=True)
    spread = jnp.mean(center * center, axis=-1, keepdims=True)
    return center, lax.rsqrt(spread + EPS)


def silu_pair(pre):
    gate = lax.logistic(pre)
    return pre * gate, gate * (1.0 + pre * (1.0 - gate))


def norm_back(cot, hat, rate, gain):
    scaled = cot * gain
    first = jnp.mean(scaled, axis=-1, keepdims=True)
    second = jnp.mean(scaled * hat, axis=-1, keepdims=True)
    return rate * (scaled - first - hat * second)


def forward(own, edges, table, src, dst, count, weights, waits, gains, res):
    w_ein, w_eout, w_nin, w_nout = weights
    g_edge, g_node = gains
    rows = edges.shape[0]
    hot_src = one_hot(table.shape[0], src)
    hot_dst = one_hot(NODE_DEV, dst)
    waits[0]()
    waits[1]()
    for at in range(0, rows, CHUNK):
        part = slice(at, at + CHUNK)
        edge = edges[part]
        sender = t_mm(hot_src[:, part], table[...]).astype(BF)
        receiver = t_mm(hot_dst[:, part], own[...]).astype(BF)
        pre = mm(edge, w_ein[:D]) + mm(sender, w_ein[D : 2 * D]) + mm(receiver, w_ein[2 * D :])
        middle, slope = silu_pair(pre)
        middle = middle.astype(BF)
        center, rate = normed(mm(middle, w_eout[...]))
        live = lax.broadcasted_iota(jnp.int32, (CHUNK, 1), 0) + at < count
        rate = jnp.where(live, rate, 0.0)
        hat = center * rate
        res["edge_new"][part] = (edge.astype(F32) + hat * g_edge).astype(BF)
        res["edge_mid"][part] = middle
        res["edge_slope"][part] = slope.astype(BF)
        res["edge_hat"][part] = hat.astype(BF)
        res["edge_rate"][part] = jnp.broadcast_to(rate, (CHUNK, 128))
    agg = mm(incidence(dst, count), res["edge_new"][...]).astype(BF)
    waits[2]()
    waits[3]()
    pre = mm(own[...], w_nin[:D]) + mm(agg, w_nin[D:])
    middle, slope = silu_pair(pre)
    middle = middle.astype(BF)
    center, rate = normed(mm(middle, w_nout[...]))
    hat = center * rate
    res["node_new"][...] = (own[...].astype(F32) + hat * g_node).astype(BF)
    res["agg"][...] = agg
    res["node_mid"][...] = middle
    res["node_slope"][...] = slope.astype(BF)
    res["node_hat"][...] = hat.astype(BF)
    res["node_rate"][...] = jnp.broadcast_to(rate, (NODE_DEV, 128))


def slot_of(shard, me, shards, sequence):
    if shards == 1:
        return 0
    apart = jnp.bitwise_xor(jnp.int32(shard), me)
    slot = jnp.int32(0)
    for bit in sequence:
        slot = slot * 2 + jnp.bitwise_and(lax.shift_right_logical(apart, jnp.int32(bit)), 1)
    return slot


class Layout:
    def __init__(self, shards):
        self.shards = shards
        self.half = {name: rows // shards // 2 for name, rows in ROWS.items()}
        self.size = {g: sum(self.half[n] for n in names) for g, names in GROUPS.items()}
        self.gains = shards * self.size["node"]
        self.base = {"node": 0, "edge": self.gains + GAINS}
        self.rows = self.base["edge"] + shards * self.size["edge"]
        self.inner = {}
        for names in GROUPS.values():
            at = 0
            for name in names:
                self.inner[name] = at
                at += self.half[name]

    def span(self, group):
        return slice(self.base[group], self.base[group] + self.shards * self.size[group])


def emit(value, name, first_row, layout, group, store, core, slots):
    half = layout.half[name]
    value = value.astype(BF)
    last_row = first_row + value.shape[0]
    for piece in range(2 * layout.shards):
        low, high = max(piece * half, first_row), min((piece + 1) * half, last_row)
        if low < high:
            keep = jnp.bitwise_xor(core, piece % 2)
            to = layout.base[group] + layout.inner[name] + low - piece * half
            if layout.shards > 1:
                to = pl.multiple_of(slots[piece // 2] * layout.size[group] + to, 16)
            store[keep, pl.ds(to, high - low), :] = value[low - first_row : high - first_row]


def backward(
    cot_node, cot_edge, own, edges, table, src, dst, count, weights, gains, res, core, me, layout, sequence,
    store, outs, work, ready,
):
    w_ein, w_eout, w_nin, w_nout = weights
    g_edge, g_node = gains
    d_own_out, d_edges_out, room, put_gains = outs
    d_outer, d_pre = work
    rows = edges.shape[0]
    shards = layout.shards
    slots = {
        g: [slot_of(i, me, shards, sequence[g]) for i in range(shards)] for g in GROUPS
    }

    def put(value, name, first_row):
        group = "node" if name in GROUPS["node"] else "edge"
        emit(value, name, first_row, layout, group, store, core, slots[group])

    hat = res["node_hat"][...].astype(F32)
    gain_node = jnp.sum(cot_node * hat, axis=0, keepdims=True)
    d_out = norm_back(cot_node, hat, res["node_rate"][:, :1], g_node).astype(BF)
    put(t_mm(res["node_mid"][...], d_out), "nout", 0)
    d_pre_node = (mm_t(d_out, w_nout[...]) * res["node_slope"][...].astype(F32)).astype(BF)
    put(t_mm(own[...], d_pre_node), "nin", 0)
    put(t_mm(res["agg"][...], d_pre_node), "nin", D)
    ready("node")
    d_own = cot_node + mm_t(d_pre_node, w_nin[:D])
    d_agg = mm_t(d_pre_node, w_nin[D:]).astype(BF)

    joins = incidence(dst, count)
    gain_edge = jnp.zeros((1, D), F32)
    for at in range(0, rows, CHUNK):
        part = slice(at, at + CHUNK)
        cot = t_mm(joins[:, part], d_agg)
        if cot_edge is not None:
            cot = cot + cot_edge[part].astype(F32)
        hat = res["edge_hat"][part].astype(F32)
        gain_edge = gain_edge + jnp.sum(cot * hat, axis=0, keepdims=True)
        outer = norm_back(cot, hat, res["edge_rate"][part, :1], g_edge).astype(BF)
        d_outer[part] = outer
        pre = (mm_t(outer, w_eout[...]) * res["edge_slope"][part].astype(F32)).astype(BF)
        d_pre[part] = pre
        d_edges_out[part] = (cot + mm_t(pre, w_ein[:D])).astype(BF)
    put(t_mm(res["edge_mid"][...], d_outer[...]), "eout", 0)
    put(t_mm(edges[...], d_pre[...]), "ein", 0)
    to_src = mm(one_hot(table.shape[0], src), d_pre[...]).astype(BF)
    to_dst = mm(one_hot(NODE_DEV, dst), d_pre[...]).astype(BF)
    put(t_mm(table[...], to_src), "ein", D)
    put(t_mm(own[...], to_dst), "ein", 2 * D)
    put_gains(jnp.concatenate([gain_edge, gain_node, jnp.zeros((GAINS - 2, D), F32)], axis=0))
    ready("edge")
    d_table = mm_t(to_src, w_ein[D : 2 * D])
    d_own = d_own + d_table[:NODE_DEV] + mm_t(to_dst, w_ein[2 * D :])
    d_own_out[...] = d_own
    d_halo = d_table[NODE_DEV:].astype(BF)
    place(-1, [d_halo[j * HALO : (j + 1) * HALO] for j in range(ROUNDS)], room)


SAVED = (
    ("edge_mid", None),
    ("edge_slope", None),
    ("edge_hat", None),
    ("agg", NODE_DEV),
    ("node_mid", NODE_DEV),
    ("node_slope", NODE_DEV),
    ("node_hat", NODE_DEV),
)


def saved_rows(rows):
    return sum(h or rows for _, h in SAVED)


def views(rows, held, rates):
    out, at = {}, 0
    for name, height in SAVED:
        out[name] = held.at[at : at + (height or rows)]
        at += height or rows
    out["edge_rate"] = rates.at[:rows]
    out["node_rate"] = rates.at[rows : rows + NODE_DEV]
    return out


class Copies:
    def __init__(self, sems):
        self.sems, self.used, self.out = sems, 0, []

    def start(self, source, target):
        copy = pltpu.make_async_copy(source, target, self.sems.at[self.used])
        self.used += 1
        copy.start()
        return copy

    def send(self, source, target):
        self.out.append(self.start(source, target))

    def either(self, choice, yes, no, targets):
        sems = [self.sems.at[self.used + i] for i in range(len(targets))]
        self.used += len(targets)

        def start(refs):
            for ref, to, sem in zip(refs, targets, sems):
                pltpu.make_async_copy(ref, to, sem).start()

        pl.when(choice)(lambda: start(yes))
        pl.when(jnp.logical_not(choice))(lambda: start(no))
        return [
            pltpu.make_async_copy(ref, to, sem).wait for ref, to, sem in zip(yes, targets, sems)
        ]

    def finish(self):
        for copy in self.out:
            copy.wait()


def shard_number(shards):
    if shards == 1:
        return jnp.int32(0)
    return lax.axis_index("dom") * lax.axis_size("rep") + lax.axis_index("rep")


def first_rows(refs):
    return [ref.at[0] for ref in refs]


def one_hots(lists):
    return [one_hot(NODE_DEV, lists[0, j : j + 1]) for j in range(ROUNDS)]


def place(sign, pieces, room):
    part, parts = lax.axis_index("dom"), lax.axis_size("dom")
    room[...] = jnp.zeros_like(room)
    for piece, offset in zip(pieces, OFFSETS):
        to = part + sign * offset

        def put(piece=piece, to=to):
            room[pl.ds(pl.multiple_of(to * HALO, HALO), HALO), :] = piece

        pl.when((to >= 0) & (to < parts))(put)


def placed(sign, room):
    part, parts = lax.axis_index("dom"), lax.axis_size("dom")
    out = []
    for offset in OFFSETS:
        source = part + sign * offset
        there = jnp.clip(source, 0, parts - 1)
        rows = room[pl.ds(pl.multiple_of(there * HALO, HALO), HALO), :]
        out.append(jnp.where((source >= 0) & (source < parts), rows, jnp.zeros_like(rows)))
    return out


def pick(hot, values):
    return [t_mm(one, values).astype(BF) for one in hot]


def fill_halo(table, room):
    for j, rows in enumerate(placed(-1, room)):
        table[NODE_DEV + j * HALO : NODE_DEV + (j + 1) * HALO] = rows


def spread(hot, pieces):
    total = mm(hot[0], pieces[0])
    for j in range(1, ROUNDS):
        total = total + mm(hot[j], pieces[j])
    return total


def pick_kernel(lists, nodes, sent, own, room, sems):
    copies = Copies(sems)
    copy = copies.start(nodes.at[lax.axis_index("segment")], own)
    hot = one_hots(lists)
    copy.wait()
    place(1, pick(hot, own[...]), room)
    copies.send(room, sent)
    copies.finish()


def first_kernel(count, src, dst, lists, g_mine, g_other, nodes, latents, *rest):
    halo, mine, other, rest = rest[0], rest[1:5], rest[5:9], rest[9:]
    (node_out, edge_out, saved_out, rate_out, sent), rest = rest[:5], rest[5:]
    held, rest = rest[:4], rest[4:]
    table, edges, saved, rates, room, node_new, edge_new, sems = rest
    core = lax.axis_index("segment")
    own = table.at[:NODE_DEV]
    copies = Copies(sems)
    coming = [copies.start(nodes.at[core], own), copies.start(latents.at[core], edges)]
    coming += [copies.start(halo, room)]
    waits = copies.either(core == 0, first_rows(mine), first_rows(other), held)
    src, dst = src[...], dst[...]
    gains = jnp.where(core == 0, g_mine[...], g_other[...])
    res = views(edges.shape[0], saved, rates)
    res.update(node_new=node_new, edge_new=edge_new)
    for copy in coming:
        copy.wait()
    fill_halo(table, room)
    forward(
        own, edges, table, src, dst, count[0], held, waits, (gains[:1], gains[1:2]), res
    )
    place(1, pick(one_hots(lists), node_new[...]), room)
    for source, target in zip(
        (room, node_new, edge_new, saved, rates),
        (sent, node_out, edge_out, saved_out, rate_out),
    ):
        copies.send(source, target)
    copies.finish()


def back_outs(copies, layout, store, outs, work):
    d_own, d_edges, sent, keep, send = outs
    d_own_s, d_edges_s, room = work

    def ready(group):
        first = layout.base[group] if group == "node" else layout.gains
        rows = pl.ds(first, layout.span(group).stop - first)
        copies.send(store.at[1, rows], send.at[rows])
        copies.send(store.at[0, rows], keep.at[rows])

    def finish():
        copies.send(room, sent)
        copies.send(d_own_s, d_own)
        copies.send(d_edges_s, d_edges)
        copies.finish()

    return ready, finish


def second_kernel(shards, count, src, dst, lists, g_mine, g_other, nodes, latents, cots, *rest):
    halo, mine, other, rest = rest[0], rest[1:5], rest[5:9], rest[9:]
    (node_out, edge_out, gain_out), rest = rest[:3], rest[3:]
    outs, rest = rest[:5], rest[5:]
    held, rest = rest[:4], rest[4:]
    table, edges, saved, rates, room, node_new, edge_new, cot, rest = *rest[:8], rest[8:]
    d_outer, d_pre, store, *work, sems = rest
    layout = Layout(shards)
    core, me = lax.axis_index("segment"), shard_number(shards)
    own = table.at[:NODE_DEV]
    copies = Copies(sems)
    coming = [copies.start(nodes, own), copies.start(latents, edges)]
    coming += [copies.start(halo, room)]
    waits = copies.either(core == 1, first_rows(mine), first_rows(other), held)
    cot_copy = copies.start(cots.at[core], cot)
    src, dst = src[...], dst[...]
    gains = jnp.where(core == 1, g_mine[...], g_other[...])
    gains = (gains[:1], gains[1:2])
    res = views(edges.shape[0], saved, rates)
    res.update(node_new=node_new, edge_new=edge_new)
    for copy in coming:
        copy.wait()
    fill_halo(table, room)
    forward(own, edges, table, src, dst, count[0], held, waits, gains, res)
    copies.send(node_new, node_out)
    copies.send(edge_new, edge_out)
    cot_copy.wait()
    ready, finish = back_outs(copies, layout, store, outs, (*work, room))

    def put_gains(value):
        gain_out[...] = value
        for side in range(2):
            store[side, layout.gains : layout.gains + GAINS] = jnp.zeros((GAINS, D), BF)

    backward(
        cot[...].astype(F32), None, own, edges, table, src, dst, count[0], held, gains, res,
        core, me, layout, SEQUENCE[1], store, (*work[:2], room, put_gains), (d_outer, d_pre), ready,
    )
    finish()


def third_kernel(
    shards, count, src, dst, lists, g_mine, g_other, gain_one, nodes, latents, d_own_in,
    d_edges_in, saved_in, rate_in, *rest
):
    halo, back, mine, other, rest = rest[0], rest[1], rest[2:6], rest[6:10], rest[10:]
    outs, rest = rest[:5], rest[5:]
    held, rest = rest[:4], rest[4:]
    table, edges, saved, rates, room, cot_own, cot_edge, got, rest = *rest[:8], rest[8:]
    d_outer, d_pre, store, *work, sems = rest
    layout = Layout(shards)
    core, me = lax.axis_index("segment"), shard_number(shards)
    own = table.at[:NODE_DEV]
    copies = Copies(sems)
    coming = [copies.start(back, got)]
    coming += [copies.start(d_own_in, cot_own), copies.start(rate_in, rates)]
    coming += [copies.start(saved_in, saved), copies.start(nodes.at[core], own)]
    coming += [copies.start(halo, room)]
    waits = copies.either(core == 0, first_rows(mine), first_rows(other), held)
    coming += [copies.start(d_edges_in, cot_edge), copies.start(latents.at[core], edges)]
    src, dst = src[...], dst[...]
    gains = jnp.where(core == 0, g_mine[...], g_other[...])
    gains = (gains[:1], gains[1:2])
    res = views(edges.shape[0], saved, rates)
    hot = one_hots(lists)
    for copy in coming:
        copy.wait()
    fill_halo(table, room)
    cot = (cot_own[...] + spread(hot, placed(1, got))).astype(BF).astype(F32)
    for wait in waits:
        wait()
    ready, finish = back_outs(copies, layout, store, outs, (*work, room))

    def put_gains(value):
        both = (value.astype(BF), gain_one[...].astype(BF))
        rows = slice(layout.gains, layout.gains + GAINS)
        store[0, rows] = jnp.where(core == 0, both[0], both[1])
        store[1, rows] = jnp.where(core == 0, both[1], both[0])

    backward(
        cot, cot_edge, own, edges, table, src, dst, count[0], held, gains, res,
        core, me, layout, SEQUENCE[0], store, (*work[:2], room, put_gains), (d_outer, d_pre), ready,
    )
    finish()


def last_kernel(lists, d_own, back, out):
    out[...] = (d_own[...] + spread(one_hots(lists), placed(1, back))).astype(BF)


def weight_scratch():
    return [pltpu.VMEM((r, D), BF) for r in ROWS.values()]


SMEM = pl.BlockSpec(memory_space=pltpu.SMEM)
VMEM = pl.BlockSpec(memory_space=pltpu.VMEM)
ANY = pl.BlockSpec(memory_space=pl.ANY)


def shape(dims, dtype):
    return jax.ShapeDtypeStruct(tuple(dims), dtype)


def call(kernel, in_specs, outs, out_specs, scratch, flops, traffic):
    return pl.pallas_call(
        kernel,
        in_specs=in_specs,
        out_shape=outs,
        out_specs=out_specs,
        scratch_shapes=scratch,
        compiler_params=pltpu.CompilerParams(vmem_limit_bytes=VMEM_LIMIT),
        cost_estimate=pl.CostEstimate(flops=flops, bytes_accessed=traffic, transcendentals=0),
    )


def exchange(rows):
    return lax.all_to_all(rows, "dom", 0, 0, tiled=True)


def other_core(value):
    return lax.ppermute(value, "segment", [(0, 1), (1, 0)])


def across(value, apart):
    if apart == 1:
        return lax.ppermute(value, "rep", [(0, 1), (1, 0)])
    step = apart // 2
    return lax.ppermute(value, "dom", [(p, p ^ step) for p in range(lax.axis_size("dom"))])


def added(pieces):
    total = pieces[0].astype(F32)
    for piece in pieces[1:]:
        total = total + piece.astype(F32)
    return total


def tied(values, others):
    return lax.optimization_barrier((list(values), list(others)))[0]


class Rows:
    def __init__(self, first, rows, arrays):
        self.rows, self.terms = rows, [(a, first) for a in arrays]

    def upper(self):
        self.rows //= 2
        return self.rows, [(a, first + self.rows) for a, first in self.terms]

    def whole(self):
        return self.rows, list(self.terms)

    def quarter(self, i):
        rows = self.rows // 4
        return rows, [(a, first + i * rows) for a, first in self.terms]

    def add(self, array, first):
        self.terms.append((array, first))


def combine(outputs):
    arrays = []
    for _, segments in outputs:
        for _, terms in segments:
            arrays += [a for a, _ in terms if all(a is not b for b in arrays)]
    total = sum(rows * len(terms) for _, segments in outputs for rows, terms in segments)
    copies = sum(len(terms) for _, segments in outputs for _, terms in segments)
    heights = [sum(rows for rows, _ in segments) for _, segments in outputs]

    def kernel(*refs):
        sources, refs = refs[: len(arrays)], refs[len(arrays) :]
        outs, refs = refs[: len(outputs)], refs[len(outputs) :]
        held, sums, sems, out_sems = refs[0], refs[1:-2], refs[-2], refs[-1]
        plan, at, used = [], 0, 0
        for _, segments in outputs:
            for rows, terms in segments:
                places = []
                for array, first in terms:
                    which = [array is a for a in arrays].index(True)
                    copy = pltpu.make_async_copy(
                        sources[which].at[first : first + rows],
                        held.at[at : at + rows],
                        sems.at[used],
                    )
                    copy.start()
                    places.append((at, copy))
                    at, used = at + rows, used + 1
                plan.append(places)
        plan, gone = iter(plan), []
        for i, (dtype, segments) in enumerate(outputs):
            to = 0
            for rows, _ in segments:
                places = next(plan)
                for _, copy in places:
                    copy.wait()
                for low in range(0, rows, 64):
                    high = min(low + 64, rows)
                    value = added([held[p + low : p + high] for p, _ in places])
                    sums[i][to + low : to + high] = value.astype(dtype)
                to += rows
            gone.append(pltpu.make_async_copy(sums[i], outs[i], out_sems.at[i]))
            gone[-1].start()
        for copy in gone:
            copy.wait()

    shapes = [((height, D), dtype) for height, (dtype, _) in zip(heights, outputs)]
    return call(
        kernel,
        [ANY] * len(arrays),
        [shape(*s) for s in shapes],
        [ANY] * len(outputs),
        [
            pltpu.VMEM((total, D), BF),
            *[pltpu.VMEM(*s) for s in shapes],
            pltpu.SemaphoreType.DMA((copies,)),
            pltpu.SemaphoreType.DMA((len(outputs),)),
        ],
        10**6,
        8 * 10**6,
    )(*arrays)


def summed(rows, terms):
    return added([a[first : first + rows] for a, first in terms]).astype(BF)


def sent_parts(parts):
    return (BF, [p.upper() for p in parts])


def receive(parts, got):
    at = 0
    for part in parts:
        part.add(got, at)
        at += part.rows
    return got


def body(
    node_latent,
    edge_latent,
    node_cot,
    edge_src,
    edge_dst,
    edge_count,
    send_index,
    w_edge_in,
    w_edge_out,
    w_node_in,
    w_node_out,
    gain_edge,
    gain_node,
):
    micro, _, _ = node_latent.shape
    rows = edge_latent.shape[1]
    assert micro == lax.axis_size("segment") == 2
    doms, reps = lax.axis_size("dom"), lax.axis_size("rep")
    core, part, rep = (lax.axis_index(a) for a in ("segment", "dom", "rep"))
    shards = doms * reps if doms * reps == 16 else 1
    first = core == 0

    src, dst = edge_src[None], edge_dst[None]

    dma = pltpu.SemaphoreType.DMA
    halo_shape = shape((doms * HALO, D), BF)
    node_s, edge_s = pltpu.VMEM((NODE_DEV, D), BF), pltpu.VMEM((rows, D), BF)
    room_s = pltpu.VMEM((doms * HALO, D), BF)
    sent = call(
        pick_kernel,
        [VMEM, ANY],
        halo_shape,
        ANY,
        [node_s, room_s, dma((2,))],
        10**7,
        7 * 10**6,
    )(send_index, node_latent)
    halo_zero = exchange(sent)
    mine = (w_edge_in, w_edge_out, w_node_in, w_node_out)
    other = tuple(other_core(w) for w in mine)
    g_mine = jnp.concatenate([gain_edge, gain_node], axis=0)
    small = (edge_count, src, dst, send_index, g_mine, other_core(g_mine))
    small_specs = [SMEM] + [VMEM] * 5

    table_s = pltpu.VMEM((NODE_DEV + ROUNDS * HALO, D), BF)
    saved_dims, rate_dims = (saved_rows(rows), D), (rows + NODE_DEV, 128)
    layer_s = [
        *weight_scratch(),
        table_s,
        edge_s,
        pltpu.VMEM(saved_dims, BF),
        pltpu.VMEM(rate_dims, F32),
        room_s,
    ]
    node_one, edge_one, saved, rates, sent = call(
        first_kernel,
        small_specs + [ANY] * (2 + 1 + 8),
        [
            shape((NODE_DEV, D), BF),
            shape((rows, D), BF),
            shape(saved_dims, BF),
            shape(rate_dims, F32),
            halo_shape,
        ],
        [ANY] * 5,
        [*layer_s, node_s, edge_s, dma((20,))],
        11 * 10**8,
        26 * 10**6,
    )(*small, node_latent, edge_latent, halo_zero, *mine, *other)
    halo_one = exchange(sent)

    layout = Layout(shards)

    def group_rows(values):
        return [
            Rows(layout.base[g], shards * layout.size[g], values) for g in GROUPS
        ]

    share = shape((layout.rows, D), BF)
    back_shapes = [
        shape((NODE_DEV, D), F32),
        shape((rows, D), BF),
        halo_shape,
        share,
        share,
    ]
    back_s = [
        edge_s,
        edge_s,
        pltpu.VMEM((2, layout.rows, D), BF),
        pltpu.VMEM((NODE_DEV, D), F32),
        edge_s,
        dma((40,)),
    ]
    node_two, edge_two, gain_one, *done = call(
        functools.partial(second_kernel, shards),
        small_specs + [ANY] * (3 + 1 + 8),
        [shape((NODE_DEV, D), BF), shape((rows, D), BF), shape((GAINS, D), F32)] + back_shapes,
        [ANY, ANY, VMEM] + [ANY] * len(back_shapes),
        [*layer_s, node_s, edge_s, node_s, *back_s],
        28 * 10**8,
        44 * 10**6,
    )(*small, node_one, edge_one, node_cot, halo_one, *mine, *other)
    d_own, d_edges, sent, keep_one, send_one = done
    back = exchange(sent)
    one = keep_one, other_core(send_one)
    if shards > 1:
        one = group_rows(one)
        gone = [summed(*p.upper()) for p in one]
        (back,) = tied([back], gone)
        got = [receive([p], across(v, a)) for p, v, a in zip(one, gone, (1, 2))]

    d_own, d_edges, sent, keep_zero, send_zero = call(
        functools.partial(third_kernel, shards),
        small_specs + [VMEM] + [ANY] * (6 + 2 + 8),
        back_shapes,
        [ANY] * len(back_shapes),
        [*layer_s, pltpu.VMEM((NODE_DEV, D), F32), edge_s, room_s, *back_s],
        18 * 10**8,
        37 * 10**6,
    )(
        *small, gain_one, node_latent, edge_latent, d_own, d_edges, saved, rates, halo_zero,
        back, *mine, *other,
    )

    if shards > 1:
        (send_zero,) = tied([send_zero], got)
        zero = keep_zero, other_core(send_zero)
        sums = Rows(layout.gains, GAINS, zero)
        nodes, edges = group_rows(zero)
        gone = combine(
            [sent_parts(one), (BF, [edges.upper()]), (BF, [nodes.upper(), sums.whole()])]
        )
        receive(one, across(gone[0], 4))
        receive([edges], across(gone[1], 2))
        receive([nodes, sums], across(gone[2], 1))
        gone = combine(
            [(BF, [edges.upper()]), (BF, [nodes.upper(), sums.whole()]), sent_parts(one)]
        )
        (sent,) = tied([sent], gone)
        back = exchange(sent)
        receive([edges], across(gone[0], 1))
        receive([nodes, sums], across(gone[1], 2))
        receive(one, across(gone[2], 8))
        zero = [sums, nodes, edges]
        far = [
            [p.quarter(i) if p.rows > GAINS else p.whole() for p in zero] for i in range(4)
        ]
        near = [p.upper() for p in one]
        far[0] += [p.whole() for p in one]
        *far, near_n, near_e, stay = combine(
            [*[(BF, v) for v in far[1:]], *[(BF, [v]) for v in near], (F32, far[0])]
        )
        got = [across(v, 4 * i) for i, v in enumerate(far, 1)]
        near = [across(near_n, 2), across(near_e, 1)]
        rows = got[0].shape[0]
        zero = added([stay[:rows], *got])
        one = added([stay[rows:], jnp.concatenate(near, axis=0)])
        sums, zero = zero[:GAINS], zero[GAINS:]
        (back,) = tied([back], far)
    else:
        back = exchange(sent)
        zero = keep_zero, other_core(send_zero)
        rows = slice(layout.gains, layout.gains + GAINS)
        sums = lax.psum(added([v[rows] for v in zero]), ("dom", "rep"))
        one, zero = (
            jnp.concatenate([added([v[layout.span(g)] for v in x]) for g in GROUPS], axis=0)
            for x in (one, zero)
        )

    d_nodes = call(
        last_kernel,
        [VMEM] * 3,
        shape((NODE_DEV, D), BF),
        VMEM,
        [],
        10**7,
        7 * 10**6,
    )(send_index, d_own, back)

    def paired(gradient, latent):
        got = other_core(jnp.where(first, latent, gradient))
        low = jnp.where(first, gradient, got)
        high = jnp.where(first, got, latent)
        return jnp.stack([low, high])[None]

    factor = float(micro * reps * NODE_DEV * doms) ** (-0.5)
    got = other_core(jnp.where(first, one, zero))
    at, places = 0, {}
    for names in GROUPS.values():
        for name in names:
            places[name] = (at, ROWS[name] // shards // 2)
            at += places[name][1]
    scale = factor if shards > 1 else 1.0

    def grads_kernel(got, one, zero, *outs):
        mine = lax.axis_index("segment") == 0
        for out, name in zip(outs, ROWS):
            at, size = places[name]
            rows = slice(at, at + size)
            kept = jnp.where(mine, zero[rows], one[rows])
            out[:size] = jnp.where(mine, kept, got[rows]) * scale
            out[size:] = jnp.where(mine, got[rows], kept) * scale

    grads = call(
        grads_kernel,
        [VMEM] * 3,
        [shape((rows // shards, D), F32) for rows in ROWS.values()],
        [VMEM] * 4,
        [],
        10**6,
        7 * 10**6,
    )(got, one, zero)
    grads = dict(zip(ROWS, grads))
    if shards == 1:
        grads = {
            k: lax.psum_scatter(v, ("dom", "rep"), scatter_dimension=0, tiled=True) * factor
            for k, v in grads.items()
        }
    width = D // (doms * reps)
    sums = lax.dynamic_slice_in_dim(sums[:2], (part * reps + rep) * width, width, axis=1) * factor
    return (
        paired(d_nodes, node_two),
        paired(d_edges, edge_two),
        grads["ein"][None],
        grads["eout"][None],
        grads["nin"][None],
        grads["nout"][None],
        sums[:1],
        sums[1:2],
    )


def solution(mesh):
    placed = (
        P("rep", "dom", None),
        P("rep", "dom", None),
        P("rep", "dom", None),
        P("dom"),
        P("dom"),
        P("dom"),
        P("dom", None, None),
        P("segment", None, None),
        P("segment", None, None),
        P("segment", None, None),
        P("segment", None, None),
        P("segment", None),
        P("segment", None),
    )
    return jax.shard_map(
        body,
        mesh=mesh,
        in_specs=placed,
        out_specs=(
            P("segment", "rep", "dom", None),
            P("segment", "rep", "dom", None),
            P("segment", ("dom", "rep"), None),
            P("segment", ("dom", "rep"), None),
            P("segment", ("dom", "rep"), None),
            P("segment", ("dom", "rep"), None),
            P("segment", ("dom", "rep")),
            P("segment", ("dom", "rep")),
        ),
        check_vma=False,
    )
```

```python
import functools

import jax
import jax.numpy as jnp
from jax import lax
from jax.experimental import pallas as pl
from jax.experimental.pallas import tpu as pltpu
from jax.sharding import PartitionSpec as P

NODE_DEV = 128
HALO = 16
OFFSETS = (1, -1, 2, -2)
ROUNDS = len(OFFSETS)
D = 512
EPS = 1e-05
CHUNK = 384
BF = jnp.bfloat16
F32 = jnp.float32
GAINS = 16
VMEM_LIMIT = 63 * 1024 * 1024
SMALL_LIMIT = 62 * 1024 * 1024

ROWS = {"ein": 3 * D, "eout": D, "nin": 2 * D, "nout": D}
GROUPS = {"node": ("nin", "nout"), "edge": ("ein", "eout")}
SEQUENCE = (
    {"node": (0, 1, 3, 2), "edge": (1, 0, 3, 2)},
    {"node": (0, 2, 3, 1), "edge": (1, 2, 3, 0)},
)


def mm(a, b):
    return lax.dot_general(a, b, (((1,), (0,)), ((), ())), preferred_element_type=F32)


def mm_t(a, b):
    return lax.dot_general(a, b, (((1,), (1,)), ((), ())), preferred_element_type=F32)


def t_mm(a, b):
    return lax.dot_general(a, b, (((0,), (0,)), ((), ())), preferred_element_type=F32)


def one_hot(rows, index):
    where = lax.broadcasted_iota(jnp.int32, (rows, index.shape[1]), 0) == index
    return jnp.where(where, 1.0, 0.0).astype(BF)


def incidence(dst, count):
    edges = dst.shape[1]
    hit = lax.broadcasted_iota(jnp.int32, (NODE_DEV, edges), 0) == dst
    live = lax.broadcasted_iota(jnp.int32, (NODE_DEV, edges), 1) < count
    return jnp.where(hit & live, 1.0, 0.0).astype(BF)


def normed(values):
    center = values - jnp.mean(values, axis=-1, keepdims=True)
    spread = jnp.mean(center * center, axis=-1, keepdims=True)
    return center, lax.rsqrt(spread + EPS)


def silu_pair(pre):
    gate = lax.logistic(pre)
    return pre * gate, gate * (1.0 + pre * (1.0 - gate))


def norm_back(cot, hat, rate, gain):
    scaled = cot * gain
    first = jnp.mean(scaled, axis=-1, keepdims=True)
    second = jnp.mean(scaled * hat, axis=-1, keepdims=True)
    return rate * (scaled - first - hat * second)


def forward(own, edges, table, src, dst, count, weights, waits, gains, res, edges_done):
    w_ein, w_eout, w_nin, w_nout = weights
    g_edge, g_node = gains
    rows = edges.shape[0]
    hot_src = one_hot(table.shape[0], src)
    hot_dst = one_hot(NODE_DEV, dst)
    waits[0]()
    waits[1]()
    for at in range(0, rows, CHUNK):
        part = slice(at, at + CHUNK)
        edge = edges[part]
        sender = t_mm(hot_src[:, part], table[...]).astype(BF)
        receiver = t_mm(hot_dst[:, part], own[...]).astype(BF)
        pre = mm(edge, w_ein[:D]) + mm(sender, w_ein[D : 2 * D]) + mm(receiver, w_ein[2 * D :])
        middle, slope = silu_pair(pre)
        middle = middle.astype(BF)
        center, rate = normed(mm(middle, w_eout[...]))
        live = lax.broadcasted_iota(jnp.int32, (CHUNK, 1), 0) + at < count
        rate = jnp.where(live, rate, 0.0)
        hat = center * rate
        res["edge_new"][part] = (edge.astype(F32) + hat * g_edge).astype(BF)
        res["edge_mid"][part] = middle
        res["edge_slope"][part] = slope.astype(BF)
        res["edge_hat"][part] = hat.astype(BF)
        res["edge_rate"][part] = jnp.broadcast_to(rate, (CHUNK, 128))
    agg = mm(incidence(dst, count), res["edge_new"][...]).astype(BF)
    edges_done()
    waits[2]()
    waits[3]()
    pre = mm(own[...], w_nin[:D]) + mm(agg, w_nin[D:])
    middle, slope = silu_pair(pre)
    middle = middle.astype(BF)
    center, rate = normed(mm(middle, w_nout[...]))
    hat = center * rate
    res["node_new"][...] = (own[...].astype(F32) + hat * g_node).astype(BF)
    res["agg"][...] = agg
    res["node_mid"][...] = middle
    res["node_slope"][...] = slope.astype(BF)
    res["node_hat"][...] = hat.astype(BF)
    res["node_rate"][...] = jnp.broadcast_to(rate, (NODE_DEV, 128))


def slot_of(shard, me, shards, sequence):
    if shards == 1:
        return 0
    apart = jnp.bitwise_xor(jnp.int32(shard), me)
    slot = jnp.int32(0)
    for bit in sequence:
        slot = slot * 2 + jnp.bitwise_and(lax.shift_right_logical(apart, jnp.int32(bit)), 1)
    return slot


class Layout:
    def __init__(self, shards):
        self.shards = shards
        self.half = {name: rows // shards // 2 for name, rows in ROWS.items()}
        self.size = {g: sum(self.half[n] for n in names) for g, names in GROUPS.items()}
        self.gains = shards * self.size["node"]
        self.base = {"node": 0, "edge": self.gains + GAINS}
        self.rows = self.base["edge"] + shards * self.size["edge"]
        self.inner = {}
        for names in GROUPS.values():
            at = 0
            for name in names:
                self.inner[name] = at
                at += self.half[name]

    def span(self, group):
        return slice(self.base[group], self.base[group] + self.shards * self.size[group])


def emit(value, name, first_row, layout, group, store, core, slots):
    half = layout.half[name]
    value = value.astype(BF)
    last_row = first_row + value.shape[0]
    for piece in range(2 * layout.shards):
        low, high = max(piece * half, first_row), min((piece + 1) * half, last_row)
        if low < high:
            keep = jnp.bitwise_xor(core, piece % 2)
            to = layout.base[group] + layout.inner[name] + low - piece * half
            if layout.shards > 1:
                to = pl.multiple_of(slots[piece // 2] * layout.size[group] + to, 16)
            store[keep, pl.ds(to, high - low), :] = value[low - first_row : high - first_row]


def backward(
    cot_node, cot_edge, own, edges, table, src, dst, count, weights, gains, res, core, me, layout, sequence,
    store, outs, work, ready, arrive,
):
    w_ein, w_eout, w_nin, w_nout = weights
    g_edge, g_node = gains
    d_own_out, d_edges_out, room, put_gains = outs
    d_outer, d_pre = work
    rows = edges.shape[0]
    shards = layout.shards
    slots = {
        g: [slot_of(i, me, shards, sequence[g]) for i in range(shards)] for g in GROUPS
    }

    def put(value, name, first_row):
        group = "node" if name in GROUPS["node"] else "edge"
        emit(value, name, first_row, layout, group, store, core, slots[group])

    hat = res["node_hat"][...].astype(F32)
    gain_node = jnp.sum(cot_node * hat, axis=0, keepdims=True)
    d_out = norm_back(cot_node, hat, res["node_rate"][:, :1], g_node).astype(BF)
    put(t_mm(res["node_mid"][...], d_out), "nout", 0)
    d_pre_node = (mm_t(d_out, w_nout[...]) * res["node_slope"][...].astype(F32)).astype(BF)
    put(t_mm(own[...], d_pre_node), "nin", 0)
    put(t_mm(res["agg"][...], d_pre_node), "nin", D)
    ready("node")
    d_own = cot_node + mm_t(d_pre_node, w_nin[:D])
    d_agg = mm_t(d_pre_node, w_nin[D:]).astype(BF)

    arrive()
    joins = incidence(dst, count)
    gain_edge = jnp.zeros((1, D), F32)
    for at in range(0, rows, CHUNK):
        part = slice(at, at + CHUNK)
        cot = t_mm(joins[:, part], d_agg)
        if cot_edge is not None:
            cot = cot + cot_edge[part].astype(F32)
        hat = res["edge_hat"][part].astype(F32)
        gain_edge = gain_edge + jnp.sum(cot * hat, axis=0, keepdims=True)
        outer = norm_back(cot, hat, res["edge_rate"][part, :1], g_edge).astype(BF)
        d_outer[part] = outer
        pre = (mm_t(outer, w_eout[...]) * res["edge_slope"][part].astype(F32)).astype(BF)
        d_pre[part] = pre
        d_edges_out[part] = (cot + mm_t(pre, w_ein[:D])).astype(BF)
    put(t_mm(res["edge_mid"][...], d_outer[...]), "eout", 0)
    put(t_mm(edges[...], d_pre[...]), "ein", 0)
    to_src = mm(one_hot(table.shape[0], src), d_pre[...]).astype(BF)
    to_dst = mm(one_hot(NODE_DEV, dst), d_pre[...]).astype(BF)
    put(t_mm(table[...], to_src), "ein", D)
    put(t_mm(own[...], to_dst), "ein", 2 * D)
    put_gains(jnp.concatenate([gain_edge, gain_node, jnp.zeros((GAINS - 2, D), F32)], axis=0))
    ready("edge")
    d_table = mm_t(to_src, w_ein[D : 2 * D])
    d_own = d_own + d_table[:NODE_DEV] + mm_t(to_dst, w_ein[2 * D :])
    d_own_out[...] = d_own
    d_halo = d_table[NODE_DEV:].astype(BF)
    place(-1, [d_halo[j * HALO : (j + 1) * HALO] for j in range(ROUNDS)], room)


SAVED = (
    ("edge_mid", None),
    ("edge_slope", None),
    ("edge_hat", None),
    ("agg", NODE_DEV),
    ("node_mid", NODE_DEV),
    ("node_slope", NODE_DEV),
    ("node_hat", NODE_DEV),
)


def saved_rows(rows):
    return sum(h or rows for _, h in SAVED)


def views(rows, held, rates):
    out, at = {}, 0
    for name, height in SAVED:
        out[name] = held.at[at : at + (height or rows)]
        at += height or rows
    out["edge_rate"] = rates.at[:rows]
    out["node_rate"] = rates.at[rows : rows + NODE_DEV]
    return out


class Copies:
    def __init__(self, sems):
        self.sems, self.used, self.out = sems, 0, []

    def start(self, source, target):
        copy = pltpu.make_async_copy(source, target, self.sems.at[self.used])
        self.used += 1
        copy.start()
        return copy

    def send(self, source, target):
        self.out.append(self.start(source, target))

    def either(self, choice, yes, no, targets):
        sems = [self.sems.at[self.used + i] for i in range(len(targets))]
        self.used += len(targets)

        def start(refs):
            for ref, to, sem in zip(refs, targets, sems):
                pltpu.make_async_copy(ref, to, sem).start()

        pl.when(choice)(lambda: start(yes))
        pl.when(jnp.logical_not(choice))(lambda: start(no))
        return [
            pltpu.make_async_copy(ref, to, sem).wait for ref, to, sem in zip(yes, targets, sems)
        ]

    def finish(self):
        for copy in self.out:
            copy.wait()


def shard_number(shards):
    if shards == 1:
        return jnp.int32(0)
    return lax.axis_index("dom") * lax.axis_size("rep") + lax.axis_index("rep")


def first_rows(refs):
    return [ref.at[0] for ref in refs]


def one_hots(lists):
    return [one_hot(NODE_DEV, lists[0, j : j + 1]) for j in range(ROUNDS)]


def place(sign, pieces, room):
    part, parts = lax.axis_index("dom"), lax.axis_size("dom")
    room[...] = jnp.zeros_like(room)
    for piece, offset in zip(pieces, OFFSETS):
        to = part + sign * offset

        def put(piece=piece, to=to):
            room[pl.ds(pl.multiple_of(to * HALO, HALO), HALO), :] = piece

        pl.when((to >= 0) & (to < parts))(put)


def placed(sign, room):
    part, parts = lax.axis_index("dom"), lax.axis_size("dom")
    out = []
    for offset in OFFSETS:
        source = part + sign * offset
        there = jnp.clip(source, 0, parts - 1)
        rows = room[pl.ds(pl.multiple_of(there * HALO, HALO), HALO), :]
        out.append(jnp.where((source >= 0) & (source < parts), rows, jnp.zeros_like(rows)))
    return out


def pick(hot, values):
    return [t_mm(one, values).astype(BF) for one in hot]


def fill_halo(table, room):
    for j, rows in enumerate(placed(-1, room)):
        table[NODE_DEV + j * HALO : NODE_DEV + (j + 1) * HALO] = rows


def spread(hot, pieces):
    total = mm(hot[0], pieces[0])
    for j in range(1, ROUNDS):
        total = total + mm(hot[j], pieces[j])
    return total


def pick_kernel(lists, nodes, sent, own, room, sems):
    copies = Copies(sems)
    copy = copies.start(nodes.at[lax.axis_index("segment")], own)
    hot = one_hots(lists)
    copy.wait()
    place(1, pick(hot, own[...]), room)
    copies.send(room, sent)
    copies.finish()


def first_kernel(count, src, dst, lists, g_mine, g_other, nodes, latents, *rest):
    halo, mine, other, rest = rest[0], rest[1:5], rest[5:9], rest[9:]
    (node_out, edge_out, saved_out, rate_out, sent), rest = rest[:5], rest[5:]
    held, rest = rest[:4], rest[4:]
    table, edges, saved, rates, room, node_new, edge_new, sems = rest
    core = lax.axis_index("segment")
    own = table.at[:NODE_DEV]
    copies = Copies(sems)
    coming = [copies.start(nodes.at[core], own), copies.start(latents.at[core], edges)]
    coming += [copies.start(halo, room)]
    waits = copies.either(core == 0, first_rows(mine), first_rows(other), held)
    src, dst = src[...], dst[...]
    gains = jnp.where(core == 0, g_mine[...], g_other[...])
    res = views(edges.shape[0], saved, rates)
    res.update(node_new=node_new, edge_new=edge_new)
    for copy in coming:
        copy.wait()
    fill_halo(table, room)
    tall = 3 * edges.shape[0]

    def edges_done():
        copies.send(edge_new, edge_out)
        copies.send(saved.at[:tall], saved_out.at[:tall])

    forward(
        own, edges, table, src, dst, count[0], held, waits, (gains[:1], gains[1:2]), res,
        edges_done,
    )
    place(1, pick(one_hots(lists), node_new[...]), room)
    for source, target in (
        (room, sent),
        (node_new, node_out),
        (saved.at[tall:], saved_out.at[tall:]),
        (rates, rate_out),
    ):
        copies.send(source, target)
    copies.finish()


def back_outs(copies, layout, store, outs, work):
    d_own, d_edges, sent, keep, send = outs
    d_own_s, d_edges_s, room = work

    def ready(group):
        first = layout.base[group] if group == "node" else layout.gains
        rows = pl.ds(first, layout.span(group).stop - first)
        copies.send(store.at[1, rows], send.at[rows])
        copies.send(store.at[0, rows], keep.at[rows])

    def finish():
        copies.send(room, sent)
        copies.send(d_own_s, d_own)
        copies.send(d_edges_s, d_edges)
        copies.finish()

    return ready, finish


def second_kernel(shards, count, src, dst, lists, g_mine, g_other, nodes, latents, cots, *rest):
    halo, mine, other, rest = rest[0], rest[1:5], rest[5:9], rest[9:]
    (node_out, edge_out, gain_out), rest = rest[:3], rest[3:]
    outs, rest = rest[:5], rest[5:]
    held, rest = rest[:4], rest[4:]
    table, edges, saved, rates, room, node_new, edge_new, cot, rest = *rest[:8], rest[8:]
    d_outer, d_pre, store, *work, sems = rest
    layout = Layout(shards)
    core, me = lax.axis_index("segment"), shard_number(shards)
    own = table.at[:NODE_DEV]
    copies = Copies(sems)
    coming = [copies.start(nodes, own), copies.start(latents, edges)]
    coming += [copies.start(halo, room)]
    waits = copies.either(core == 1, first_rows(mine), first_rows(other), held)
    cot_copy = copies.start(cots.at[core], cot)
    src, dst = src[...], dst[...]
    gains = jnp.where(core == 1, g_mine[...], g_other[...])
    gains = (gains[:1], gains[1:2])
    res = views(edges.shape[0], saved, rates)
    res.update(node_new=node_new, edge_new=edge_new)
    for copy in coming:
        copy.wait()
    fill_halo(table, room)
    forward(
        own, edges, table, src, dst, count[0], held, waits, gains, res,
        lambda: copies.send(edge_new, edge_out),
    )
    copies.send(node_new, node_out)
    cot_copy.wait()
    ready, finish = back_outs(copies, layout, store, outs, (*work, room))

    def put_gains(value):
        gain_out[...] = value
        for side in range(2):
            store[side, layout.gains : layout.gains + GAINS] = jnp.zeros((GAINS, D), BF)

    backward(
        cot[...].astype(F32), None, own, edges, table, src, dst, count[0], held, gains, res,
        core, me, layout, SEQUENCE[1], store, (*work[:2], room, put_gains), (d_outer, d_pre), ready, lambda: None,
    )
    finish()


def third_kernel(
    shards, count, src, dst, lists, g_mine, g_other, gain_one, nodes, latents, d_own_in,
    d_edges_in, saved_in, rate_in, *rest
):
    halo, back, mine, other, rest = rest[0], rest[1], rest[2:6], rest[6:10], rest[10:]
    outs, rest = rest[:5], rest[5:]
    held, rest = rest[:4], rest[4:]
    table, edges, saved, rates, room, cot_own, cot_edge, got, rest = *rest[:8], rest[8:]
    d_outer, d_pre, store, *work, sems = rest
    layout = Layout(shards)
    core, me = lax.axis_index("segment"), shard_number(shards)
    own = table.at[:NODE_DEV]
    copies = Copies(sems)
    tall = 3 * edges.shape[0]
    coming = [copies.start(back, got), copies.start(d_own_in, cot_own)]
    coming += [copies.start(rate_in, rates), copies.start(nodes.at[core], own)]
    coming += [copies.start(saved_in.at[tall:], saved.at[tall:]), copies.start(halo, room)]
    order = (3, 2, 1, 0)
    waits = copies.either(
        core == 0, *[[v[i] for i in order] for v in (first_rows(mine), first_rows(other), held)]
    )
    waits = [waits[i] for i in order]
    late = [copies.start(d_edges_in, cot_edge), copies.start(saved_in.at[:tall], saved.at[:tall])]
    late += [copies.start(latents.at[core], edges)]
    src, dst = src[...], dst[...]
    gains = jnp.where(core == 0, g_mine[...], g_other[...])
    gains = (gains[:1], gains[1:2])
    res = views(edges.shape[0], saved, rates)
    hot = one_hots(lists)
    for copy in coming:
        copy.wait()
    fill_halo(table, room)
    cot = (cot_own[...] + spread(hot, placed(1, got))).astype(BF).astype(F32)
    waits[3]()
    waits[2]()

    def arrive():
        for copy in late:
            copy.wait()
        waits[1]()
        waits[0]()

    ready, finish = back_outs(copies, layout, store, outs, (*work, room))

    def put_gains(value):
        both = (value.astype(BF), gain_one[...].astype(BF))
        rows = slice(layout.gains, layout.gains + GAINS)
        store[0, rows] = jnp.where(core == 0, both[0], both[1])
        store[1, rows] = jnp.where(core == 0, both[1], both[0])

    backward(
        cot, cot_edge, own, edges, table, src, dst, count[0], held, gains, res,
        core, me, layout, SEQUENCE[0], store, (*work[:2], room, put_gains), (d_outer, d_pre), ready, arrive,
    )
    finish()


def last_kernel(lists, d_own, back, out):
    out[...] = (d_own[...] + spread(one_hots(lists), placed(1, back))).astype(BF)


def weight_scratch():
    return [pltpu.VMEM((r, D), BF) for r in ROWS.values()]


SMEM = pl.BlockSpec(memory_space=pltpu.SMEM)
VMEM = pl.BlockSpec(memory_space=pltpu.VMEM)
ANY = pl.BlockSpec(memory_space=pl.ANY)


def shape(dims, dtype):
    return jax.ShapeDtypeStruct(tuple(dims), dtype)


def call(kernel, in_specs, outs, out_specs, scratch, flops, traffic, limit=SMALL_LIMIT):
    return pl.pallas_call(
        kernel,
        in_specs=in_specs,
        out_shape=outs,
        out_specs=out_specs,
        scratch_shapes=scratch,
        compiler_params=pltpu.CompilerParams(vmem_limit_bytes=limit),
        cost_estimate=pl.CostEstimate(flops=flops, bytes_accessed=traffic, transcendentals=0),
    )


def exchange(rows):
    return lax.all_to_all(rows, "dom", 0, 0, tiled=True)


def other_core(value):
    return lax.ppermute(value, "segment", [(0, 1), (1, 0)])


def across(value, apart):
    if apart == 1:
        return lax.ppermute(value, "rep", [(0, 1), (1, 0)])
    step = apart // 2
    return lax.ppermute(value, "dom", [(p, p ^ step) for p in range(lax.axis_size("dom"))])


def added(pieces):
    total = pieces[0].astype(F32)
    for piece in pieces[1:]:
        total = total + piece.astype(F32)
    return total


def tied(values, others):
    return lax.optimization_barrier((list(values), list(others)))[0]


class Rows:
    def __init__(self, first, rows, arrays):
        self.rows, self.terms = rows, [(a, first) for a in arrays]

    def upper(self):
        self.rows //= 2
        return self.rows, [(a, first + self.rows) for a, first in self.terms]

    def whole(self):
        return self.rows, list(self.terms)

    def quarter(self, i):
        rows = self.rows // 4
        return rows, [(a, first + i * rows) for a, first in self.terms]

    def add(self, array, first):
        self.terms.append((array, first))


def combine(outputs):
    arrays = []
    for _, segments in outputs:
        for _, terms in segments:
            arrays += [a for a, _ in terms if all(a is not b for b in arrays)]
    total = sum(rows * len(terms) for _, segments in outputs for rows, terms in segments)
    copies = sum(len(terms) for _, segments in outputs for _, terms in segments)
    heights = [sum(rows for rows, _ in segments) for _, segments in outputs]

    def kernel(*refs):
        sources, refs = refs[: len(arrays)], refs[len(arrays) :]
        outs, refs = refs[: len(outputs)], refs[len(outputs) :]
        held, sums, sems, out_sems = refs[0], refs[1:-2], refs[-2], refs[-1]
        plan, at, used = [], 0, 0
        for _, segments in outputs:
            for rows, terms in segments:
                places = []
                for array, first in terms:
                    which = [array is a for a in arrays].index(True)
                    copy = pltpu.make_async_copy(
                        sources[which].at[first : first + rows],
                        held.at[at : at + rows],
                        sems.at[used],
                    )
                    copy.start()
                    places.append((at, copy))
                    at, used = at + rows, used + 1
                plan.append(places)
        plan, gone = iter(plan), []
        for i, (dtype, segments) in enumerate(outputs):
            to = 0
            for rows, _ in segments:
                places = next(plan)
                for _, copy in places:
                    copy.wait()
                for low in range(0, rows, 64):
                    high = min(low + 64, rows)
                    value = added([held[p + low : p + high] for p, _ in places])
                    sums[i][to + low : to + high] = value.astype(dtype)
                to += rows
            gone.append(pltpu.make_async_copy(sums[i], outs[i], out_sems.at[i]))
            gone[-1].start()
        for copy in gone:
            copy.wait()

    shapes = [((height, D), dtype) for height, (dtype, _) in zip(heights, outputs)]
    return call(
        kernel,
        [ANY] * len(arrays),
        [shape(*s) for s in shapes],
        [ANY] * len(outputs),
        [
            pltpu.VMEM((total, D), BF),
            *[pltpu.VMEM(*s) for s in shapes],
            pltpu.SemaphoreType.DMA((copies,)),
            pltpu.SemaphoreType.DMA((len(outputs),)),
        ],
        10**6,
        8 * 10**6,
    )(*arrays)


def summed(rows, terms):
    return added([a[first : first + rows] for a, first in terms]).astype(BF)


def sent_parts(parts):
    return (BF, [p.upper() for p in parts])


def receive(parts, got):
    at = 0
    for part in parts:
        part.add(got, at)
        at += part.rows
    return got


def body(
    node_latent,
    edge_latent,
    node_cot,
    edge_src,
    edge_dst,
    edge_count,
    send_index,
    w_edge_in,
    w_edge_out,
    w_node_in,
    w_node_out,
    gain_edge,
    gain_node,
):
    micro, _, _ = node_latent.shape
    rows = edge_latent.shape[1]
    assert micro == lax.axis_size("segment") == 2
    doms, reps = lax.axis_size("dom"), lax.axis_size("rep")
    core, part, rep = (lax.axis_index(a) for a in ("segment", "dom", "rep"))
    shards = doms * reps if doms * reps == 16 else 1
    first = core == 0

    src, dst = edge_src[None], edge_dst[None]

    dma = pltpu.SemaphoreType.DMA
    halo_shape = shape((doms * HALO, D), BF)
    node_s, edge_s = pltpu.VMEM((NODE_DEV, D), BF), pltpu.VMEM((rows, D), BF)
    room_s = pltpu.VMEM((doms * HALO, D), BF)
    sent = call(
        pick_kernel,
        [VMEM, ANY],
        halo_shape,
        ANY,
        [node_s, room_s, dma((2,))],
        10**7,
        7 * 10**6,
    )(send_index, node_latent)
    halo_zero = exchange(sent)
    mine = (w_edge_in, w_edge_out, w_node_in, w_node_out)
    other = tuple(other_core(w) for w in mine)
    g_mine = jnp.concatenate([gain_edge, gain_node], axis=0)
    small = (edge_count, src, dst, send_index, g_mine, other_core(g_mine))
    small_specs = [SMEM] + [VMEM] * 5

    table_s = pltpu.VMEM((NODE_DEV + ROUNDS * HALO, D), BF)
    saved_dims, rate_dims = (saved_rows(rows), D), (rows + NODE_DEV, 128)
    layer_s = [
        *weight_scratch(),
        table_s,
        edge_s,
        pltpu.VMEM(saved_dims, BF),
        pltpu.VMEM(rate_dims, F32),
        room_s,
    ]
    node_one, edge_one, saved, rates, sent = call(
        first_kernel,
        small_specs + [ANY] * (2 + 1 + 8),
        [
            shape((NODE_DEV, D), BF),
            shape((rows, D), BF),
            shape(saved_dims, BF),
            shape(rate_dims, F32),
            halo_shape,
        ],
        [ANY] * 5,
        [*layer_s, node_s, edge_s, dma((20,))],
        11 * 10**8,
        26 * 10**6,
        VMEM_LIMIT,
    )(*small, node_latent, edge_latent, halo_zero, *mine, *other)
    halo_one = exchange(sent)

    layout = Layout(shards)

    def group_rows(values):
        return [
            Rows(layout.base[g], shards * layout.size[g], values) for g in GROUPS
        ]

    share = shape((layout.rows, D), BF)
    back_shapes = [
        shape((NODE_DEV, D), F32),
        shape((rows, D), BF),
        halo_shape,
        share,
        share,
    ]
    back_s = [
        edge_s,
        edge_s,
        pltpu.VMEM((2, layout.rows, D), BF),
        pltpu.VMEM((NODE_DEV, D), F32),
        edge_s,
        dma((40,)),
    ]
    node_two, edge_two, gain_one, *done = call(
        functools.partial(second_kernel, shards),
        small_specs + [ANY] * (3 + 1 + 8),
        [shape((NODE_DEV, D), BF), shape((rows, D), BF), shape((GAINS, D), F32)] + back_shapes,
        [ANY, ANY, VMEM] + [ANY] * len(back_shapes),
        [*layer_s, node_s, edge_s, node_s, *back_s],
        28 * 10**8,
        44 * 10**6,
        VMEM_LIMIT,
    )(*small, node_one, edge_one, node_cot, halo_one, *mine, *other)
    d_own, d_edges, sent, keep_one, send_one = done
    back = exchange(sent)
    one = keep_one, other_core(send_one)
    if shards > 1:
        one = group_rows(one)
        gone = [summed(*p.upper()) for p in one]
        (back,) = tied([back], gone)
        got = [receive([p], across(v, a)) for p, v, a in zip(one, gone, (1, 2))]

    d_own, d_edges, sent, keep_zero, send_zero = call(
        functools.partial(third_kernel, shards),
        small_specs + [VMEM] + [ANY] * (6 + 2 + 8),
        back_shapes,
        [ANY] * len(back_shapes),
        [*layer_s, pltpu.VMEM((NODE_DEV, D), F32), edge_s, room_s, *back_s],
        18 * 10**8,
        37 * 10**6,
        VMEM_LIMIT,
    )(
        *small, gain_one, node_latent, edge_latent, d_own, d_edges, saved, rates, halo_zero,
        back, *mine, *other,
    )

    if shards > 1:
        (send_zero,) = tied([send_zero], got)
        zero = keep_zero, other_core(send_zero)
        sums = Rows(layout.gains, GAINS, zero)
        nodes, edges = group_rows(zero)
        gone = combine(
            [sent_parts(one), (BF, [edges.upper()]), (BF, [nodes.upper(), sums.whole()])]
        )
        receive(one, across(gone[0], 4))
        receive([edges], across(gone[1], 2))
        receive([nodes, sums], across(gone[2], 1))
        gone = combine(
            [(BF, [edges.upper()]), (BF, [nodes.upper(), sums.whole()]), sent_parts(one)]
        )
        (sent,) = tied([sent], gone)
        back = exchange(sent)
        receive([edges], across(gone[0], 1))
        receive([nodes, sums], across(gone[1], 2))
        receive(one, across(gone[2], 8))
        zero = [sums, nodes, edges]
        far = [
            [p.quarter(i) if p.rows > GAINS else p.whole() for p in zero] for i in range(4)
        ]
        *far, stay = combine([*[(BF, v) for v in far[1:]], (F32, far[0])])
        got = [across(v, 4 * i) for i, v in enumerate(far, 1)]
        got_one = tied([one[1].terms.pop()[0]], far)[0]
        one[0].terms.pop()
        receive(one, got_one)
        near = [p.upper() for p in one]
        near_n, near_e, stay_one = combine(
            [*[(BF, [v]) for v in near], (F32, [p.whole() for p in one])]
        )
        near = [across(near_n, 2), across(near_e, 1)]
        zero = added([stay, *got])
        one = added([stay_one, jnp.concatenate(near, axis=0)])
        sums, zero = zero[:GAINS], zero[GAINS:]
        (back,) = tied([back], far)
    else:
        back = exchange(sent)
        zero = keep_zero, other_core(send_zero)
        rows = slice(layout.gains, layout.gains + GAINS)
        sums = lax.psum(added([v[rows] for v in zero]), ("dom", "rep"))
        one, zero = (
            jnp.concatenate([added([v[layout.span(g)] for v in x]) for g in GROUPS], axis=0)
            for x in (one, zero)
        )

    d_nodes = call(
        last_kernel,
        [VMEM] * 3,
        shape((NODE_DEV, D), BF),
        VMEM,
        [],
        10**7,
        7 * 10**6,
    )(send_index, d_own, back)

    def paired(gradient, latent):
        got = other_core(jnp.where(first, latent, gradient))
        low = jnp.where(first, gradient, got)
        high = jnp.where(first, got, latent)
        return jnp.stack([low, high])[None]

    factor = float(micro * reps * NODE_DEV * doms) ** (-0.5)
    got = other_core(jnp.where(first, one, zero))
    at, places = 0, {}
    for names in GROUPS.values():
        for name in names:
            places[name] = (at, ROWS[name] // shards // 2)
            at += places[name][1]
    scale = factor if shards > 1 else 1.0

    def grads_kernel(got, one, zero, *outs):
        mine = lax.axis_index("segment") == 0
        for out, name in zip(outs, ROWS):
            at, size = places[name]
            rows = slice(at, at + size)
            kept = jnp.where(mine, zero[rows], one[rows])
            out[:size] = jnp.where(mine, kept, got[rows]) * scale
            out[size:] = jnp.where(mine, got[rows], kept) * scale

    grads = call(
        grads_kernel,
        [VMEM] * 3,
        [shape((rows // shards, D), F32) for rows in ROWS.values()],
        [VMEM] * 4,
        [],
        10**6,
        7 * 10**6,
        16 * 1024 * 1024,
    )(got, one, zero)
    grads = dict(zip(ROWS, grads))
    if shards == 1:
        grads = {
            k: lax.psum_scatter(v, ("dom", "rep"), scatter_dimension=0, tiled=True) * factor
            for k, v in grads.items()
        }
    width = D // (doms * reps)
    sums = lax.dynamic_slice_in_dim(sums[:2], (part * reps + rep) * width, width, axis=1) * factor
    return (
        paired(d_nodes, node_two),
        paired(d_edges, edge_two),
        grads["ein"][None],
        grads["eout"][None],
        grads["nin"][None],
        grads["nout"][None],
        sums[:1],
        sums[1:2],
    )


def solution(mesh):
    placed = (
        P("rep", "dom", None),
        P("rep", "dom", None),
        P("rep", "dom", None),
        P("dom"),
        P("dom"),
        P("dom"),
        P("dom", None, None),
        P("segment", None, None),
        P("segment", None, None),
        P("segment", None, None),
        P("segment", None, None),
        P("segment", None),
        P("segment", None),
    )
    return jax.shard_map(
        body,
        mesh=mesh,
        in_specs=placed,
        out_specs=(
            P("segment", "rep", "dom", None),
            P("segment", "rep", "dom", None),
            P("segment", ("dom", "rep"), None),
            P("segment", ("dom", "rep"), None),
            P("segment", ("dom", "rep"), None),
            P("segment", ("dom", "rep"), None),
            P("segment", ("dom", "rep")),
            P("segment", ("dom", "rep")),
        ),
        check_vma=False,
    )
```

```python
import functools

import jax
import jax.numpy as jnp
from jax import lax
from jax.experimental import pallas as pl
from jax.experimental.pallas import tpu as pltpu
from jax.sharding import PartitionSpec as P

NODE_DEV = 128
HALO = 16
OFFSETS = (1, -1, 2, -2)
ROUNDS = len(OFFSETS)
D = 512
EPS = 1e-05
CHUNK = 384
BF = jnp.bfloat16
F32 = jnp.float32
GAINS = 16
VMEM_LIMIT = 63 * 1024 * 1024
SMALL_LIMIT = 59 * 1024 * 1024

ROWS = {"ein": 3 * D, "eout": D, "nin": 2 * D, "nout": D}
GROUPS = {"node": ("nin", "nout"), "edge": ("ein", "eout")}
SEQUENCE = (
    {"node": (0, 1, 3, 2), "edge": (1, 0, 3, 2)},
    {"node": (0, 2, 3, 1), "edge": (1, 2, 3, 0)},
)


def mm(a, b):
    return lax.dot_general(a, b, (((1,), (0,)), ((), ())), preferred_element_type=F32)


def mm_t(a, b):
    return lax.dot_general(a, b, (((1,), (1,)), ((), ())), preferred_element_type=F32)


def t_mm(a, b):
    return lax.dot_general(a, b, (((0,), (0,)), ((), ())), preferred_element_type=F32)


def one_hot(rows, index):
    where = lax.broadcasted_iota(jnp.int32, (rows, index.shape[1]), 0) == index
    return jnp.where(where, 1.0, 0.0).astype(BF)


def incidence(dst, count):
    edges = dst.shape[1]
    hit = lax.broadcasted_iota(jnp.int32, (NODE_DEV, edges), 0) == dst
    live = lax.broadcasted_iota(jnp.int32, (NODE_DEV, edges), 1) < count
    return jnp.where(hit & live, 1.0, 0.0).astype(BF)


def normed(values):
    center = values - jnp.mean(values, axis=-1, keepdims=True)
    spread = jnp.mean(center * center, axis=-1, keepdims=True)
    return center, lax.rsqrt(spread + EPS)


def silu_pair(pre):
    gate = lax.logistic(pre)
    return pre * gate, gate * (1.0 + pre * (1.0 - gate))


def norm_back(cot, hat, rate, gain):
    scaled = cot * gain
    first = jnp.mean(scaled, axis=-1, keepdims=True)
    second = jnp.mean(scaled * hat, axis=-1, keepdims=True)
    return rate * (scaled - first - hat * second)


def forward(own, edges, table, src, dst, count, weights, waits, gains, res, edges_done):
    w_ein, w_eout, w_nin, w_nout = weights
    g_edge, g_node = gains
    rows = edges.shape[0]
    hot_src = one_hot(table.shape[0], src)
    hot_dst = one_hot(NODE_DEV, dst)
    waits[0]()
    waits[1]()
    for at in range(0, rows, CHUNK):
        part = slice(at, at + CHUNK)
        edge = edges[part]
        sender = t_mm(hot_src[:, part], table[...]).astype(BF)
        receiver = t_mm(hot_dst[:, part], own[...]).astype(BF)
        pre = mm(edge, w_ein[:D]) + mm(sender, w_ein[D : 2 * D]) + mm(receiver, w_ein[2 * D :])
        middle, slope = silu_pair(pre)
        middle = middle.astype(BF)
        center, rate = normed(mm(middle, w_eout[...]))
        live = lax.broadcasted_iota(jnp.int32, (CHUNK, 1), 0) + at < count
        rate = jnp.where(live, rate, 0.0)
        hat = center * rate
        res["edge_new"][part] = (edge.astype(F32) + hat * g_edge).astype(BF)
        res["edge_mid"][part] = middle
        res["edge_slope"][part] = slope.astype(BF)
        res["edge_hat"][part] = hat.astype(BF)
        res["edge_rate"][part] = jnp.broadcast_to(rate, (CHUNK, 128))
    agg = mm(incidence(dst, count), res["edge_new"][...]).astype(BF)
    edges_done()
    waits[2]()
    waits[3]()
    pre = mm(own[...], w_nin[:D]) + mm(agg, w_nin[D:])
    middle, slope = silu_pair(pre)
    middle = middle.astype(BF)
    center, rate = normed(mm(middle, w_nout[...]))
    hat = center * rate
    res["node_new"][...] = (own[...].astype(F32) + hat * g_node).astype(BF)
    res["agg"][...] = agg
    res["node_mid"][...] = middle
    res["node_slope"][...] = slope.astype(BF)
    res["node_hat"][...] = hat.astype(BF)
    res["node_rate"][...] = jnp.broadcast_to(rate, (NODE_DEV, 128))


def slot_of(shard, me, shards, sequence):
    if shards == 1:
        return 0
    apart = jnp.bitwise_xor(jnp.int32(shard), me)
    slot = jnp.int32(0)
    for bit in sequence:
        slot = slot * 2 + jnp.bitwise_and(lax.shift_right_logical(apart, jnp.int32(bit)), 1)
    return slot


class Layout:
    def __init__(self, shards):
        self.shards = shards
        self.half = {name: rows // shards // 2 for name, rows in ROWS.items()}
        self.size = {g: sum(self.half[n] for n in names) for g, names in GROUPS.items()}
        self.gains = shards * self.size["node"]
        self.base = {"node": 0, "edge": self.gains + GAINS}
        self.rows = self.base["edge"] + shards * self.size["edge"]
        self.inner = {}
        for names in GROUPS.values():
            at = 0
            for name in names:
                self.inner[name] = at
                at += self.half[name]

    def parcel(self, group):
        return slice(0, self.gains) if group == "node" else slice(self.gains, self.rows)

    def extent(self, group):
        return (0 if group == "node" else GAINS), self.shards * self.size[group]


def emit(value, name, first_row, layout, group, store, core, slots):
    half = layout.half[name]
    value = value.astype(BF)
    last_row = first_row + value.shape[0]
    for piece in range(2 * layout.shards):
        low, high = max(piece * half, first_row), min((piece + 1) * half, last_row)
        if low < high:
            keep = jnp.bitwise_xor(core, piece % 2)
            to = layout.base[group] + layout.inner[name] + low - piece * half
            if layout.shards > 1:
                to = pl.multiple_of(slots[piece // 2] * layout.size[group] + to, 16)
            store[keep, pl.ds(to, high - low), :] = value[low - first_row : high - first_row]


def backward(
    cot_node, cot_edge, own, edges, table, src, dst, count, weights, gains, res, core, me, layout, sequence,
    store, outs, work, ready, arrive,
):
    w_ein, w_eout, w_nin, w_nout = weights
    g_edge, g_node = gains
    d_own_out, d_edges_out, room, put_gains = outs
    d_outer, d_pre = work
    rows = edges.shape[0]
    shards = layout.shards
    slots = {
        g: [slot_of(i, me, shards, sequence[g]) for i in range(shards)] for g in GROUPS
    }

    def put(value, name, first_row):
        group = "node" if name in GROUPS["node"] else "edge"
        emit(value, name, first_row, layout, group, store, core, slots[group])

    hat = res["node_hat"][...].astype(F32)
    gain_node = jnp.sum(cot_node * hat, axis=0, keepdims=True)
    d_out = norm_back(cot_node, hat, res["node_rate"][:, :1], g_node).astype(BF)
    put(t_mm(res["node_mid"][...], d_out), "nout", 0)
    d_pre_node = (mm_t(d_out, w_nout[...]) * res["node_slope"][...].astype(F32)).astype(BF)
    put(t_mm(own[...], d_pre_node), "nin", 0)
    put(t_mm(res["agg"][...], d_pre_node), "nin", D)
    ready("node")
    d_own = cot_node + mm_t(d_pre_node, w_nin[:D])
    d_agg = mm_t(d_pre_node, w_nin[D:]).astype(BF)

    arrive()
    joins = incidence(dst, count)
    gain_edge = jnp.zeros((1, D), F32)
    for at in range(0, rows, CHUNK):
        part = slice(at, at + CHUNK)
        cot = t_mm(joins[:, part], d_agg)
        if cot_edge is not None:
            cot = cot + cot_edge[part].astype(F32)
        hat = res["edge_hat"][part].astype(F32)
        gain_edge = gain_edge + jnp.sum(cot * hat, axis=0, keepdims=True)
        outer = norm_back(cot, hat, res["edge_rate"][part, :1], g_edge).astype(BF)
        d_outer[part] = outer
        pre = (mm_t(outer, w_eout[...]) * res["edge_slope"][part].astype(F32)).astype(BF)
        d_pre[part] = pre
        d_edges_out[part] = (cot + mm_t(pre, w_ein[:D])).astype(BF)
    put(t_mm(res["edge_mid"][...], d_outer[...]), "eout", 0)
    put(t_mm(edges[...], d_pre[...]), "ein", 0)
    to_src = mm(one_hot(table.shape[0], src), d_pre[...]).astype(BF)
    to_dst = mm(one_hot(NODE_DEV, dst), d_pre[...]).astype(BF)
    put(t_mm(table[...], to_src), "ein", D)
    put(t_mm(own[...], to_dst), "ein", 2 * D)
    put_gains(jnp.concatenate([gain_edge, gain_node, jnp.zeros((GAINS - 2, D), F32)], axis=0))
    ready("edge")
    d_table = mm_t(to_src, w_ein[D : 2 * D])
    d_own = d_own + d_table[:NODE_DEV] + mm_t(to_dst, w_ein[2 * D :])
    d_own_out[...] = d_own
    d_halo = d_table[NODE_DEV:].astype(BF)
    place(-1, [d_halo[j * HALO : (j + 1) * HALO] for j in range(ROUNDS)], room)


SAVED = (
    ("edge_mid", None),
    ("edge_slope", None),
    ("edge_hat", None),
    ("agg", NODE_DEV),
    ("node_mid", NODE_DEV),
    ("node_slope", NODE_DEV),
    ("node_hat", NODE_DEV),
)


def saved_rows(rows):
    return sum(h or rows for _, h in SAVED)


def views(rows, held, rates):
    out, at = {}, 0
    for name, height in SAVED:
        out[name] = held.at[at : at + (height or rows)]
        at += height or rows
    out["edge_rate"] = rates.at[:rows]
    out["node_rate"] = rates.at[rows : rows + NODE_DEV]
    return out


class Copies:
    def __init__(self, sems):
        self.sems, self.used, self.out = sems, 0, []

    def start(self, source, target):
        copy = pltpu.make_async_copy(source, target, self.sems.at[self.used])
        self.used += 1
        copy.start()
        return copy

    def send(self, source, target):
        self.out.append(self.start(source, target))

    def either(self, choice, yes, no, targets):
        sems = [self.sems.at[self.used + i] for i in range(len(targets))]
        self.used += len(targets)

        def start(refs):
            for ref, to, sem in zip(refs, targets, sems):
                pltpu.make_async_copy(ref, to, sem).start()

        pl.when(choice)(lambda: start(yes))
        pl.when(jnp.logical_not(choice))(lambda: start(no))
        return [
            pltpu.make_async_copy(ref, to, sem).wait for ref, to, sem in zip(yes, targets, sems)
        ]

    def finish(self):
        for copy in self.out:
            copy.wait()


def shard_number(shards):
    if shards == 1:
        return jnp.int32(0)
    return lax.axis_index("dom") * lax.axis_size("rep") + lax.axis_index("rep")


def first_rows(refs):
    return [ref.at[0] for ref in refs]


def one_hots(lists):
    return [one_hot(NODE_DEV, lists[0, j : j + 1]) for j in range(ROUNDS)]


def place(sign, pieces, room):
    part, parts = lax.axis_index("dom"), lax.axis_size("dom")
    room[...] = jnp.zeros_like(room)
    for piece, offset in zip(pieces, OFFSETS):
        to = part + sign * offset

        def put(piece=piece, to=to):
            room[pl.ds(pl.multiple_of(to * HALO, HALO), HALO), :] = piece

        pl.when((to >= 0) & (to < parts))(put)


def placed(sign, room):
    part, parts = lax.axis_index("dom"), lax.axis_size("dom")
    out = []
    for offset in OFFSETS:
        source = part + sign * offset
        there = jnp.clip(source, 0, parts - 1)
        rows = room[pl.ds(pl.multiple_of(there * HALO, HALO), HALO), :]
        out.append(jnp.where((source >= 0) & (source < parts), rows, jnp.zeros_like(rows)))
    return out


def pick(hot, values):
    return [t_mm(one, values).astype(BF) for one in hot]


def fill_halo(table, room):
    for j, rows in enumerate(placed(-1, room)):
        table[NODE_DEV + j * HALO : NODE_DEV + (j + 1) * HALO] = rows


def spread(hot, pieces):
    total = mm(hot[0], pieces[0])
    for j in range(1, ROUNDS):
        total = total + mm(hot[j], pieces[j])
    return total


def pick_kernel(lists, nodes, sent, own, room, sems):
    copies = Copies(sems)
    copy = copies.start(nodes.at[lax.axis_index("segment")], own)
    hot = one_hots(lists)
    copy.wait()
    place(1, pick(hot, own[...]), room)
    copies.send(room, sent)
    copies.finish()


def first_kernel(count, src, dst, lists, g_mine, g_other, nodes, latents, *rest):
    halo, mine, other, rest = rest[0], rest[1:5], rest[5:9], rest[9:]
    (node_out, edge_out, saved_out, rate_out, sent), rest = rest[:5], rest[5:]
    held, rest = rest[:4], rest[4:]
    table, edges, saved, rates, room, node_new, edge_new, sems = rest
    core = lax.axis_index("segment")
    own = table.at[:NODE_DEV]
    copies = Copies(sems)
    coming = [copies.start(nodes.at[core], own), copies.start(latents.at[core], edges)]
    coming += [copies.start(halo, room)]
    waits = copies.either(core == 0, first_rows(mine), first_rows(other), held)
    src, dst = src[...], dst[...]
    gains = jnp.where(core == 0, g_mine[...], g_other[...])
    res = views(edges.shape[0], saved, rates)
    res.update(node_new=node_new, edge_new=edge_new)
    for copy in coming:
        copy.wait()
    fill_halo(table, room)
    tall = 3 * edges.shape[0]

    def edges_done():
        copies.send(edge_new, edge_out)
        copies.send(saved.at[:tall], saved_out.at[:tall])

    forward(
        own, edges, table, src, dst, count[0], held, waits, (gains[:1], gains[1:2]), res,
        edges_done,
    )
    place(1, pick(one_hots(lists), node_new[...]), room)
    for source, target in (
        (room, sent),
        (node_new, node_out),
        (saved.at[tall:], saved_out.at[tall:]),
        (rates, rate_out),
    ):
        copies.send(source, target)
    copies.finish()


def back_outs(copies, layout, store, outs, work):
    d_own, d_edges, sent, *ends = outs
    d_own_s, d_edges_s, room = work

    def ready(group):
        i, rows = list(GROUPS).index(group), layout.parcel(group)
        rows = pl.ds(rows.start, rows.stop - rows.start)
        copies.send(store.at[1, rows], ends[2 + i])
        copies.send(store.at[0, rows], ends[i])

    def finish():
        copies.send(room, sent)
        copies.send(d_own_s, d_own)
        copies.send(d_edges_s, d_edges)
        copies.finish()

    return ready, finish


def second_kernel(shards, count, src, dst, lists, g_mine, g_other, nodes, latents, cots, *rest):
    halo, mine, other, rest = rest[0], rest[1:5], rest[5:9], rest[9:]
    (node_out, edge_out, gain_out), rest = rest[:3], rest[3:]
    outs, rest = rest[:7], rest[7:]
    held, rest = rest[:4], rest[4:]
    table, edges, saved, rates, room, node_new, edge_new, cot, rest = *rest[:8], rest[8:]
    d_outer, d_pre, store, *work, sems = rest
    layout = Layout(shards)
    core, me = lax.axis_index("segment"), shard_number(shards)
    own = table.at[:NODE_DEV]
    copies = Copies(sems)
    coming = [copies.start(nodes, own), copies.start(latents, edges)]
    coming += [copies.start(halo, room)]
    waits = copies.either(core == 1, first_rows(mine), first_rows(other), held)
    cot_copy = copies.start(cots.at[core], cot)
    src, dst = src[...], dst[...]
    gains = jnp.where(core == 1, g_mine[...], g_other[...])
    gains = (gains[:1], gains[1:2])
    res = views(edges.shape[0], saved, rates)
    res.update(node_new=node_new, edge_new=edge_new)
    for copy in coming:
        copy.wait()
    fill_halo(table, room)
    forward(
        own, edges, table, src, dst, count[0], held, waits, gains, res,
        lambda: copies.send(edge_new, edge_out),
    )
    copies.send(node_new, node_out)
    cot_copy.wait()
    ready, finish = back_outs(copies, layout, store, outs, (*work, room))

    def put_gains(value):
        gain_out[...] = value
        for side in range(2):
            store[side, layout.gains : layout.gains + GAINS] = jnp.zeros((GAINS, D), BF)

    backward(
        cot[...].astype(F32), None, own, edges, table, src, dst, count[0], held, gains, res,
        core, me, layout, SEQUENCE[1], store, (*work[:2], room, put_gains), (d_outer, d_pre), ready, lambda: None,
    )
    finish()


def third_kernel(
    shards, count, src, dst, lists, g_mine, g_other, gain_one, nodes, latents, d_own_in,
    d_edges_in, saved_in, rate_in, *rest
):
    halo, back, mine, other, rest = rest[0], rest[1], rest[2:6], rest[6:10], rest[10:]
    outs, rest = rest[:7], rest[7:]
    held, rest = rest[:4], rest[4:]
    table, edges, saved, rates, room, cot_own, cot_edge, got, rest = *rest[:8], rest[8:]
    d_outer, d_pre, store, *work, sems = rest
    layout = Layout(shards)
    core, me = lax.axis_index("segment"), shard_number(shards)
    own = table.at[:NODE_DEV]
    copies = Copies(sems)
    tall = 3 * edges.shape[0]
    coming = [copies.start(back, got), copies.start(d_own_in, cot_own)]
    coming += [copies.start(rate_in, rates), copies.start(nodes.at[core], own)]
    coming += [copies.start(saved_in.at[tall:], saved.at[tall:]), copies.start(halo, room)]
    order = (3, 2, 1, 0)
    waits = copies.either(
        core == 0, *[[v[i] for i in order] for v in (first_rows(mine), first_rows(other), held)]
    )
    waits = [waits[i] for i in order]
    late = [copies.start(d_edges_in, cot_edge), copies.start(saved_in.at[:tall], saved.at[:tall])]
    late += [copies.start(latents.at[core], edges)]
    src, dst = src[...], dst[...]
    gains = jnp.where(core == 0, g_mine[...], g_other[...])
    gains = (gains[:1], gains[1:2])
    res = views(edges.shape[0], saved, rates)
    hot = one_hots(lists)
    for copy in coming:
        copy.wait()
    fill_halo(table, room)
    cot = (cot_own[...] + spread(hot, placed(1, got))).astype(BF).astype(F32)
    waits[3]()
    waits[2]()

    def arrive():
        for copy in late:
            copy.wait()
        waits[1]()
        waits[0]()

    ready, finish = back_outs(copies, layout, store, outs, (*work, room))

    def put_gains(value):
        both = (value.astype(BF), gain_one[...].astype(BF))
        rows = slice(layout.gains, layout.gains + GAINS)
        store[0, rows] = jnp.where(core == 0, both[0], both[1])
        store[1, rows] = jnp.where(core == 0, both[1], both[0])

    backward(
        cot, cot_edge, own, edges, table, src, dst, count[0], held, gains, res,
        core, me, layout, SEQUENCE[0], store, (*work[:2], room, put_gains), (d_outer, d_pre), ready, arrive,
    )
    finish()


def last_kernel(lists, d_own, back, out):
    out[...] = (d_own[...] + spread(one_hots(lists), placed(1, back))).astype(BF)


def weight_scratch():
    return [pltpu.VMEM((r, D), BF) for r in ROWS.values()]


SMEM = pl.BlockSpec(memory_space=pltpu.SMEM)
VMEM = pl.BlockSpec(memory_space=pltpu.VMEM)
ANY = pl.BlockSpec(memory_space=pl.ANY)


def shape(dims, dtype):
    return jax.ShapeDtypeStruct(tuple(dims), dtype)


def call(kernel, in_specs, outs, out_specs, scratch, flops, traffic, limit=SMALL_LIMIT):
    return pl.pallas_call(
        kernel,
        in_specs=in_specs,
        out_shape=outs,
        out_specs=out_specs,
        scratch_shapes=scratch,
        compiler_params=pltpu.CompilerParams(vmem_limit_bytes=limit),
        cost_estimate=pl.CostEstimate(flops=flops, bytes_accessed=traffic, transcendentals=0),
    )


def exchange(rows):
    return lax.all_to_all(rows, "dom", 0, 0, tiled=True)


def other_core(value):
    return lax.ppermute(value, "segment", [(0, 1), (1, 0)])


def across(value, apart):
    if apart == 1:
        return lax.ppermute(value, "rep", [(0, 1), (1, 0)])
    step = apart // 2
    return lax.ppermute(value, "dom", [(p, p ^ step) for p in range(lax.axis_size("dom"))])


def added(pieces):
    total = pieces[0].astype(F32)
    for piece in pieces[1:]:
        total = total + piece.astype(F32)
    return total


def tied(values, others):
    return lax.optimization_barrier((list(values), list(others)))[0]


class Rows:
    def __init__(self, first, rows, arrays):
        self.rows, self.terms = rows, [(a, first) for a in arrays]

    def upper(self):
        self.rows //= 2
        return self.rows, [(a, first + self.rows) for a, first in self.terms]

    def whole(self):
        return self.rows, list(self.terms)

    def quarter(self, i):
        rows = self.rows // 4
        return rows, [(a, first + i * rows) for a, first in self.terms]

    def add(self, array, first):
        self.terms.append((array, first))


def combine(outputs):
    arrays = []
    for _, segments in outputs:
        for _, terms in segments:
            arrays += [a for a, _ in terms if all(a is not b for b in arrays)]
    total = sum(rows * len(terms) for _, segments in outputs for rows, terms in segments)
    copies = sum(len(terms) for _, segments in outputs for _, terms in segments)
    heights = [sum(rows for rows, _ in segments) for _, segments in outputs]

    def kernel(*refs):
        sources, refs = refs[: len(arrays)], refs[len(arrays) :]
        outs, refs = refs[: len(outputs)], refs[len(outputs) :]
        held, sums, sems, out_sems = refs[0], refs[1:-2], refs[-2], refs[-1]
        plan, at, used = [], 0, 0
        for _, segments in outputs:
            for rows, terms in segments:
                places = []
                for array, first in terms:
                    which = [array is a for a in arrays].index(True)
                    copy = pltpu.make_async_copy(
                        sources[which].at[first : first + rows],
                        held.at[at : at + rows],
                        sems.at[used],
                    )
                    copy.start()
                    places.append((at, copy))
                    at, used = at + rows, used + 1
                plan.append(places)
        plan, gone = iter(plan), []
        for i, (dtype, segments) in enumerate(outputs):
            to = 0
            for rows, _ in segments:
                places = next(plan)
                for _, copy in places:
                    copy.wait()
                for low in range(0, rows, 64):
                    high = min(low + 64, rows)
                    value = added([held[p + low : p + high] for p, _ in places])
                    sums[i][to + low : to + high] = value.astype(dtype)
                to += rows
            gone.append(pltpu.make_async_copy(sums[i], outs[i], out_sems.at[i]))
            gone[-1].start()
        for copy in gone:
            copy.wait()

    shapes = [((height, D), dtype) for height, (dtype, _) in zip(heights, outputs)]
    return call(
        kernel,
        [ANY] * len(arrays),
        [shape(*s) for s in shapes],
        [ANY] * len(outputs),
        [
            pltpu.VMEM((total, D), BF),
            *[pltpu.VMEM(*s) for s in shapes],
            pltpu.SemaphoreType.DMA((copies,)),
            pltpu.SemaphoreType.DMA((len(outputs),)),
        ],
        10**6,
        8 * 10**6,
    )(*arrays)


def summed(rows, terms):
    return added([a[first : first + rows] for a, first in terms]).astype(BF)


def sent_parts(parts):
    return (BF, [p.upper() for p in parts])


def receive(parts, got):
    at = 0
    for part in parts:
        part.add(got, at)
        at += part.rows
    return got


def body(
    node_latent,
    edge_latent,
    node_cot,
    edge_src,
    edge_dst,
    edge_count,
    send_index,
    w_edge_in,
    w_edge_out,
    w_node_in,
    w_node_out,
    gain_edge,
    gain_node,
):
    micro, _, _ = node_latent.shape
    rows = edge_latent.shape[1]
    assert micro == lax.axis_size("segment") == 2
    doms, reps = lax.axis_size("dom"), lax.axis_size("rep")
    core, part, rep = (lax.axis_index(a) for a in ("segment", "dom", "rep"))
    shards = doms * reps if doms * reps == 16 else 1
    first = core == 0

    src, dst = edge_src[None], edge_dst[None]

    dma = pltpu.SemaphoreType.DMA
    halo_shape = shape((doms * HALO, D), BF)
    node_s, edge_s = pltpu.VMEM((NODE_DEV, D), BF), pltpu.VMEM((rows, D), BF)
    room_s = pltpu.VMEM((doms * HALO, D), BF)
    sent = call(
        pick_kernel,
        [VMEM, ANY],
        halo_shape,
        ANY,
        [node_s, room_s, dma((2,))],
        10**7,
        7 * 10**6,
    )(send_index, node_latent)
    halo_zero = exchange(sent)
    mine = (w_edge_in, w_edge_out, w_node_in, w_node_out)
    other = tuple(other_core(w) for w in mine)
    g_mine = jnp.concatenate([gain_edge, gain_node], axis=0)
    small = (edge_count, src, dst, send_index, g_mine, other_core(g_mine))
    small_specs = [SMEM] + [VMEM] * 5

    table_s = pltpu.VMEM((NODE_DEV + ROUNDS * HALO, D), BF)
    saved_dims, rate_dims = (saved_rows(rows), D), (rows + NODE_DEV, 128)
    layer_s = [
        *weight_scratch(),
        table_s,
        edge_s,
        pltpu.VMEM(saved_dims, BF),
        pltpu.VMEM(rate_dims, F32),
        room_s,
    ]
    node_one, edge_one, saved, rates, sent = call(
        first_kernel,
        small_specs + [ANY] * (2 + 1 + 8),
        [
            shape((NODE_DEV, D), BF),
            shape((rows, D), BF),
            shape(saved_dims, BF),
            shape(rate_dims, F32),
            halo_shape,
        ],
        [ANY] * 5,
        [*layer_s, node_s, edge_s, dma((20,))],
        11 * 10**8,
        26 * 10**6,
        VMEM_LIMIT,
    )(*small, node_latent, edge_latent, halo_zero, *mine, *other)
    halo_one = exchange(sent)

    layout = Layout(shards)

    def group_rows(values):
        return [Rows(*layout.extent(g), v) for g, v in zip(GROUPS, values)]

    parcels = [layout.parcel(g) for g in GROUPS]
    share = [shape((p.stop - p.start, D), BF) for p in parcels]
    back_shapes = [
        shape((NODE_DEV, D), F32),
        shape((rows, D), BF),
        halo_shape,
        *share,
        *share,
    ]
    back_s = [
        edge_s,
        edge_s,
        pltpu.VMEM((2, layout.rows, D), BF),
        pltpu.VMEM((NODE_DEV, D), F32),
        edge_s,
        dma((40,)),
    ]
    node_two, edge_two, gain_one, *done = call(
        functools.partial(second_kernel, shards),
        small_specs + [ANY] * (3 + 1 + 8),
        [shape((NODE_DEV, D), BF), shape((rows, D), BF), shape((GAINS, D), F32)] + back_shapes,
        [ANY, ANY, VMEM] + [ANY] * len(back_shapes),
        [*layer_s, node_s, edge_s, node_s, *back_s],
        28 * 10**8,
        44 * 10**6,
        VMEM_LIMIT,
    )(*small, node_one, edge_one, node_cot, halo_one, *mine, *other)
    d_own, d_edges, sent, *ends = done
    back = exchange(sent)
    one = [(k, other_core(v)) for k, v in zip(ends[:2], ends[2:])]
    if shards > 1:
        one = group_rows(one)
        gone = [summed(*p.upper()) for p in one]
        (back,) = tied([back], gone)
        got = [receive([p], across(v, a)) for p, v, a in zip(one, gone, (1, 2))]

    d_own, d_edges, sent, *ends = call(
        functools.partial(third_kernel, shards),
        small_specs + [VMEM] + [ANY] * (6 + 2 + 8),
        back_shapes,
        [ANY] * len(back_shapes),
        [*layer_s, pltpu.VMEM((NODE_DEV, D), F32), edge_s, room_s, *back_s],
        18 * 10**8,
        37 * 10**6,
        VMEM_LIMIT,
    )(
        *small, gain_one, node_latent, edge_latent, d_own, d_edges, saved, rates, halo_zero,
        back, *mine, *other,
    )

    def paired(gradient, latent):
        got = other_core(jnp.where(first, latent, gradient))
        low = jnp.where(first, gradient, got)
        high = jnp.where(first, got, latent)
        return jnp.stack([low, high])[None]

    def own_gradient(back):
        return call(
            last_kernel,
            [VMEM] * 3,
            shape((NODE_DEV, D), BF),
            VMEM,
            [],
            10**7,
            7 * 10**6,
        )(send_index, d_own, back)

    if shards > 1:
        send_e, send_n = tied([ends[3], ends[2]], got)
        one_gone = jnp.concatenate([summed(*p.upper()) for p in one], axis=0)
        receive(one, across(one_gone, 4))
        got_e, got_n = other_core(send_e), other_core(send_n)
        (got_e,) = tied([got_e], [one_gone])
        sums = Rows(0, GAINS, (ends[1], got_e))
        nodes, edges = group_rows([(ends[0], got_n), (ends[1], got_e)])
        gone = summed(*edges.upper())
        receive([edges], across(gone, 2))
        nodes.terms[-1] = (tied([got_n], [gone])[0], 0)
        gone = jnp.concatenate([summed(*nodes.upper()), summed(*sums.whole())], axis=0)
        got = receive([nodes, sums], across(gone, 1))
        d_edges, edge_two = tied([d_edges, edge_two], [gone])
        one_gone = jnp.concatenate([summed(*p.upper()) for p in one], axis=0)
        receive(one, across(one_gone, 8))
        (got,) = tied([got], [one_gone])
        nodes.terms[-1], sums.terms[-1] = (got, 0), (got, nodes.rows)
        gone = combine([(BF, [edges.upper()]), (BF, [nodes.upper(), sums.whole()])])
        (sent,) = tied([sent], gone)
        back = exchange(sent)
        receive([edges], across(gone[0], 1))
        receive([nodes, sums], across(gone[1], 2))
        zero = [sums, nodes, edges]
        far = [
            [p.quarter(i) if p.rows > GAINS else p.whole() for p in zero] for i in range(4)
        ]
        near = [p.upper() for p in one]
        *far, stay, near_n, near_e, stay_one = combine(
            [
                *[(BF, v) for v in far[1:]],
                (F32, far[0]),
                *[(BF, [v]) for v in near],
                (F32, [p.whole() for p in one]),
            ]
        )
        got = [across(v, 4 * i) for i, v in enumerate(far, 1)]
        near = [across(near_n, 2), across(near_e, 1)]
        zero = added([stay, *got])
        (back,) = tied([back], far)
        node_pair = paired(own_gradient(back), node_two)
        one = added([stay_one, jnp.concatenate(near, axis=0)])
        sums, zero = zero[:GAINS], zero[GAINS:]
    else:
        node_pair = paired(own_gradient(exchange(sent)), node_two)
        zero = [(k, other_core(v)) for k, v in zip(ends[:2], ends[2:])]
        sums = lax.psum(added([v[:GAINS] for v in zero[1]]), ("dom", "rep"))
        one, zero = (
            jnp.concatenate([added([v[-layout.extent(g)[1] :] for v in y]) for g, y in zip(GROUPS, x)])
            for x in (one, zero)
        )


    edge_pair = paired(d_edges, edge_two)
    factor = float(micro * reps * NODE_DEV * doms) ** (-0.5)
    got = other_core(jnp.where(first, one, zero))
    at, places = 0, {}
    for names in GROUPS.values():
        for name in names:
            places[name] = (at, ROWS[name] // shards // 2)
            at += places[name][1]
    scale = factor if shards > 1 else 1.0

    def grads_kernel(got, one, zero, *outs):
        mine = lax.axis_index("segment") == 0
        for out, name in zip(outs, ROWS):
            at, size = places[name]
            rows = slice(at, at + size)
            kept = jnp.where(mine, zero[rows], one[rows])
            out[:size] = jnp.where(mine, kept, got[rows]) * scale
            out[size:] = jnp.where(mine, got[rows], kept) * scale

    grads = call(
        grads_kernel,
        [VMEM] * 3,
        [shape((rows // shards, D), F32) for rows in ROWS.values()],
        [VMEM] * 4,
        [],
        10**6,
        7 * 10**6,
        16 * 1024 * 1024,
    )(got, one, zero)
    grads = dict(zip(ROWS, grads))
    if shards == 1:
        grads = {
            k: lax.psum_scatter(v, ("dom", "rep"), scatter_dimension=0, tiled=True) * factor
            for k, v in grads.items()
        }
    width = D // (doms * reps)
    sums = lax.dynamic_slice_in_dim(sums[:2], (part * reps + rep) * width, width, axis=1) * factor
    return (
        node_pair,
        edge_pair,
        grads["ein"][None],
        grads["eout"][None],
        grads["nin"][None],
        grads["nout"][None],
        sums[:1],
        sums[1:2],
    )


def solution(mesh):
    placed = (
        P("rep", "dom", None),
        P("rep", "dom", None),
        P("rep", "dom", None),
        P("dom"),
        P("dom"),
        P("dom"),
        P("dom", None, None),
        P("segment", None, None),
        P("segment", None, None),
        P("segment", None, None),
        P("segment", None, None),
        P("segment", None),
        P("segment", None),
    )
    return jax.shard_map(
        body,
        mesh=mesh,
        in_specs=placed,
        out_specs=(
            P("segment", "rep", "dom", None),
            P("segment", "rep", "dom", None),
            P("segment", ("dom", "rep"), None),
            P("segment", ("dom", "rep"), None),
            P("segment", ("dom", "rep"), None),
            P("segment", ("dom", "rep"), None),
            P("segment", ("dom", "rep")),
            P("segment", ("dom", "rep")),
        ),
        check_vma=False,
    )
```

```python
import functools

import jax
import jax.numpy as jnp
from jax import lax
from jax.experimental import pallas as pl
from jax.experimental.pallas import tpu as pltpu
from jax.sharding import PartitionSpec as P

NODE_DEV = 128
HALO = 16
OFFSETS = (1, -1, 2, -2)
ROUNDS = len(OFFSETS)
D = 512
EPS = 1e-05
CHUNK = 384
BF = jnp.bfloat16
F32 = jnp.float32
GAINS = 16
VMEM_LIMIT = 63 * 1024 * 1024
SMALL_LIMIT = 52 * 1024 * 1024

ROWS = {"ein": 3 * D, "eout": D, "nin": 2 * D, "nout": D}
GROUPS = {"node": ("nin", "nout"), "edge": ("ein", "eout")}
SEQUENCE = (
    {"node": (0, 1, 3, 2), "edge": (1, 0, 3, 2)},
    {"node": (0, 2, 3, 1), "edge": (1, 2, 3, 0)},
)


def mm(a, b):
    return lax.dot_general(a, b, (((1,), (0,)), ((), ())), preferred_element_type=F32)


def mm_t(a, b):
    return lax.dot_general(a, b, (((1,), (1,)), ((), ())), preferred_element_type=F32)


def t_mm(a, b):
    return lax.dot_general(a, b, (((0,), (0,)), ((), ())), preferred_element_type=F32)


def one_hot(rows, index):
    where = lax.broadcasted_iota(jnp.int32, (rows, index.shape[1]), 0) == index
    return jnp.where(where, 1.0, 0.0).astype(BF)


def incidence(dst, count):
    edges = dst.shape[1]
    hit = lax.broadcasted_iota(jnp.int32, (NODE_DEV, edges), 0) == dst
    live = lax.broadcasted_iota(jnp.int32, (NODE_DEV, edges), 1) < count
    return jnp.where(hit & live, 1.0, 0.0).astype(BF)


def normed(values):
    center = values - jnp.mean(values, axis=-1, keepdims=True)
    spread = jnp.mean(center * center, axis=-1, keepdims=True)
    return center, lax.rsqrt(spread + EPS)


def silu_pair(pre):
    gate = lax.logistic(pre)
    return pre * gate, gate * (1.0 + pre * (1.0 - gate))


def norm_back(cot, hat, rate, gain):
    scaled = cot * gain
    first = jnp.mean(scaled, axis=-1, keepdims=True)
    second = jnp.mean(scaled * hat, axis=-1, keepdims=True)
    return rate * (scaled - first - hat * second)


def forward(own, edges, table, src, dst, count, weights, waits, gains, res, edges_done):
    w_ein, w_eout, w_nin, w_nout = weights
    g_edge, g_node = gains
    rows = edges.shape[0]
    hot_src = one_hot(table.shape[0], src)
    hot_dst = one_hot(NODE_DEV, dst)
    waits[0]()
    waits[1]()
    for at in range(0, rows, CHUNK):
        part = slice(at, at + CHUNK)
        edge = edges[part]
        sender = t_mm(hot_src[:, part], table[...]).astype(BF)
        receiver = t_mm(hot_dst[:, part], own[...]).astype(BF)
        pre = mm(edge, w_ein[:D]) + mm(sender, w_ein[D : 2 * D]) + mm(receiver, w_ein[2 * D :])
        middle, slope = silu_pair(pre)
        middle = middle.astype(BF)
        center, rate = normed(mm(middle, w_eout[...]))
        live = lax.broadcasted_iota(jnp.int32, (CHUNK, 1), 0) + at < count
        rate = jnp.where(live, rate, 0.0)
        hat = center * rate
        res["edge_new"][part] = (edge.astype(F32) + hat * g_edge).astype(BF)
        res["edge_mid"][part] = middle
        res["edge_slope"][part] = slope.astype(BF)
        res["edge_hat"][part] = hat.astype(BF)
        res["edge_rate"][part] = jnp.broadcast_to(rate, (CHUNK, 128))
    agg = mm(incidence(dst, count), res["edge_new"][...]).astype(BF)
    edges_done()
    waits[2]()
    waits[3]()
    pre = mm(own[...], w_nin[:D]) + mm(agg, w_nin[D:])
    middle, slope = silu_pair(pre)
    middle = middle.astype(BF)
    center, rate = normed(mm(middle, w_nout[...]))
    hat = center * rate
    res["node_new"][...] = (own[...].astype(F32) + hat * g_node).astype(BF)
    res["agg"][...] = agg
    res["node_mid"][...] = middle
    res["node_slope"][...] = slope.astype(BF)
    res["node_hat"][...] = hat.astype(BF)
    res["node_rate"][...] = jnp.broadcast_to(rate, (NODE_DEV, 128))


def slot_of(shard, me, shards, sequence):
    if shards == 1:
        return 0
    apart = jnp.bitwise_xor(jnp.int32(shard), me)
    slot = jnp.int32(0)
    for bit in sequence:
        slot = slot * 2 + jnp.bitwise_and(lax.shift_right_logical(apart, jnp.int32(bit)), 1)
    return slot


class Layout:
    def __init__(self, shards):
        self.shards = shards
        self.half = {name: rows // shards // 2 for name, rows in ROWS.items()}
        self.size = {g: sum(self.half[n] for n in names) for g, names in GROUPS.items()}
        self.gains = shards * self.size["node"]
        self.base = {"node": 0, "edge": self.gains + GAINS}
        self.rows = self.base["edge"] + shards * self.size["edge"]
        self.inner = {}
        for names in GROUPS.values():
            at = 0
            for name in names:
                self.inner[name] = at
                at += self.half[name]

    def parcel(self, group):
        return slice(0, self.gains) if group == "node" else slice(self.gains, self.rows)

    def extent(self, group):
        return (0 if group == "node" else GAINS), self.shards * self.size[group]


def emit(value, name, first_row, layout, group, store, core, slots):
    half = layout.half[name]
    value = value.astype(BF)
    last_row = first_row + value.shape[0]
    for piece in range(2 * layout.shards):
        low, high = max(piece * half, first_row), min((piece + 1) * half, last_row)
        if low < high:
            keep = jnp.bitwise_xor(core, piece % 2)
            to = layout.base[group] + layout.inner[name] + low - piece * half
            if layout.shards > 1:
                to = pl.multiple_of(slots[piece // 2] * layout.size[group] + to, 16)
            store[keep, pl.ds(to, high - low), :] = value[low - first_row : high - first_row]


def backward(
    cot_node, cot_edge, own, edges, table, src, dst, count, weights, gains, res, core, me, layout, sequence,
    store, outs, work, ready, arrive,
):
    w_ein, w_eout, w_nin, w_nout = weights
    g_edge, g_node = gains
    d_own_out, d_edges_out, room, put_gains = outs
    d_outer, d_pre = work
    rows = edges.shape[0]
    shards = layout.shards
    slots = {
        g: [slot_of(i, me, shards, sequence[g]) for i in range(shards)] for g in GROUPS
    }

    def put(value, name, first_row):
        group = "node" if name in GROUPS["node"] else "edge"
        emit(value, name, first_row, layout, group, store, core, slots[group])

    hat = res["node_hat"][...].astype(F32)
    gain_node = jnp.sum(cot_node * hat, axis=0, keepdims=True)
    d_out = norm_back(cot_node, hat, res["node_rate"][:, :1], g_node).astype(BF)
    put(t_mm(res["node_mid"][...], d_out), "nout", 0)
    d_pre_node = (mm_t(d_out, w_nout[...]) * res["node_slope"][...].astype(F32)).astype(BF)
    put(t_mm(own[...], d_pre_node), "nin", 0)
    put(t_mm(res["agg"][...], d_pre_node), "nin", D)
    ready("node")
    d_own = cot_node + mm_t(d_pre_node, w_nin[:D])
    d_agg = mm_t(d_pre_node, w_nin[D:]).astype(BF)

    arrive()
    joins = incidence(dst, count)
    gain_edge = jnp.zeros((1, D), F32)
    for at in range(0, rows, CHUNK):
        part = slice(at, at + CHUNK)
        cot = t_mm(joins[:, part], d_agg)
        if cot_edge is not None:
            cot = cot + cot_edge[part].astype(F32)
        hat = res["edge_hat"][part].astype(F32)
        gain_edge = gain_edge + jnp.sum(cot * hat, axis=0, keepdims=True)
        outer = norm_back(cot, hat, res["edge_rate"][part, :1], g_edge).astype(BF)
        d_outer[part] = outer
        pre = (mm_t(outer, w_eout[...]) * res["edge_slope"][part].astype(F32)).astype(BF)
        d_pre[part] = pre
        d_edges_out[part] = (cot + mm_t(pre, w_ein[:D])).astype(BF)
    put(t_mm(res["edge_mid"][...], d_outer[...]), "eout", 0)
    put(t_mm(edges[...], d_pre[...]), "ein", 0)
    to_src = mm(one_hot(table.shape[0], src), d_pre[...]).astype(BF)
    to_dst = mm(one_hot(NODE_DEV, dst), d_pre[...]).astype(BF)
    put(t_mm(table[...], to_src), "ein", D)
    put(t_mm(own[...], to_dst), "ein", 2 * D)
    put_gains(jnp.concatenate([gain_edge, gain_node, jnp.zeros((GAINS - 2, D), F32)], axis=0))
    ready("edge")
    d_table = mm_t(to_src, w_ein[D : 2 * D])
    d_own = d_own + d_table[:NODE_DEV] + mm_t(to_dst, w_ein[2 * D :])
    d_own_out[...] = d_own
    d_halo = d_table[NODE_DEV:].astype(BF)
    place(-1, [d_halo[j * HALO : (j + 1) * HALO] for j in range(ROUNDS)], room)


SAVED = (
    ("edge_mid", None),
    ("edge_slope", None),
    ("edge_hat", None),
    ("agg", NODE_DEV),
    ("node_mid", NODE_DEV),
    ("node_slope", NODE_DEV),
    ("node_hat", NODE_DEV),
)


def saved_rows(rows):
    return sum(h or rows for _, h in SAVED)


def views(rows, held, rates):
    out, at = {}, 0
    for name, height in SAVED:
        out[name] = held.at[at : at + (height or rows)]
        at += height or rows
    out["edge_rate"] = rates.at[:rows]
    out["node_rate"] = rates.at[rows : rows + NODE_DEV]
    return out


class Copies:
    def __init__(self, sems):
        self.sems, self.used, self.out = sems, 0, []

    def start(self, source, target):
        copy = pltpu.make_async_copy(source, target, self.sems.at[self.used])
        self.used += 1
        copy.start()
        return copy

    def send(self, source, target):
        self.out.append(self.start(source, target))

    def either(self, choice, yes, no, targets):
        sems = [self.sems.at[self.used + i] for i in range(len(targets))]
        self.used += len(targets)

        def start(refs):
            for ref, to, sem in zip(refs, targets, sems):
                pltpu.make_async_copy(ref, to, sem).start()

        pl.when(choice)(lambda: start(yes))
        pl.when(jnp.logical_not(choice))(lambda: start(no))
        return [
            pltpu.make_async_copy(ref, to, sem).wait for ref, to, sem in zip(yes, targets, sems)
        ]

    def finish(self):
        for copy in self.out:
            copy.wait()


def shard_number(shards):
    if shards == 1:
        return jnp.int32(0)
    return lax.axis_index("dom") * lax.axis_size("rep") + lax.axis_index("rep")


def first_rows(refs):
    return [ref.at[0] for ref in refs]


def one_hots(lists):
    return [one_hot(NODE_DEV, lists[0, j : j + 1]) for j in range(ROUNDS)]


def place(sign, pieces, room):
    part, parts = lax.axis_index("dom"), lax.axis_size("dom")
    room[...] = jnp.zeros_like(room)
    for piece, offset in zip(pieces, OFFSETS):
        to = part + sign * offset

        def put(piece=piece, to=to):
            room[pl.ds(pl.multiple_of(to * HALO, HALO), HALO), :] = piece

        pl.when((to >= 0) & (to < parts))(put)


def placed(sign, room):
    part, parts = lax.axis_index("dom"), lax.axis_size("dom")
    out = []
    for offset in OFFSETS:
        source = part + sign * offset
        there = jnp.clip(source, 0, parts - 1)
        rows = room[pl.ds(pl.multiple_of(there * HALO, HALO), HALO), :]
        out.append(jnp.where((source >= 0) & (source < parts), rows, jnp.zeros_like(rows)))
    return out


def pick(hot, values):
    return [t_mm(one, values).astype(BF) for one in hot]


def fill_halo(table, room):
    for j, rows in enumerate(placed(-1, room)):
        table[NODE_DEV + j * HALO : NODE_DEV + (j + 1) * HALO] = rows


def spread(hot, pieces):
    total = mm(hot[0], pieces[0])
    for j in range(1, ROUNDS):
        total = total + mm(hot[j], pieces[j])
    return total


def pick_kernel(lists, nodes, sent, own, room, sems):
    copies = Copies(sems)
    copy = copies.start(nodes.at[lax.axis_index("segment")], own)
    hot = one_hots(lists)
    copy.wait()
    place(1, pick(hot, own[...]), room)
    copies.send(room, sent)
    copies.finish()


def first_kernel(count, src, dst, lists, g_mine, g_other, nodes, latents, *rest):
    halo, mine, other, rest = rest[0], rest[1:5], rest[5:9], rest[9:]
    (node_out, edge_out, saved_out, rate_out, sent), rest = rest[:5], rest[5:]
    held, rest = rest[:4], rest[4:]
    table, edges, saved, rates, room, node_new, edge_new, sems = rest
    core = lax.axis_index("segment")
    own = table.at[:NODE_DEV]
    copies = Copies(sems)
    coming = [copies.start(nodes.at[core], own), copies.start(latents.at[core], edges)]
    coming += [copies.start(halo, room)]
    waits = copies.either(core == 0, first_rows(mine), first_rows(other), held)
    src, dst = src[...], dst[...]
    gains = jnp.where(core == 0, g_mine[...], g_other[...])
    res = views(edges.shape[0], saved, rates)
    res.update(node_new=node_new, edge_new=edge_new)
    for copy in coming:
        copy.wait()
    fill_halo(table, room)
    tall = 3 * edges.shape[0]

    def edges_done():
        copies.send(edge_new, edge_out)
        copies.send(saved.at[:tall], saved_out.at[:tall])

    forward(
        own, edges, table, src, dst, count[0], held, waits, (gains[:1], gains[1:2]), res,
        edges_done,
    )
    place(1, pick(one_hots(lists), node_new[...]), room)
    for source, target in (
        (room, sent),
        (node_new, node_out),
        (saved.at[tall:], saved_out.at[tall:]),
        (rates, rate_out),
    ):
        copies.send(source, target)
    copies.finish()


def back_outs(copies, layout, store, outs, work):
    d_own, d_edges, sent, *ends = outs
    d_own_s, d_edges_s, room = work

    def ready(group):
        i, rows = list(GROUPS).index(group), layout.parcel(group)
        rows = pl.ds(rows.start, rows.stop - rows.start)
        copies.send(store.at[1, rows], ends[2 + i])
        copies.send(store.at[0, rows], ends[i])

    def finish():
        copies.send(room, sent)
        copies.send(d_own_s, d_own)
        copies.send(d_edges_s, d_edges)
        copies.finish()

    return ready, finish


def second_kernel(shards, count, src, dst, lists, g_mine, g_other, nodes, latents, cots, *rest):
    halo, mine, other, rest = rest[0], rest[1:5], rest[5:9], rest[9:]
    (node_out, edge_out, gain_out), rest = rest[:3], rest[3:]
    outs, rest = rest[:7], rest[7:]
    held, rest = rest[:4], rest[4:]
    table, edges, saved, rates, room, node_new, edge_new, cot, rest = *rest[:8], rest[8:]
    d_outer, d_pre, store, *work, sems = rest
    layout = Layout(shards)
    core, me = lax.axis_index("segment"), shard_number(shards)
    own = table.at[:NODE_DEV]
    copies = Copies(sems)
    coming = [copies.start(nodes, own), copies.start(latents, edges)]
    coming += [copies.start(halo, room)]
    waits = copies.either(core == 1, first_rows(mine), first_rows(other), held)
    cot_copy = copies.start(cots.at[core], cot)
    src, dst = src[...], dst[...]
    gains = jnp.where(core == 1, g_mine[...], g_other[...])
    gains = (gains[:1], gains[1:2])
    res = views(edges.shape[0], saved, rates)
    res.update(node_new=node_new, edge_new=edge_new)
    for copy in coming:
        copy.wait()
    fill_halo(table, room)
    forward(
        own, edges, table, src, dst, count[0], held, waits, gains, res,
        lambda: copies.send(edge_new, edge_out),
    )
    copies.send(node_new, node_out)
    cot_copy.wait()
    ready, finish = back_outs(copies, layout, store, outs, (*work, room))

    def put_gains(value):
        gain_out[...] = value
        for side in range(2):
            store[side, layout.gains : layout.gains + GAINS] = jnp.zeros((GAINS, D), BF)

    backward(
        cot[...].astype(F32), None, own, edges, table, src, dst, count[0], held, gains, res,
        core, me, layout, SEQUENCE[1], store, (*work[:2], room, put_gains), (d_outer, d_pre), ready, lambda: None,
    )
    finish()


def third_kernel(
    shards, count, src, dst, lists, g_mine, g_other, gain_one, nodes, latents, d_own_in,
    d_edges_in, saved_in, rate_in, *rest
):
    halo, back, mine, other, rest = rest[0], rest[1], rest[2:6], rest[6:10], rest[10:]
    outs, rest = rest[:7], rest[7:]
    held, rest = rest[:4], rest[4:]
    table, edges, saved, rates, room, cot_own, cot_edge, got, rest = *rest[:8], rest[8:]
    d_outer, d_pre, store, *work, sems = rest
    layout = Layout(shards)
    core, me = lax.axis_index("segment"), shard_number(shards)
    own = table.at[:NODE_DEV]
    copies = Copies(sems)
    tall = 3 * edges.shape[0]
    coming = [copies.start(back, got), copies.start(d_own_in, cot_own)]
    coming += [copies.start(rate_in, rates), copies.start(nodes.at[core], own)]
    coming += [copies.start(saved_in.at[tall:], saved.at[tall:]), copies.start(halo, room)]
    order = (3, 2, 1, 0)
    waits = copies.either(
        core == 0, *[[v[i] for i in order] for v in (first_rows(mine), first_rows(other), held)]
    )
    waits = [waits[i] for i in order]
    late = [copies.start(d_edges_in, cot_edge), copies.start(saved_in.at[:tall], saved.at[:tall])]
    late += [copies.start(latents.at[core], edges)]
    src, dst = src[...], dst[...]
    gains = jnp.where(core == 0, g_mine[...], g_other[...])
    gains = (gains[:1], gains[1:2])
    res = views(edges.shape[0], saved, rates)
    hot = one_hots(lists)
    for copy in coming:
        copy.wait()
    fill_halo(table, room)
    cot = (cot_own[...] + spread(hot, placed(1, got))).astype(BF).astype(F32)
    waits[3]()
    waits[2]()

    def arrive():
        for copy in late:
            copy.wait()
        waits[1]()
        waits[0]()

    ready, finish = back_outs(copies, layout, store, outs, (*work, room))

    def put_gains(value):
        both = (value.astype(BF), gain_one[...].astype(BF))
        rows = slice(layout.gains, layout.gains + GAINS)
        store[0, rows] = jnp.where(core == 0, both[0], both[1])
        store[1, rows] = jnp.where(core == 0, both[1], both[0])

    backward(
        cot, cot_edge, own, edges, table, src, dst, count[0], held, gains, res,
        core, me, layout, SEQUENCE[0], store, (*work[:2], room, put_gains), (d_outer, d_pre), ready, arrive,
    )
    finish()


def last_kernel(lists, d_own, back, out):
    out[...] = (d_own[...] + spread(one_hots(lists), placed(1, back))).astype(BF)


def weight_scratch():
    return [pltpu.VMEM((r, D), BF) for r in ROWS.values()]


SMEM = pl.BlockSpec(memory_space=pltpu.SMEM)
VMEM = pl.BlockSpec(memory_space=pltpu.VMEM)
ANY = pl.BlockSpec(memory_space=pl.ANY)


def shape(dims, dtype):
    return jax.ShapeDtypeStruct(tuple(dims), dtype)


def call(kernel, in_specs, outs, out_specs, scratch, flops, traffic, limit=SMALL_LIMIT):
    return pl.pallas_call(
        kernel,
        in_specs=in_specs,
        out_shape=outs,
        out_specs=out_specs,
        scratch_shapes=scratch,
        compiler_params=pltpu.CompilerParams(vmem_limit_bytes=limit),
        cost_estimate=pl.CostEstimate(flops=flops, bytes_accessed=traffic, transcendentals=0),
    )


def exchange(rows):
    return lax.all_to_all(rows, "dom", 0, 0, tiled=True)


def other_core(value):
    return lax.ppermute(value, "segment", [(0, 1), (1, 0)])


def across(value, apart):
    if apart == 1:
        return lax.ppermute(value, "rep", [(0, 1), (1, 0)])
    step = apart // 2
    return lax.ppermute(value, "dom", [(p, p ^ step) for p in range(lax.axis_size("dom"))])


def added(pieces):
    total = pieces[0].astype(F32)
    for piece in pieces[1:]:
        total = total + piece.astype(F32)
    return total


def tied(values, others):
    return lax.optimization_barrier((list(values), list(others)))[0]


class Rows:
    def __init__(self, first, rows, arrays):
        self.rows, self.terms = rows, [(a, first) for a in arrays]

    def upper(self):
        self.rows //= 2
        return self.rows, [(a, first + self.rows) for a, first in self.terms]

    def whole(self):
        return self.rows, list(self.terms)

    def quarter(self, i):
        rows = self.rows // 4
        return rows, [(a, first + i * rows) for a, first in self.terms]

    def add(self, array, first):
        self.terms.append((array, first))


def combine(outputs):
    arrays = []
    for _, segments in outputs:
        for _, terms in segments:
            arrays += [a for a, _ in terms if all(a is not b for b in arrays)]
    total = sum(rows * len(terms) for _, segments in outputs for rows, terms in segments)
    copies = sum(len(terms) for _, segments in outputs for _, terms in segments)
    heights = [sum(rows for rows, _ in segments) for _, segments in outputs]

    def kernel(*refs):
        sources, refs = refs[: len(arrays)], refs[len(arrays) :]
        outs, refs = refs[: len(outputs)], refs[len(outputs) :]
        held, sums, sems, out_sems = refs[0], refs[1:-2], refs[-2], refs[-1]
        plan, at, used = [], 0, 0
        for _, segments in outputs:
            for rows, terms in segments:
                places = []
                for array, first in terms:
                    which = [array is a for a in arrays].index(True)
                    copy = pltpu.make_async_copy(
                        sources[which].at[first : first + rows],
                        held.at[at : at + rows],
                        sems.at[used],
                    )
                    copy.start()
                    places.append((at, copy))
                    at, used = at + rows, used + 1
                plan.append(places)
        plan, gone = iter(plan), []
        for i, (dtype, segments) in enumerate(outputs):
            to = 0
            for rows, _ in segments:
                places = next(plan)
                for _, copy in places:
                    copy.wait()
                for low in range(0, rows, 64):
                    high = min(low + 64, rows)
                    value = added([held[p + low : p + high] for p, _ in places])
                    sums[i][to + low : to + high] = value.astype(dtype)
                to += rows
            gone.append(pltpu.make_async_copy(sums[i], outs[i], out_sems.at[i]))
            gone[-1].start()
        for copy in gone:
            copy.wait()

    shapes = [((height, D), dtype) for height, (dtype, _) in zip(heights, outputs)]
    return call(
        kernel,
        [ANY] * len(arrays),
        [shape(*s) for s in shapes],
        [ANY] * len(outputs),
        [
            pltpu.VMEM((total, D), BF),
            *[pltpu.VMEM(*s) for s in shapes],
            pltpu.SemaphoreType.DMA((copies,)),
            pltpu.SemaphoreType.DMA((len(outputs),)),
        ],
        10**6,
        8 * 10**6,
    )(*arrays)


def summed(rows, terms):
    return added([a[first : first + rows] for a, first in terms]).astype(BF)


def sent_parts(parts):
    return (BF, [p.upper() for p in parts])


def receive(parts, got):
    at = 0
    for part in parts:
        part.add(got, at)
        at += part.rows
    return got


def body(
    node_latent,
    edge_latent,
    node_cot,
    edge_src,
    edge_dst,
    edge_count,
    send_index,
    w_edge_in,
    w_edge_out,
    w_node_in,
    w_node_out,
    gain_edge,
    gain_node,
):
    micro, _, _ = node_latent.shape
    rows = edge_latent.shape[1]
    assert micro == lax.axis_size("segment") == 2
    doms, reps = lax.axis_size("dom"), lax.axis_size("rep")
    core, part, rep = (lax.axis_index(a) for a in ("segment", "dom", "rep"))
    shards = doms * reps if doms * reps == 16 else 1
    first = core == 0

    src, dst = edge_src[None], edge_dst[None]

    dma = pltpu.SemaphoreType.DMA
    halo_shape = shape((doms * HALO, D), BF)
    node_s, edge_s = pltpu.VMEM((NODE_DEV, D), BF), pltpu.VMEM((rows, D), BF)
    room_s = pltpu.VMEM((doms * HALO, D), BF)
    sent = call(
        pick_kernel,
        [VMEM, ANY],
        halo_shape,
        ANY,
        [node_s, room_s, dma((2,))],
        10**7,
        7 * 10**6,
    )(send_index, node_latent)
    halo_zero = exchange(sent)
    mine = (w_edge_in, w_edge_out, w_node_in, w_node_out)
    other = tuple(other_core(w) for w in mine)
    g_mine = jnp.concatenate([gain_edge, gain_node], axis=0)
    small = (edge_count, src, dst, send_index, g_mine, other_core(g_mine))
    small_specs = [SMEM] + [VMEM] * 5

    table_s = pltpu.VMEM((NODE_DEV + ROUNDS * HALO, D), BF)
    saved_dims, rate_dims = (saved_rows(rows), D), (rows + NODE_DEV, 128)
    layer_s = [
        *weight_scratch(),
        table_s,
        edge_s,
        pltpu.VMEM(saved_dims, BF),
        pltpu.VMEM(rate_dims, F32),
        room_s,
    ]
    node_one, edge_one, saved, rates, sent = call(
        first_kernel,
        small_specs + [ANY] * (2 + 1 + 8),
        [
            shape((NODE_DEV, D), BF),
            shape((rows, D), BF),
            shape(saved_dims, BF),
            shape(rate_dims, F32),
            halo_shape,
        ],
        [ANY] * 5,
        [*layer_s, node_s, edge_s, dma((20,))],
        11 * 10**8,
        26 * 10**6,
        VMEM_LIMIT,
    )(*small, node_latent, edge_latent, halo_zero, *mine, *other)
    halo_one = exchange(sent)

    layout = Layout(shards)

    def group_rows(values):
        return [Rows(*layout.extent(g), v) for g, v in zip(GROUPS, values)]

    parcels = [layout.parcel(g) for g in GROUPS]
    share = [shape((p.stop - p.start, D), BF) for p in parcels]
    back_shapes = [
        shape((NODE_DEV, D), F32),
        shape((rows, D), BF),
        halo_shape,
        *share,
        *share,
    ]
    back_s = [
        edge_s,
        edge_s,
        pltpu.VMEM((2, layout.rows, D), BF),
        pltpu.VMEM((NODE_DEV, D), F32),
        edge_s,
        dma((40,)),
    ]
    node_two, edge_two, gain_one, *done = call(
        functools.partial(second_kernel, shards),
        small_specs + [ANY] * (3 + 1 + 8),
        [shape((NODE_DEV, D), BF), shape((rows, D), BF), shape((GAINS, D), F32)] + back_shapes,
        [ANY, ANY, VMEM] + [ANY] * len(back_shapes),
        [*layer_s, node_s, edge_s, node_s, *back_s],
        28 * 10**8,
        44 * 10**6,
        VMEM_LIMIT,
    )(*small, node_one, edge_one, node_cot, halo_one, *mine, *other)
    d_own, d_edges, sent, *ends = done
    back = exchange(sent)
    one = [(k, other_core(v)) for k, v in zip(ends[:2], ends[2:])]
    if shards > 1:
        one = group_rows(one)
        gone = [summed(*p.upper()) for p in one]
        (back,) = tied([back], gone)
        got = [receive([p], across(v, a)) for p, v, a in zip(one, gone, (1, 2))]

    d_own, d_edges, sent, *ends = call(
        functools.partial(third_kernel, shards),
        small_specs + [VMEM] + [ANY] * (6 + 2 + 8),
        back_shapes,
        [ANY] * len(back_shapes),
        [*layer_s, pltpu.VMEM((NODE_DEV, D), F32), edge_s, room_s, *back_s],
        18 * 10**8,
        37 * 10**6,
        VMEM_LIMIT,
    )(
        *small, gain_one, node_latent, edge_latent, d_own, d_edges, saved, rates, halo_zero,
        back, *mine, *other,
    )

    def paired(gradient, latent):
        got = other_core(jnp.where(first, latent, gradient))
        low = jnp.where(first, gradient, got)
        high = jnp.where(first, got, latent)
        return jnp.stack([low, high])[None]

    def own_gradient(back):
        return call(
            last_kernel,
            [VMEM] * 3,
            shape((NODE_DEV, D), BF),
            VMEM,
            [],
            10**7,
            7 * 10**6,
        )(send_index, d_own, back)

    if shards > 1:
        send_e, send_n = tied([ends[3], ends[2]], got)
        one_gone = jnp.concatenate([summed(*p.upper()) for p in one], axis=0)
        receive(one, across(one_gone, 4))
        got_e, got_n = other_core(send_e), other_core(send_n)
        (got_e,) = tied([got_e], [one_gone])
        sums = Rows(0, GAINS, (ends[1], got_e))
        nodes, edges = group_rows([(ends[0], got_n), (ends[1], got_e)])
        gone = summed(*edges.upper())
        receive([edges], across(gone, 2))
        nodes.terms[-1] = (tied([got_n], [gone])[0], 0)
        gone = jnp.concatenate([summed(*nodes.upper()), summed(*sums.whole())], axis=0)
        got = receive([nodes, sums], across(gone, 1))
        d_edges, edge_two = tied([d_edges, edge_two], [gone])
        one_gone = jnp.concatenate([summed(*p.upper()) for p in one], axis=0)
        receive(one, across(one_gone, 8))
        (got,) = tied([got], [one_gone])
        nodes.terms[-1], sums.terms[-1] = (got, 0), (got, nodes.rows)
        gone = combine([(BF, [edges.upper()]), (BF, [nodes.upper(), sums.whole()])])
        (sent,) = tied([sent], gone)
        back = exchange(sent)
        receive([edges], across(gone[0], 1))
        receive([nodes, sums], across(gone[1], 2))
        zero = [sums, nodes, edges]
        far = [
            [p.quarter(i) if p.rows > GAINS else p.whole() for p in zero] for i in range(4)
        ]
        near = [p.upper() for p in one]
        *far, stay, near_n, near_e, stay_one = combine(
            [
                *[(BF, v) for v in far[1:]],
                (F32, far[0]),
                *[(BF, [v]) for v in near],
                (F32, [p.whole() for p in one]),
            ]
        )
        got = [across(v, 4 * i) for i, v in enumerate(far, 1)]
        near = [across(near_n, 2), across(near_e, 1)]
        zero = added([stay, *got])
        (back,) = tied([back], far)
        node_pair = paired(own_gradient(back), node_two)
        one = added([stay_one, jnp.concatenate(near, axis=0)])
        sums, zero = zero[:GAINS], zero[GAINS:]
    else:
        node_pair = paired(own_gradient(exchange(sent)), node_two)
        zero = [(k, other_core(v)) for k, v in zip(ends[:2], ends[2:])]
        sums = lax.psum(added([v[:GAINS] for v in zero[1]]), ("dom", "rep"))
        one, zero = (
            jnp.concatenate([added([v[-layout.extent(g)[1] :] for v in y]) for g, y in zip(GROUPS, x)])
            for x in (one, zero)
        )


    edge_pair = paired(d_edges, edge_two)
    factor = float(micro * reps * NODE_DEV * doms) ** (-0.5)
    got = other_core(jnp.where(first, one, zero))
    at, places = 0, {}
    for names in GROUPS.values():
        for name in names:
            places[name] = (at, ROWS[name] // shards // 2)
            at += places[name][1]
    scale = factor if shards > 1 else 1.0

    def grads_kernel(got, one, zero, *outs):
        mine = lax.axis_index("segment") == 0
        for out, name in zip(outs, ROWS):
            at, size = places[name]
            rows = slice(at, at + size)
            kept = jnp.where(mine, zero[rows], one[rows])
            out[:size] = jnp.where(mine, kept, got[rows]) * scale
            out[size:] = jnp.where(mine, got[rows], kept) * scale

    grads = call(
        grads_kernel,
        [VMEM] * 3,
        [shape((rows // shards, D), F32) for rows in ROWS.values()],
        [VMEM] * 4,
        [],
        10**6,
        7 * 10**6,
        16 * 1024 * 1024,
    )(got, one, zero)
    grads = dict(zip(ROWS, grads))
    if shards == 1:
        grads = {
            k: lax.psum_scatter(v, ("dom", "rep"), scatter_dimension=0, tiled=True) * factor
            for k, v in grads.items()
        }
    width = D // (doms * reps)
    sums = lax.dynamic_slice_in_dim(sums[:2], (part * reps + rep) * width, width, axis=1) * factor
    return (
        node_pair,
        edge_pair,
        grads["ein"][None],
        grads["eout"][None],
        grads["nin"][None],
        grads["nout"][None],
        sums[:1],
        sums[1:2],
    )


def solution(mesh):
    placed = (
        P("rep", "dom", None),
        P("rep", "dom", None),
        P("rep", "dom", None),
        P("dom"),
        P("dom"),
        P("dom"),
        P("dom", None, None),
        P("segment", None, None),
        P("segment", None, None),
        P("segment", None, None),
        P("segment", None, None),
        P("segment", None),
        P("segment", None),
    )
    return jax.shard_map(
        body,
        mesh=mesh,
        in_specs=placed,
        out_specs=(
            P("segment", "rep", "dom", None),
            P("segment", "rep", "dom", None),
            P("segment", ("dom", "rep"), None),
            P("segment", ("dom", "rep"), None),
            P("segment", ("dom", "rep"), None),
            P("segment", ("dom", "rep"), None),
            P("segment", ("dom", "rep")),
            P("segment", ("dom", "rep")),
        ),
        check_vma=False,
    )
```

```python
import functools

import jax
import jax.numpy as jnp
from jax import lax
from jax.experimental import pallas as pl
from jax.experimental.pallas import tpu as pltpu
from jax.sharding import PartitionSpec as P

NODE_DEV = 128
HALO = 16
OFFSETS = (1, -1, 2, -2)
ROUNDS = len(OFFSETS)
D = 512
EPS = 1e-05
CHUNK = 384
BF = jnp.bfloat16
F32 = jnp.float32
GAINS = 16
VMEM_LIMIT = 63 * 1024 * 1024
SMALL_LIMIT = 52 * 1024 * 1024

ROWS = {"ein": 3 * D, "eout": D, "nin": 2 * D, "nout": D}
GROUPS = {"node": ("nin", "nout"), "edge": ("ein", "eout")}
SEQUENCE = (
    {"node": (0, 1, 3, 2), "edge": (1, 0, 3, 2)},
    {"node": (0, 2, 3, 1), "edge": (1, 2, 3, 0)},
)


def mm(a, b):
    return lax.dot_general(a, b, (((1,), (0,)), ((), ())), preferred_element_type=F32)


def mm_t(a, b):
    return lax.dot_general(a, b, (((1,), (1,)), ((), ())), preferred_element_type=F32)


def t_mm(a, b):
    return lax.dot_general(a, b, (((0,), (0,)), ((), ())), preferred_element_type=F32)


def one_hot(rows, index):
    where = lax.broadcasted_iota(jnp.int32, (rows, index.shape[1]), 0) == index
    return jnp.where(where, 1.0, 0.0).astype(BF)


def incidence(dst, count):
    edges = dst.shape[1]
    hit = lax.broadcasted_iota(jnp.int32, (NODE_DEV, edges), 0) == dst
    live = lax.broadcasted_iota(jnp.int32, (NODE_DEV, edges), 1) < count
    return jnp.where(hit & live, 1.0, 0.0).astype(BF)


def normed(values):
    center = values - jnp.mean(values, axis=-1, keepdims=True)
    spread = jnp.mean(center * center, axis=-1, keepdims=True)
    return center, lax.rsqrt(spread + EPS)


def silu_pair(pre):
    gate = lax.logistic(pre)
    return pre * gate, gate * (1.0 + pre * (1.0 - gate))


def norm_back(cot, hat, rate, gain):
    scaled = cot * gain
    first = jnp.mean(scaled, axis=-1, keepdims=True)
    second = jnp.mean(scaled * hat, axis=-1, keepdims=True)
    return rate * (scaled - first - hat * second)


def forward(own, edges, table, src, dst, count, weights, waits, gains, res, edges_done, here):
    w_ein, w_eout, w_nin, w_nout = weights
    g_edge, g_node = gains
    rows = edges.shape[0]
    edges_here, table_here = here
    hot_src = one_hot(table.shape[0], src)
    hot_dst = one_hot(NODE_DEV, dst)
    table_here()
    edges_here()
    waits[0]()
    for at in range(0, rows, CHUNK):
        part = slice(at, at + CHUNK)
        edge = edges[part]
        pre = mm(edge, w_ein[:D])
        if at == 0:
            waits[1]()
            waits[2]()
        sender = t_mm(hot_src[:, part], table[...]).astype(BF)
        receiver = t_mm(hot_dst[:, part], own[...]).astype(BF)
        pre = pre + mm(sender, w_ein[D : 2 * D]) + mm(receiver, w_ein[2 * D :])
        if at == 0:
            waits[3]()
        middle, slope = silu_pair(pre)
        middle = middle.astype(BF)
        center, rate = normed(mm(middle, w_eout[...]))
        live = lax.broadcasted_iota(jnp.int32, (CHUNK, 1), 0) + at < count
        rate = jnp.where(live, rate, 0.0)
        hat = center * rate
        res["edge_new"][part] = (edge.astype(F32) + hat * g_edge).astype(BF)
        res["edge_mid"][part] = middle
        res["edge_slope"][part] = slope.astype(BF)
        res["edge_hat"][part] = hat.astype(BF)
        res["edge_rate"][part] = jnp.broadcast_to(rate, (CHUNK, 128))
    agg = mm(incidence(dst, count), res["edge_new"][...]).astype(BF)
    edges_done()
    waits[4]()
    waits[5]()
    pre = mm(own[...], w_nin[:D]) + mm(agg, w_nin[D:])
    middle, slope = silu_pair(pre)
    middle = middle.astype(BF)
    center, rate = normed(mm(middle, w_nout[...]))
    hat = center * rate
    res["node_new"][...] = (own[...].astype(F32) + hat * g_node).astype(BF)
    res["agg"][...] = agg
    res["node_mid"][...] = middle
    res["node_slope"][...] = slope.astype(BF)
    res["node_hat"][...] = hat.astype(BF)
    res["node_rate"][...] = jnp.broadcast_to(rate, (NODE_DEV, 128))


def slot_of(shard, me, shards, sequence):
    if shards == 1:
        return 0
    apart = jnp.bitwise_xor(jnp.int32(shard), me)
    slot = jnp.int32(0)
    for bit in sequence:
        slot = slot * 2 + jnp.bitwise_and(lax.shift_right_logical(apart, jnp.int32(bit)), 1)
    return slot


class Layout:
    def __init__(self, shards):
        self.shards = shards
        self.half = {name: rows // shards // 2 for name, rows in ROWS.items()}
        self.size = {g: sum(self.half[n] for n in names) for g, names in GROUPS.items()}
        self.gains = shards * self.size["node"]
        self.base = {"node": 0, "edge": self.gains + GAINS}
        self.rows = self.base["edge"] + shards * self.size["edge"]
        self.inner = {}
        for names in GROUPS.values():
            at = 0
            for name in names:
                self.inner[name] = at
                at += self.half[name]

    def parcel(self, group):
        return slice(0, self.gains) if group == "node" else slice(self.gains, self.rows)

    def extent(self, group):
        return (0 if group == "node" else GAINS), self.shards * self.size[group]


def emit(value, name, first_row, layout, group, store, core, slots):
    half = layout.half[name]
    value = value.astype(BF)
    last_row = first_row + value.shape[0]
    for piece in range(2 * layout.shards):
        low, high = max(piece * half, first_row), min((piece + 1) * half, last_row)
        if low < high:
            keep = jnp.bitwise_xor(core, piece % 2)
            to = layout.base[group] + layout.inner[name] + low - piece * half
            if layout.shards > 1:
                to = pl.multiple_of(slots[piece // 2] * layout.size[group] + to, 16)
            store[keep, pl.ds(to, high - low), :] = value[low - first_row : high - first_row]


def backward(
    cot_node, cot_edge, own, edges, table, src, dst, count, weights, gains, res, core, me, layout, sequence,
    store, outs, work, ready, arrive,
):
    w_ein, w_eout, w_nin, w_nout = weights
    g_edge, g_node = gains
    d_own_out, d_edges_out, room, put_gains = outs
    d_outer, d_pre = work
    rows = edges.shape[0]
    shards = layout.shards
    slots = {
        g: [slot_of(i, me, shards, sequence[g]) for i in range(shards)] for g in GROUPS
    }

    def put(value, name, first_row):
        group = "node" if name in GROUPS["node"] else "edge"
        emit(value, name, first_row, layout, group, store, core, slots[group])

    hat = res["node_hat"][...].astype(F32)
    gain_node = jnp.sum(cot_node * hat, axis=0, keepdims=True)
    d_out = norm_back(cot_node, hat, res["node_rate"][:, :1], g_node).astype(BF)
    put(t_mm(res["node_mid"][...], d_out), "nout", 0)
    d_pre_node = (mm_t(d_out, w_nout[...]) * res["node_slope"][...].astype(F32)).astype(BF)
    put(t_mm(own[...], d_pre_node), "nin", 0)
    put(t_mm(res["agg"][...], d_pre_node), "nin", D)
    ready("node")
    d_own = cot_node + mm_t(d_pre_node, w_nin[:D])
    d_agg = mm_t(d_pre_node, w_nin[D:]).astype(BF)

    arrive()
    joins = incidence(dst, count)
    gain_edge = jnp.zeros((1, D), F32)
    for at in range(0, rows, CHUNK):
        part = slice(at, at + CHUNK)
        cot = t_mm(joins[:, part], d_agg)
        if cot_edge is not None:
            cot = cot + cot_edge[part].astype(F32)
        hat = res["edge_hat"][part].astype(F32)
        gain_edge = gain_edge + jnp.sum(cot * hat, axis=0, keepdims=True)
        outer = norm_back(cot, hat, res["edge_rate"][part, :1], g_edge).astype(BF)
        d_outer[part] = outer
        pre = (mm_t(outer, w_eout[...]) * res["edge_slope"][part].astype(F32)).astype(BF)
        d_pre[part] = pre
        d_edges_out[part] = (cot + mm_t(pre, w_ein[:D])).astype(BF)
    put(t_mm(res["edge_mid"][...], d_outer[...]), "eout", 0)
    put(t_mm(edges[...], d_pre[...]), "ein", 0)
    to_src = mm(one_hot(table.shape[0], src), d_pre[...]).astype(BF)
    to_dst = mm(one_hot(NODE_DEV, dst), d_pre[...]).astype(BF)
    put(t_mm(table[...], to_src), "ein", D)
    put(t_mm(own[...], to_dst), "ein", 2 * D)
    put_gains(jnp.concatenate([gain_edge, gain_node, jnp.zeros((GAINS - 2, D), F32)], axis=0))
    ready("edge")
    d_table = mm_t(to_src, w_ein[D : 2 * D])
    d_own = d_own + d_table[:NODE_DEV] + mm_t(to_dst, w_ein[2 * D :])
    d_own_out[...] = d_own
    d_halo = d_table[NODE_DEV:].astype(BF)
    place(-1, [d_halo[j * HALO : (j + 1) * HALO] for j in range(ROUNDS)], room)


SAVED = (
    ("edge_mid", None),
    ("edge_slope", None),
    ("edge_hat", None),
    ("agg", NODE_DEV),
    ("node_mid", NODE_DEV),
    ("node_slope", NODE_DEV),
    ("node_hat", NODE_DEV),
)


def saved_rows(rows):
    return sum(h or rows for _, h in SAVED)


def views(rows, held, rates):
    out, at = {}, 0
    for name, height in SAVED:
        out[name] = held.at[at : at + (height or rows)]
        at += height or rows
    out["edge_rate"] = rates.at[:rows]
    out["node_rate"] = rates.at[rows : rows + NODE_DEV]
    return out


class Copies:
    def __init__(self, sems):
        self.sems, self.used, self.out = sems, 0, []

    def start(self, source, target):
        copy = pltpu.make_async_copy(source, target, self.sems.at[self.used])
        self.used += 1
        copy.start()
        return copy

    def send(self, source, target):
        self.out.append(self.start(source, target))

    def either(self, choice, yes, no, targets):
        sems = [self.sems.at[self.used + i] for i in range(len(targets))]
        self.used += len(targets)

        def start(refs):
            for ref, to, sem in zip(refs, targets, sems):
                pltpu.make_async_copy(ref, to, sem).start()

        pl.when(choice)(lambda: start(yes))
        pl.when(jnp.logical_not(choice))(lambda: start(no))
        return [
            pltpu.make_async_copy(ref, to, sem).wait for ref, to, sem in zip(yes, targets, sems)
        ]

    def finish(self):
        for copy in self.out:
            copy.wait()


def shard_number(shards):
    if shards == 1:
        return jnp.int32(0)
    return lax.axis_index("dom") * lax.axis_size("rep") + lax.axis_index("rep")


def first_rows(refs):
    return [ref.at[0] for ref in refs]


def one_hots(lists):
    return [one_hot(NODE_DEV, lists[0, j : j + 1]) for j in range(ROUNDS)]


def place(sign, pieces, room):
    part, parts = lax.axis_index("dom"), lax.axis_size("dom")
    room[...] = jnp.zeros_like(room)
    for piece, offset in zip(pieces, OFFSETS):
        to = part + sign * offset

        def put(piece=piece, to=to):
            room[pl.ds(pl.multiple_of(to * HALO, HALO), HALO), :] = piece

        pl.when((to >= 0) & (to < parts))(put)


def placed(sign, room):
    part, parts = lax.axis_index("dom"), lax.axis_size("dom")
    out = []
    for offset in OFFSETS:
        source = part + sign * offset
        there = jnp.clip(source, 0, parts - 1)
        rows = room[pl.ds(pl.multiple_of(there * HALO, HALO), HALO), :]
        out.append(jnp.where((source >= 0) & (source < parts), rows, jnp.zeros_like(rows)))
    return out


def pick(hot, values):
    return [t_mm(one, values).astype(BF) for one in hot]


def fill_halo(table, room):
    for j, rows in enumerate(placed(-1, room)):
        table[NODE_DEV + j * HALO : NODE_DEV + (j + 1) * HALO] = rows


def spread(hot, pieces):
    total = mm(hot[0], pieces[0])
    for j in range(1, ROUNDS):
        total = total + mm(hot[j], pieces[j])
    return total


def pick_kernel(lists, nodes, sent, own, room, sems):
    copies = Copies(sems)
    copy = copies.start(nodes.at[lax.axis_index("segment")], own)
    hot = one_hots(lists)
    copy.wait()
    place(1, pick(hot, own[...]), room)
    copies.send(room, sent)
    copies.finish()


def weight_parts(weights):
    first, *others = weights
    return [first.at[:D], first.at[D : 2 * D], first.at[2 * D :], *others]


def arrivals(copies, nodes, own, latents, edges, halo, room, table, core, section, weights):
    late = copies.start(latents, edges)
    parts = [weight_parts(v) for v in weights]
    waits = copies.either(core == section, *[p[:1] for p in parts])
    coming = [copies.start(nodes, own), copies.start(halo, room)]
    waits += copies.either(core == section, *[p[1:] for p in parts])

    def table_here():
        for copy in coming:
            copy.wait()
        fill_halo(table, room)

    return waits, (late.wait, table_here)


def first_kernel(count, src, dst, lists, g_mine, g_other, nodes, latents, *rest):
    halo, mine, other, rest = rest[0], rest[1:5], rest[5:9], rest[9:]
    (node_out, edge_out, saved_out, rate_out, sent), rest = rest[:5], rest[5:]
    held, rest = rest[:4], rest[4:]
    table, edges, saved, rates, room, node_new, edge_new, sems = rest
    core = lax.axis_index("segment")
    own = table.at[:NODE_DEV]
    copies = Copies(sems)
    waits, here = arrivals(
        copies, nodes.at[core], own, latents.at[core], edges, halo, room, table, core, 0,
        (first_rows(mine), first_rows(other), held),
    )
    src, dst = src[...], dst[...]
    gains = jnp.where(core == 0, g_mine[...], g_other[...])
    res = views(edges.shape[0], saved, rates)
    res.update(node_new=node_new, edge_new=edge_new)
    tall = 3 * edges.shape[0]

    def edges_done():
        copies.send(edge_new, edge_out)
        copies.send(saved.at[:tall], saved_out.at[:tall])

    forward(
        own, edges, table, src, dst, count[0], held, waits, (gains[:1], gains[1:2]), res,
        edges_done, here,
    )
    place(1, pick(one_hots(lists), node_new[...]), room)
    for source, target in (
        (room, sent),
        (node_new, node_out),
        (saved.at[tall:], saved_out.at[tall:]),
        (rates, rate_out),
    ):
        copies.send(source, target)
    copies.finish()


def back_outs(copies, layout, store, outs, work):
    d_own, d_edges, sent, *ends = outs
    d_own_s, d_edges_s, room = work

    def ready(group):
        i, rows = list(GROUPS).index(group), layout.parcel(group)
        rows = pl.ds(rows.start, rows.stop - rows.start)
        copies.send(store.at[1, rows], ends[2 + i])
        copies.send(store.at[0, rows], ends[i])

    def finish():
        copies.send(room, sent)
        copies.send(d_own_s, d_own)
        copies.send(d_edges_s, d_edges)
        copies.finish()

    return ready, finish


def second_kernel(shards, count, src, dst, lists, g_mine, g_other, nodes, latents, cots, *rest):
    halo, mine, other, rest = rest[0], rest[1:5], rest[5:9], rest[9:]
    (node_out, edge_out, gain_out), rest = rest[:3], rest[3:]
    outs, rest = rest[:7], rest[7:]
    held, rest = rest[:4], rest[4:]
    table, edges, saved, rates, room, node_new, edge_new, cot, rest = *rest[:8], rest[8:]
    d_outer, d_pre, store, *work, sems = rest
    layout = Layout(shards)
    core, me = lax.axis_index("segment"), shard_number(shards)
    own = table.at[:NODE_DEV]
    copies = Copies(sems)
    waits, here = arrivals(
        copies, nodes, own, latents, edges, halo, room, table, core, 1,
        (first_rows(mine), first_rows(other), held),
    )
    cot_copy = copies.start(cots.at[core], cot)
    src, dst = src[...], dst[...]
    gains = jnp.where(core == 1, g_mine[...], g_other[...])
    gains = (gains[:1], gains[1:2])
    res = views(edges.shape[0], saved, rates)
    res.update(node_new=node_new, edge_new=edge_new)
    forward(
        own, edges, table, src, dst, count[0], held, waits, gains, res,
        lambda: copies.send(edge_new, edge_out), here,
    )
    copies.send(node_new, node_out)
    cot_copy.wait()
    ready, finish = back_outs(copies, layout, store, outs, (*work, room))

    def put_gains(value):
        gain_out[...] = value
        for side in range(2):
            store[side, layout.gains : layout.gains + GAINS] = jnp.zeros((GAINS, D), BF)

    backward(
        cot[...].astype(F32), None, own, edges, table, src, dst, count[0], held, gains, res,
        core, me, layout, SEQUENCE[1], store, (*work[:2], room, put_gains), (d_outer, d_pre), ready, lambda: None,
    )
    finish()


def third_kernel(
    shards, count, src, dst, lists, g_mine, g_other, gain_one, nodes, latents, d_own_in,
    d_edges_in, saved_in, rate_in, *rest
):
    halo, back, mine, other, rest = rest[0], rest[1], rest[2:6], rest[6:10], rest[10:]
    outs, rest = rest[:7], rest[7:]
    held, rest = rest[:4], rest[4:]
    table, edges, saved, rates, room, cot_own, cot_edge, got, rest = *rest[:8], rest[8:]
    d_outer, d_pre, store, *work, sems = rest
    layout = Layout(shards)
    core, me = lax.axis_index("segment"), shard_number(shards)
    own = table.at[:NODE_DEV]
    copies = Copies(sems)
    tall = 3 * edges.shape[0]
    coming = [copies.start(back, got), copies.start(d_own_in, cot_own)]
    coming += [copies.start(rate_in, rates), copies.start(nodes.at[core], own)]
    coming += [copies.start(saved_in.at[tall:], saved.at[tall:]), copies.start(halo, room)]
    order = (3, 2, 1, 0)
    waits = copies.either(
        core == 0, *[[v[i] for i in order] for v in (first_rows(mine), first_rows(other), held)]
    )
    waits = [waits[i] for i in order]
    late = [copies.start(d_edges_in, cot_edge), copies.start(saved_in.at[:tall], saved.at[:tall])]
    late += [copies.start(latents.at[core], edges)]
    src, dst = src[...], dst[...]
    gains = jnp.where(core == 0, g_mine[...], g_other[...])
    gains = (gains[:1], gains[1:2])
    res = views(edges.shape[0], saved, rates)
    hot = one_hots(lists)
    for copy in coming:
        copy.wait()
    fill_halo(table, room)
    cot = (cot_own[...] + spread(hot, placed(1, got))).astype(BF).astype(F32)
    waits[3]()
    waits[2]()

    def arrive():
        for copy in late:
            copy.wait()
        waits[1]()
        waits[0]()

    ready, finish = back_outs(copies, layout, store, outs, (*work, room))

    def put_gains(value):
        both = (value.astype(BF), gain_one[...].astype(BF))
        rows = slice(layout.gains, layout.gains + GAINS)
        store[0, rows] = jnp.where(core == 0, both[0], both[1])
        store[1, rows] = jnp.where(core == 0, both[1], both[0])

    backward(
        cot, cot_edge, own, edges, table, src, dst, count[0], held, gains, res,
        core, me, layout, SEQUENCE[0], store, (*work[:2], room, put_gains), (d_outer, d_pre), ready, arrive,
    )
    finish()


def last_kernel(lists, d_own, back, out):
    out[...] = (d_own[...] + spread(one_hots(lists), placed(1, back))).astype(BF)


def weight_scratch():
    return [pltpu.VMEM((r, D), BF) for r in ROWS.values()]


SMEM = pl.BlockSpec(memory_space=pltpu.SMEM)
VMEM = pl.BlockSpec(memory_space=pltpu.VMEM)
ANY = pl.BlockSpec(memory_space=pl.ANY)


def shape(dims, dtype):
    return jax.ShapeDtypeStruct(tuple(dims), dtype)


def call(kernel, in_specs, outs, out_specs, scratch, flops, traffic, limit=SMALL_LIMIT):
    return pl.pallas_call(
        kernel,
        in_specs=in_specs,
        out_shape=outs,
        out_specs=out_specs,
        scratch_shapes=scratch,
        compiler_params=pltpu.CompilerParams(vmem_limit_bytes=limit),
        cost_estimate=pl.CostEstimate(flops=flops, bytes_accessed=traffic, transcendentals=0),
    )


def exchange(rows):
    return lax.all_to_all(rows, "dom", 0, 0, tiled=True)


def other_core(value):
    return lax.ppermute(value, "segment", [(0, 1), (1, 0)])


def across(value, apart):
    if apart == 1:
        return lax.ppermute(value, "rep", [(0, 1), (1, 0)])
    step = apart // 2
    return lax.ppermute(value, "dom", [(p, p ^ step) for p in range(lax.axis_size("dom"))])


def added(pieces):
    total = pieces[0].astype(F32)
    for piece in pieces[1:]:
        total = total + piece.astype(F32)
    return total


def tied(values, others):
    return lax.optimization_barrier((list(values), list(others)))[0]


class Rows:
    def __init__(self, first, rows, arrays):
        self.rows, self.terms = rows, [(a, first) for a in arrays]

    def upper(self):
        self.rows //= 2
        return self.rows, [(a, first + self.rows) for a, first in self.terms]

    def whole(self):
        return self.rows, list(self.terms)

    def quarter(self, i):
        rows = self.rows // 4
        return rows, [(a, first + i * rows) for a, first in self.terms]

    def add(self, array, first):
        self.terms.append((array, first))


def combine(outputs):
    arrays = []
    for _, segments in outputs:
        for _, terms in segments:
            arrays += [a for a, _ in terms if all(a is not b for b in arrays)]
    total = sum(rows * len(terms) for _, segments in outputs for rows, terms in segments)
    copies = sum(len(terms) for _, segments in outputs for _, terms in segments)
    heights = [sum(rows for rows, _ in segments) for _, segments in outputs]

    def kernel(*refs):
        sources, refs = refs[: len(arrays)], refs[len(arrays) :]
        outs, refs = refs[: len(outputs)], refs[len(outputs) :]
        held, sums, sems, out_sems = refs[0], refs[1:-2], refs[-2], refs[-1]
        plan, at, used = [], 0, 0
        for _, segments in outputs:
            for rows, terms in segments:
                places = []
                for array, first in terms:
                    which = [array is a for a in arrays].index(True)
                    copy = pltpu.make_async_copy(
                        sources[which].at[first : first + rows],
                        held.at[at : at + rows],
                        sems.at[used],
                    )
                    copy.start()
                    places.append((at, copy))
                    at, used = at + rows, used + 1
                plan.append(places)
        plan, gone = iter(plan), []
        for i, (dtype, segments) in enumerate(outputs):
            to = 0
            for rows, _ in segments:
                places = next(plan)
                for _, copy in places:
                    copy.wait()
                for low in range(0, rows, 64):
                    high = min(low + 64, rows)
                    value = added([held[p + low : p + high] for p, _ in places])
                    sums[i][to + low : to + high] = value.astype(dtype)
                to += rows
            gone.append(pltpu.make_async_copy(sums[i], outs[i], out_sems.at[i]))
            gone[-1].start()
        for copy in gone:
            copy.wait()

    shapes = [((height, D), dtype) for height, (dtype, _) in zip(heights, outputs)]
    return call(
        kernel,
        [ANY] * len(arrays),
        [shape(*s) for s in shapes],
        [ANY] * len(outputs),
        [
            pltpu.VMEM((total, D), BF),
            *[pltpu.VMEM(*s) for s in shapes],
            pltpu.SemaphoreType.DMA((copies,)),
            pltpu.SemaphoreType.DMA((len(outputs),)),
        ],
        10**6,
        8 * 10**6,
    )(*arrays)


def summed(rows, terms):
    return added([a[first : first + rows] for a, first in terms]).astype(BF)


def sent_parts(parts):
    return (BF, [p.upper() for p in parts])


def receive(parts, got):
    at = 0
    for part in parts:
        part.add(got, at)
        at += part.rows
    return got


def body(
    node_latent,
    edge_latent,
    node_cot,
    edge_src,
    edge_dst,
    edge_count,
    send_index,
    w_edge_in,
    w_edge_out,
    w_node_in,
    w_node_out,
    gain_edge,
    gain_node,
):
    micro, _, _ = node_latent.shape
    rows = edge_latent.shape[1]
    assert micro == lax.axis_size("segment") == 2
    doms, reps = lax.axis_size("dom"), lax.axis_size("rep")
    core, part, rep = (lax.axis_index(a) for a in ("segment", "dom", "rep"))
    shards = doms * reps if doms * reps == 16 else 1
    first = core == 0

    src, dst = edge_src[None], edge_dst[None]

    dma = pltpu.SemaphoreType.DMA
    halo_shape = shape((doms * HALO, D), BF)
    node_s, edge_s = pltpu.VMEM((NODE_DEV, D), BF), pltpu.VMEM((rows, D), BF)
    room_s = pltpu.VMEM((doms * HALO, D), BF)
    sent = call(
        pick_kernel,
        [VMEM, ANY],
        halo_shape,
        ANY,
        [node_s, room_s, dma((2,))],
        10**7,
        7 * 10**6,
    )(send_index, node_latent)
    halo_zero = exchange(sent)
    mine = (w_edge_in, w_edge_out, w_node_in, w_node_out)
    other = tuple(other_core(w) for w in mine)
    g_mine = jnp.concatenate([gain_edge, gain_node], axis=0)
    small = (edge_count, src, dst, send_index, g_mine, other_core(g_mine))
    small_specs = [SMEM] + [VMEM] * 5

    table_s = pltpu.VMEM((NODE_DEV + ROUNDS * HALO, D), BF)
    saved_dims, rate_dims = (saved_rows(rows), D), (rows + NODE_DEV, 128)
    layer_s = [
        *weight_scratch(),
        table_s,
        edge_s,
        pltpu.VMEM(saved_dims, BF),
        pltpu.VMEM(rate_dims, F32),
        room_s,
    ]
    node_one, edge_one, saved, rates, sent = call(
        first_kernel,
        small_specs + [ANY] * (2 + 1 + 8),
        [
            shape((NODE_DEV, D), BF),
            shape((rows, D), BF),
            shape(saved_dims, BF),
            shape(rate_dims, F32),
            halo_shape,
        ],
        [ANY] * 5,
        [*layer_s, node_s, edge_s, dma((20,))],
        11 * 10**8,
        26 * 10**6,
        VMEM_LIMIT,
    )(*small, node_latent, edge_latent, halo_zero, *mine, *other)
    halo_one = exchange(sent)

    layout = Layout(shards)

    def group_rows(values):
        return [Rows(*layout.extent(g), v) for g, v in zip(GROUPS, values)]

    parcels = [layout.parcel(g) for g in GROUPS]
    share = [shape((p.stop - p.start, D), BF) for p in parcels]
    back_shapes = [
        shape((NODE_DEV, D), F32),
        shape((rows, D), BF),
        halo_shape,
        *share,
        *share,
    ]
    back_s = [
        edge_s,
        edge_s,
        pltpu.VMEM((2, layout.rows, D), BF),
        pltpu.VMEM((NODE_DEV, D), F32),
        edge_s,
        dma((40,)),
    ]
    node_two, edge_two, gain_one, *done = call(
        functools.partial(second_kernel, shards),
        small_specs + [ANY] * (3 + 1 + 8),
        [shape((NODE_DEV, D), BF), shape((rows, D), BF), shape((GAINS, D), F32)] + back_shapes,
        [ANY, ANY, VMEM] + [ANY] * len(back_shapes),
        [*layer_s, node_s, edge_s, node_s, *back_s],
        28 * 10**8,
        44 * 10**6,
        VMEM_LIMIT,
    )(*small, node_one, edge_one, node_cot, halo_one, *mine, *other)
    d_own, d_edges, sent, *ends = done
    back = exchange(sent)
    one = [(k, other_core(v)) for k, v in zip(ends[:2], ends[2:])]
    if shards > 1:
        one = group_rows(one)
        gone = [summed(*p.upper()) for p in one]
        (back,) = tied([back], gone)
        got = [receive([p], across(v, a)) for p, v, a in zip(one, gone, (1, 2))]

    d_own, d_edges, sent, *ends = call(
        functools.partial(third_kernel, shards),
        small_specs + [VMEM] + [ANY] * (6 + 2 + 8),
        back_shapes,
        [ANY] * len(back_shapes),
        [*layer_s, pltpu.VMEM((NODE_DEV, D), F32), edge_s, room_s, *back_s],
        18 * 10**8,
        37 * 10**6,
        VMEM_LIMIT,
    )(
        *small, gain_one, node_latent, edge_latent, d_own, d_edges, saved, rates, halo_zero,
        back, *mine, *other,
    )

    def paired(gradient, latent):
        got = other_core(jnp.where(first, latent, gradient))
        low = jnp.where(first, gradient, got)
        high = jnp.where(first, got, latent)
        return jnp.stack([low, high])[None]

    def own_gradient(back):
        return call(
            last_kernel,
            [VMEM] * 3,
            shape((NODE_DEV, D), BF),
            VMEM,
            [],
            10**7,
            7 * 10**6,
        )(send_index, d_own, back)

    if shards > 1:
        send_e, send_n = tied([ends[3], ends[2]], got)
        one_gone = jnp.concatenate([summed(*p.upper()) for p in one], axis=0)
        receive(one, across(one_gone, 4))
        got_e, got_n = other_core(send_e), other_core(send_n)
        (got_e,) = tied([got_e], [one_gone])
        sums = Rows(0, GAINS, (ends[1], got_e))
        nodes, edges = group_rows([(ends[0], got_n), (ends[1], got_e)])
        gone = summed(*edges.upper())
        receive([edges], across(gone, 2))
        nodes.terms[-1] = (tied([got_n], [gone])[0], 0)
        gone = jnp.concatenate([summed(*nodes.upper()), summed(*sums.whole())], axis=0)
        got = receive([nodes, sums], across(gone, 1))
        d_edges, edge_two = tied([d_edges, edge_two], [gone])
        one_gone = jnp.concatenate([summed(*p.upper()) for p in one], axis=0)
        receive(one, across(one_gone, 8))
        (got,) = tied([got], [one_gone])
        nodes.terms[-1], sums.terms[-1] = (got, 0), (got, nodes.rows)
        gone = combine([(BF, [edges.upper()]), (BF, [nodes.upper(), sums.whole()])])
        (sent,) = tied([sent], gone)
        back = exchange(sent)
        receive([edges], across(gone[0], 1))
        receive([nodes, sums], across(gone[1], 2))
        zero = [sums, nodes, edges]
        far = [
            [p.quarter(i) if p.rows > GAINS else p.whole() for p in zero] for i in range(4)
        ]
        near = [p.upper() for p in one]
        *far, stay, near_n, near_e, stay_one = combine(
            [
                *[(BF, v) for v in far[1:]],
                (F32, far[0]),
                *[(BF, [v]) for v in near],
                (F32, [p.whole() for p in one]),
            ]
        )
        got = [across(v, 4 * i) for i, v in enumerate(far, 1)]
        near = [across(near_n, 2), across(near_e, 1)]
        zero = added([stay, *got])
        (back,) = tied([back], far)
        node_pair = paired(own_gradient(back), node_two)
        one = added([stay_one, jnp.concatenate(near, axis=0)])
        sums, zero = zero[:GAINS], zero[GAINS:]
    else:
        node_pair = paired(own_gradient(exchange(sent)), node_two)
        zero = [(k, other_core(v)) for k, v in zip(ends[:2], ends[2:])]
        sums = lax.psum(added([v[:GAINS] for v in zero[1]]), ("dom", "rep"))
        one, zero = (
            jnp.concatenate([added([v[-layout.extent(g)[1] :] for v in y]) for g, y in zip(GROUPS, x)])
            for x in (one, zero)
        )


    edge_pair = paired(d_edges, edge_two)
    factor = float(micro * reps * NODE_DEV * doms) ** (-0.5)
    got = other_core(jnp.where(first, one, zero))
    at, places = 0, {}
    for names in GROUPS.values():
        for name in names:
            places[name] = (at, ROWS[name] // shards // 2)
            at += places[name][1]
    scale = factor if shards > 1 else 1.0

    def grads_kernel(got, one, zero, *outs):
        mine = lax.axis_index("segment") == 0
        for out, name in zip(outs, ROWS):
            at, size = places[name]
            rows = slice(at, at + size)
            kept = jnp.where(mine, zero[rows], one[rows])
            out[:size] = jnp.where(mine, kept, got[rows]) * scale
            out[size:] = jnp.where(mine, got[rows], kept) * scale

    grads = call(
        grads_kernel,
        [VMEM] * 3,
        [shape((rows // shards, D), F32) for rows in ROWS.values()],
        [VMEM] * 4,
        [],
        10**6,
        7 * 10**6,
        16 * 1024 * 1024,
    )(got, one, zero)
    grads = dict(zip(ROWS, grads))
    if shards == 1:
        grads = {
            k: lax.psum_scatter(v, ("dom", "rep"), scatter_dimension=0, tiled=True) * factor
            for k, v in grads.items()
        }
    width = D // (doms * reps)
    sums = lax.dynamic_slice_in_dim(sums[:2], (part * reps + rep) * width, width, axis=1) * factor
    return (
        node_pair,
        edge_pair,
        grads["ein"][None],
        grads["eout"][None],
        grads["nin"][None],
        grads["nout"][None],
        sums[:1],
        sums[1:2],
    )


def solution(mesh):
    placed = (
        P("rep", "dom", None),
        P("rep", "dom", None),
        P("rep", "dom", None),
        P("dom"),
        P("dom"),
        P("dom"),
        P("dom", None, None),
        P("segment", None, None),
        P("segment", None, None),
        P("segment", None, None),
        P("segment", None, None),
        P("segment", None),
        P("segment", None),
    )
    return jax.shard_map(
        body,
        mesh=mesh,
        in_specs=placed,
        out_specs=(
            P("segment", "rep", "dom", None),
            P("segment", "rep", "dom", None),
            P("segment", ("dom", "rep"), None),
            P("segment", ("dom", "rep"), None),
            P("segment", ("dom", "rep"), None),
            P("segment", ("dom", "rep"), None),
            P("segment", ("dom", "rep")),
            P("segment", ("dom", "rep")),
        ),
        check_vma=False,
    )
```
